32 devices in a mesh: section: 4 (over y, x), dp: 8 (over z, core).
Axes of the slice: x: 2, y: 2, z: 4, core: 2. Of those that a mesh axis runs over, the one named last changes fastest.
Arguments:
- embedding: float32 [64, 512, 256], P('dp'), may hold values from -6 to 6
- cotangent: float32 [64, 512, 256], P('dp'), may hold values from -6 to 6
- counts: int32 [64], P('dp'), may hold values from 1 to 4, as said below
- owner_list: int32 [48], replicated, may hold values from 0 to 7, as said below
- tiles_owned: float32 [48, 128, 256], P('dp'), may hold values from -0.375 to 0.375
- first_owned: float32 [48, 128, 256], P('dp'), may hold values from -80 to 80
- second_owned: float32 [48, 128, 256], P('dp'), may hold values from 15.72864 to 65.536
- small_params: float32 [18, 256], replicated, may hold values from -0.9 to 1.5, as said below
- small_first: float32 [18, 256], replicated, may hold values from -80 to 80
- small_second: float32 [18, 256], replicated, may hold values from 15.72864 to 65.536
Outputs:
- final_states: float32 [64, 512, 256], P('dp', 'section')
- embed_grad: float32 [64, 512, 256], P('dp', 'section')
- tile_grad: float32 [48, 128, 256], P('dp')
- tile_first: float32 [48, 128, 256], P('dp')
- tile_second: float32 [48, 128, 256], P('dp')
- tile_new: float32 [48, 128, 256], P('dp')
- small_grad: float32 [18, 256], replicated
- small_first_new: float32 [18, 256], replicated
- small_second_new: float32 [18, 256], replicated
- small_new: float32 [18, 256], replicated
The draws below stay inside these ranges and needn't reach their ends.
Inputs may be any that keep to these rules, and one draw needn't show every extreme that they name: `counts`: among the 8 prompts of each index of dp one has 4 loops and another has 1. `owner_list`: every index of dp owns exactly 6 tiles. `small_params`: norm gains lie in 0.5 to 1.5, shifts and biases in -0.9 to 0.9.
All inputs are finite; a program needn't handle non-finite values.
Results may differ from the reference program's by a relative error of at most 0.0085.
The reference program's roundings to bfloat16 on the way count: a program that leaves them out, or rounds other values in their place, can miss the bound.
Values may be sent and summed in bfloat16 or wider, within the bound.
No kernel may reach another device: no remote copies, remote signals or barrier semaphores. Data moves between devices by JAX's collectives and lax.ppermute only.
A program may use at most 192 MiB of HBM per device.

```python
import math
import jax
import jax.numpy as jnp
from jax import lax

D = 256
HEADS = 8
HALF = 128
SEQ = 512
PROMPTS_DEV = 8
PROMPTS = 64
TILES = 48
OWN = 6
STEP = 10
N_SECTION = 4
N_DP = 8


def draw_counts(key, part):
    loops_drawn = jax.random.randint(jax.random.fold_in(key, 1), (N_DP, PROMPTS_DEV), 1, N_SECTION + 1)
    longest = jax.random.randint(jax.random.fold_in(key, 2), (N_DP, 1), 0, PROMPTS_DEV)
    offset = jax.random.randint(jax.random.fold_in(key, 3), (N_DP, 1), 1, PROMPTS_DEV)
    shortest = (longest + offset) % PROMPTS_DEV
    position = jnp.arange(PROMPTS_DEV)[None, :]
    loops_drawn = jnp.where(position == longest, N_SECTION, loops_drawn)
    loops_drawn = jnp.where(position == shortest, 1, loops_drawn)
    return loops_drawn.reshape(N_DP * PROMPTS_DEV).astype(jnp.int32)


def draw_owner_list(key, part):
    shuffled = jax.random.permutation(jax.random.fold_in(key, 5), TILES)
    return (shuffled // OWN).astype(jnp.int32)


def draw_small_params(key, part):
    base_key = jax.random.fold_in(key, 7)
    noise = jax.random.normal(base_key, (18, D), jnp.float32)
    row_kind = jnp.arange(18)[:, None] % 9
    is_gain = (row_kind == 0) | (row_kind == 2)
    gains = 1.0 + 0.2 * jnp.clip(noise, -2.5, 2.5)
    shifts = 0.3 * jnp.clip(noise, -3.0, 3.0)
    return jnp.where(is_gain, gains, shifts).astype(jnp.float32)


def shard_levels(rng, shape, shards, low, high):
    loudness = 1.0
    for dim, blocks in shards:
        steps = jax.random.uniform(jax.random.fold_in(jax.random.fold_in(rng, 6), dim), (blocks,), jnp.float32, low / len(shards), high / len(shards))
        loudness = loudness * jnp.repeat(jnp.exp(steps), shape[dim] // blocks).reshape((-1,) + (1,) * (len(shape) - 1 - dim))
    return loudness


def scatter_about(key, shape, deviation, limit, split=(), kind=jnp.bfloat16):
    result = deviation * jax.random.normal(key, shape, jnp.float32)
    if split:
        result = result * shard_levels(key, shape, split, -0.22, 0.18)
    return jnp.clip(result, -limit, limit).astype(kind)


def setup_inputs(seed: int = 0) -> dict:
    key_of = jax.random.split(jax.random.key(seed), 11)
    embedding = scatter_about(key_of[0], (PROMPTS, SEQ, D), 1.0, 6.0, ((0, 8),), jnp.float32)
    cotangent = scatter_about(key_of[1], (PROMPTS, SEQ, D), 1.0, 6.0, ((0, 8),), jnp.float32)
    counts = draw_counts(jax.random.fold_in(key_of[10], 71), 0)
    owner_list = draw_owner_list(jax.random.fold_in(key_of[10], 71), 0)
    tiles_owned = scatter_about(key_of[4], (TILES, HALF, D), D ** -0.5, 0.375, ((0, 8),), jnp.float32)
    first_owned = scatter_about(key_of[5], (TILES, HALF, D), (0.04 * (PROMPTS * SEQ * N_SECTION) ** 0.5), 80.0, ((0, 8),), jnp.float32)
    second_owned = jnp.clip(jnp.exp(math.log(65.536) - 1.4271164 * jax.random.uniform(key_of[6], (TILES, HALF, D), jnp.float32) ** shard_levels(key_of[6], (TILES, HALF, D), ((0, 8),), -0.2, 0.2)), 15.72864, 65.536)
    small_params = draw_small_params(jax.random.fold_in(key_of[10], 71), 0)
    small_first = scatter_about(key_of[8], (18, D), (0.04 * (PROMPTS * SEQ * N_SECTION) ** 0.5), 80.0, (), jnp.float32)
    small_second = jnp.clip(jnp.exp(jax.random.uniform(key_of[9], (18, D), jnp.float32, math.log(15.72864), math.log(65.536))), 15.72864, 65.536)
    return {"embedding": embedding, "cotangent": cotangent, "counts": counts, "owner_list": owner_list, "tiles_owned": tiles_owned, "first_owned": first_owned, "second_owned": second_owned, "small_params": small_params, "small_first": small_first, "small_second": small_second}


@jax.custom_vjp
def low(v):
    return lax.optimization_barrier(v.astype(jnp.bfloat16)).astype(jnp.float32)

@jax.custom_vjp
def low_back(v):
    return v

def low_keep(v):
    return (low(v), None)

def low_pass(kept, grad):
    return (grad,)

def back_keep(v):
    return (v, None)

def back_low(kept, grad):
    return (low(grad),)
low.defvjp(low_keep, low_pass)
low_back.defvjp(back_keep, back_low)
highest = lax.Precision.HIGHEST
beta_one = 0.9
beta_two = 0.999
learn_rate = 0.05
small_rate = 0.3
weight_decay = 0.1
adam_eps = 1e-08
norm_eps = 1e-05
masked_score = -1e+30

def layer_norm(vector, gain, shift):
    center = vector - lax.optimization_barrier(jnp.mean(vector, axis=-1, keepdims=True))
    spread = lax.optimization_barrier(jnp.mean(center * center, axis=-1, keepdims=True))
    return center * lax.rsqrt(spread + norm_eps) * gain + shift

def matmul(left, right):
    return jnp.dot(left, right, precision=highest, preferred_element_type=jnp.float32)

def unpack(tile_full, layer):
    half_rows = tile_full.shape[1]
    model_width = tile_full.shape[2]
    first_tile = 24 * layer
    squares = [tile_full[first_tile + 2 * square_num:first_tile + 2 * square_num + 2].reshape(model_width, model_width) for square_num in range(4)]
    w_up = tile_full[first_tile + 8:first_tile + 16].reshape(2, 4, half_rows, model_width).transpose(0, 2, 1, 3).reshape(model_width, 4 * model_width)
    w_down = tile_full[first_tile + 16:first_tile + 24].reshape(4 * model_width, model_width)
    return (squares[0], squares[1], squares[2], squares[3], w_up, w_down)

def layer_forward(vector, weights, layer_rows):
    w_query, w_key, w_value, w_out, w_up, w_down = weights
    length, model_width = vector.shape
    head_size = model_width // HEADS
    normed = low(layer_norm(vector, layer_rows[0], layer_rows[1]))
    queries = low(low_back(matmul(normed, w_query))).reshape(length, HEADS, head_size)
    key_rows = low(low_back(matmul(normed, w_key))).reshape(length, HEADS, head_size)
    value_rows = low(low_back(matmul(normed, w_value))).reshape(length, HEADS, head_size)
    raw_scores = low_back(jnp.einsum('qhd,khd->hqk', queries, key_rows, precision=highest))
    causal = jnp.arange(length)[:, None] >= jnp.arange(length)[None, :]
    scores = jnp.where(causal[None], raw_scores * head_size ** (-0.5), masked_score)
    attn_probs = low(jax.nn.softmax(scores, axis=-1))
    context = low(low_back(jnp.einsum('hqk,khd->qhd', attn_probs, value_rows, precision=highest))).reshape(length, model_width)
    residual = vector + low_back(matmul(context, w_out))
    normed_two = low(layer_norm(residual, layer_rows[2], layer_rows[3]))
    before = low_back(matmul(normed_two, w_up) + layer_rows[4:8].reshape(-1))
    activated = low(jax.nn.gelu(before))
    return residual + low_back(matmul(activated, w_down)) + layer_rows[8]

def block_step(state_in, tile_low, small_params):
    middle = layer_forward(state_in, unpack(tile_low, 0), small_params[0:9])
    return layer_forward(middle, unpack(tile_low, 1), small_params[9:18])

def loop_prompt(embed_row, count, tile_low, small_params):
    stepper = jax.checkpoint(block_step)
    state_now = jnp.zeros_like(embed_row)
    for section in range(N_SECTION):
        output = stepper(state_now + embed_row, tile_low, small_params)
        state_now = jnp.where(count > section, output, state_now)
    return state_now

def adam_update(gradient, first_old, second_old, weight, decay_rate, rate):
    first_new = beta_one * first_old + (1.0 - beta_one) * gradient
    second_new = beta_two * second_old + (1.0 - beta_two) * gradient * gradient
    corr_one = 1.0 - beta_one ** STEP
    corr_two = 1.0 - beta_two ** STEP
    update = first_new / corr_one / (jnp.sqrt(second_new / corr_two) + adam_eps)
    return (first_new, second_new, weight - rate * (update + decay_rate * weight))

def reference(embedding, cotangent, counts, owner_list, tiles_owned, first_owned, second_owned, small_params, small_first, small_second):
    tile_order = jnp.argsort(owner_list, stable=True).astype(jnp.int32)
    back_order = jnp.argsort(tile_order, stable=True).astype(jnp.int32)
    tile_full = tiles_owned[back_order]

    def per_prompt(totals, item):
        embed_row, cot_row, count = item

        def prompt_fn(row_value, tile_value, small_value):
            return loop_prompt(row_value, count, low(tile_value), small_value)
        output, pull = jax.vjp(prompt_fn, embed_row, tile_full, small_params)
        grad_row, grad_tiles, grad_small = pull(cot_row)
        return ((totals[0] + grad_tiles, totals[1] + grad_small), (output, grad_row))
    start = (jnp.zeros(tile_full.shape, jnp.float32), jnp.zeros(small_params.shape, jnp.float32))
    (grad_tiles, grad_small), (final_states, embed_grad) = lax.scan(per_prompt, start, (embedding, cotangent, counts))
    tile_grad = grad_tiles[tile_order]
    tile_first, tile_second, tile_new = adam_update(tile_grad, first_owned, second_owned, tiles_owned, weight_decay, learn_rate)
    small_first_new, small_second_new, small_new = adam_update(grad_small, small_first, small_second, small_params, 0.0, small_rate)
    return (final_states, embed_grad, tile_grad, tile_first, tile_second, tile_new, grad_small, small_first_new, small_second_new, small_new)
```

```python
import functools, math
import jax
import jax.numpy as jnp
from jax import lax
from jax.experimental import pallas as pl
from jax.experimental.pallas import tpu as pltpu

F32, BF16 = jnp.float32, jnp.bfloat16
HEADS = 8
EPS = 1e-5
MASKED = -1e30
GC0 = math.sqrt(2.0 / math.pi)
GC1 = 0.044715


def nn(a, b):
    return lax.dot_general(a, b, (((1,), (0,)), ((), ())), preferred_element_type=F32)


def nt(a, b):
    return lax.dot_general(a, b, (((1,), (1,)), ((), ())), preferred_element_type=F32)


def tn(a, b):
    return lax.dot_general(a, b, (((0,), (0,)), ((), ())), preferred_element_type=F32)


def wide(col, n):
    return jnp.concatenate([col] * (n // 128), axis=1)


def fold(a):
    r = a[:, 0:128]
    for i in range(1, a.shape[1] // 128):
        r = r + a[:, 128 * i : 128 * i + 128]
    return r


def normed(x):
    d = x.shape[0]
    mean = jnp.sum(x, axis=0, keepdims=True) * (1.0 / d)
    xc = x - mean
    var = jnp.sum(xc * xc, axis=0, keepdims=True) * (1.0 / d)
    rstd = lax.rsqrt(var + EPS)
    return xc * rstd, rstd


def norm_back(dn, xhat, rstd, gain):
    d = dn.shape[0]
    dx = dn * gain
    a = jnp.sum(dx, axis=0, keepdims=True) * (1.0 / d)
    b = jnp.sum(dx * xhat, axis=0, keepdims=True) * (1.0 / d)
    return rstd * (dx - a - xhat * b)


def split2(v):
    hi = v.astype(BF16)
    return hi, (v - hi.astype(F32)).astype(BF16)


class R:
    pass


def layer_fwd(r, l, sl, T, D):
    hd = D // HEADS
    pr = lambda k, n=1: r.pb[l, pl.ds(k * D, n * D), :]
    x = r.cur[...]
    r.xs[sl] = x
    xhat, _ = normed(x)
    r.n1[...] = (xhat * wide(pr(0), T) + wide(pr(1), T)).astype(BF16)
    for i in range(3):
        r.qkv[sl, pl.ds(i * D, D), :] = nn(r.wt_qkv[l, pl.ds(i * D, D), :], r.n1[...]).astype(BF16)
    c2 = hd**-0.5 * math.log2(math.e)
    ones16 = jnp.ones((16, T), BF16)

    def head(h):
        q = r.qkv[sl, pl.ds(h * hd, hd), :]
        k = r.qkv[sl, pl.ds(D + h * hd, hd), :]
        v = r.qkv[sl, pl.ds(2 * D + h * hd, hd), :]
        qhi, qlo = split2(q.astype(F32) * c2)
        qe = jnp.concatenate([qhi, qlo], axis=0)
        ke = jnp.concatenate([k, k], axis=0)
        ve = jnp.concatenate([v, ones16], axis=0)
        off = 0
        for b in range(T // 256):
            kk = 256 * (b + 1)
            s = tn(ke[:, :kk], qe[:, 256 * b : 256 * b + 256])
            tail = s[kk - 256 :, :] + r.mask[...]
            if b == 0:
                mx = jnp.max(tail, axis=0, keepdims=True)
                e = jnp.exp2(tail - mx).astype(BF16)
            else:
                lead = s[: kk - 256, :]
                mx = jnp.maximum(jnp.max(tail, axis=0, keepdims=True), jnp.max(lead, axis=0, keepdims=True))
                e = jnp.concatenate([jnp.exp2(lead - mx).astype(BF16), jnp.exp2(tail - mx).astype(BF16)], axis=0)
            r.es[sl, h, pl.ds(off, kk), :] = e
            off += kk
            o = nn(ve[:, :kk], e)
            linv = 1.0 / o[hd : hd + 1, :]
            r.linv[sl, pl.ds(h, 1), pl.ds(256 * b, 256)] = linv
            r.ctx[sl, pl.ds(h * hd, hd), pl.ds(256 * b, 256)] = (o[:hd, :] * linv).astype(BF16)

    def body(i, _):
        for u in range(r.unroll):
            head(i * r.unroll + u)
        return 0

    lax.fori_loop(0, HEADS // r.unroll, body, 0)
    m = r.xs[sl] + nn(r.wt_o[l], r.ctx[sl])
    r.cur[...] = m
    mhat, _ = normed(m)
    r.n2[...] = (mhat * wide(pr(2), T) + wide(pr(3), T)).astype(BF16)
    for i in range(4):
        u = nn(r.wt_up[l, pl.ds(i * D, D), :], r.n2[...]) + wide(pr(4 + i), T)
        t = jnp.tanh(u * (GC0 + (GC0 * GC1) * (u * u)))
        hu = 0.5 * u
        r.g[pl.ds(i * D, D), :] = (hu + hu * t).astype(BF16)
    r.cur[...] = r.cur[...] + nn(r.wt_down[l], r.g[...]) + wide(pr(8), T)


def layer_bwd(r, l, sl, T, D):
    hd = D // HEADS
    c = hd**-0.5
    pr = lambda k, n=1: r.pb[l, pl.ds(k * D, n * D), :]

    def add_small(k, v):
        r.sg[l, pl.ds(k * D, D), :] = r.sg[l, pl.ds(k * D, D), :] + fold(v)

    dy = r.dcur[...]
    r.dylow[...] = dy.astype(BF16)
    add_small(8, dy)
    mhat, rstd2 = normed(r.xs[sl] + nn(r.wt_o[l], r.ctx[sl]))
    r.hat[...] = mhat
    r.n2[...] = (mhat * wide(pr(2), T) + wide(pr(3), T)).astype(BF16)
    for i in range(4):
        u = nn(r.wt_up[l, pl.ds(i * D, D), :], r.n2[...]) + wide(pr(4 + i), T)
        u2 = u * u
        t = jnp.tanh(u * (GC0 + (GC0 * GC1) * u2))
        hu = 0.5 * u
        r.g[pl.ds(i * D, D), :] = (hu + hu * t).astype(BF16)
        gp = (0.5 + 0.5 * t) + (hu - hu * t * t) * (GC0 + (3.0 * GC0 * GC1) * u2)
        du = gp * nn(r.w_down[l, pl.ds(i * D, D), :], r.dylow[...])
        add_small(4 + i, du)
        r.du[pl.ds(i * D, D), :] = du.astype(BF16)
    dn2 = nn(r.w_up[l], r.du[...])
    add_small(2, dn2 * r.hat[...])
    add_small(3, dn2)
    dm = r.dcur[...] + norm_back(dn2, r.hat[...], rstd2, wide(pr(2), T))
    r.dcur[...] = dm
    r.dmlow[...] = dm.astype(BF16)

    def add_tiles(t, v, gap=1):
        for a in range(2):
            at = r.place[24 * l + t + gap * a]
            r.acc[at] = r.acc[at] + v[128 * a : 128 * a + 128]

    for i in range(4):
        add_tiles(16 + 2 * i, nt(r.g[pl.ds(i * D, D), :], r.dylow[...]))
    for i in range(4):
        add_tiles(8 + i, nt(r.n2[...], r.du[pl.ds(i * D, D), :]), 4)
    add_tiles(6, nt(r.ctx[sl], r.dmlow[...]))
    r.dctx[...] = nn(r.w_o[l], r.dmlow[...]).astype(BF16)
    row = lax.broadcasted_iota(jnp.int32, (16, T), 0)
    ones3 = jnp.where(row < 3, 1.0, 0.0).astype(BF16)

    def head(h):
        q = r.qkv[sl, pl.ds(h * hd, hd), :]
        k = r.qkv[sl, pl.ds(D + h * hd, hd), :]
        v = r.qkv[sl, pl.ds(2 * D + h * hd, hd), :]
        dctx = r.dctx[pl.ds(h * hd, hd), :].astype(F32)
        ctx = r.ctx[sl, pl.ds(h * hd, hd), :].astype(F32)
        linv = r.linv[sl, pl.ds(h, 1), :] * c
        dcl = dctx * linv
        nd = -jnp.sum(dctx * ctx, axis=0, keepdims=True) * linv
        hi, lo = split2(dcl)
        n0 = nd.astype(BF16).astype(F32)
        n1 = (nd - n0).astype(BF16).astype(F32)
        n2 = nd - n0 - n1
        extra = jnp.where(row == 0, n0, jnp.where(row == 1, n1, jnp.where(row == 2, n2, 0.0))).astype(BF16)
        de = jnp.concatenate([hi, lo, extra], axis=0)
        ve = jnp.concatenate([v, v, ones3], axis=0)
        off = 0
        dk = None
        dv = None
        nb = T // 256
        dks = [None] * nb
        dvs = [None] * nb
        for b in range(nb):
            kk = 256 * (b + 1)
            qs = slice(256 * b, 256 * b + 256)
            e = r.es[sl, h, pl.ds(off, kk), :]
            off += kk
            dsr = tn(ve[:, :kk], de[:, qs])
            ds = (e.astype(F32) * dsr).astype(BF16)
            r.dqkv[pl.ds(h * hd, hd), pl.ds(256 * b, 256)] = nn(k[:, :kk], ds).astype(BF16)
            dkb = nt(q[:, qs], ds)
            dvb = nt(de[: 2 * hd, qs], e)
            for j in range(b + 1):
                js = slice(256 * j, 256 * j + 256)
                dks[j] = dkb[:, js] if dks[j] is None else dks[j] + dkb[:, js]
                dvs[j] = dvb[:, js] if dvs[j] is None else dvs[j] + dvb[:, js]
        for j in range(nb):
            r.dqkv[pl.ds(D + h * hd, hd), pl.ds(256 * j, 256)] = dks[j].astype(BF16)
            r.dqkv[pl.ds(2 * D + h * hd, hd), pl.ds(256 * j, 256)] = (
                (dvs[j][:hd] + dvs[j][hd:]) * (1.0 / c)
            ).astype(BF16)

    def body(i, _):
        for u in range(r.unroll):
            head(i * r.unroll + u)
        return 0

    lax.fori_loop(0, HEADS // r.unroll, body, 0)
    xhat, rstd1 = normed(r.xs[sl])
    r.hat[...] = xhat
    r.n1[...] = (xhat * wide(pr(0), T) + wide(pr(1), T)).astype(BF16)
    for i in range(3):
        add_tiles(2 * i, nt(r.n1[...], r.dqkv[pl.ds(i * D, D), :]))
    dn1 = nn(r.w_qkv[l], r.dqkv[...])
    add_small(0, dn1 * r.hat[...])
    add_small(1, dn1)
    r.dcur[...] = r.dcur[...] + norm_back(dn1, r.hat[...], rstd1, wide(pr(0), T))


def kernel(S, N, unroll, nprompts, counts, place, rows, emb, cot, tiles, pbr, fin, eg, gt, sgo, *scr):
    r = R()
    (r.pb, r.wt_qkv, r.wt_o, r.wt_up, r.wt_down, r.w_qkv, r.w_o, r.w_up, r.w_down, r.mask,
     r.cur, r.dcur, r.embT, r.gsum, r.io, r.n1, r.n2, r.hat, r.g, r.du, r.dylow, r.dmlow, r.dctx, r.dqkv,
     r.xs, r.qkv, r.es, r.linv, r.ctx, r.sem) = scr[:30]
    redo = N > S
    if redo:
        r.hs = scr[30]
    r.acc, r.sg, r.place = gt, sgo, place
    r.unroll = unroll
    T, D = r.io.shape
    H = 128

    def spot(l, t):
        if t < 6:
            return r.w_qkv.at[l, pl.ds(t % 2 * H, H), pl.ds(t // 2 * D, D)]
        if t < 8:
            return r.w_o.at[l, pl.ds((t - 6) * H, H), :]
        if t < 16:
            return r.w_up.at[l, pl.ds((t - 8) // 4 * H, H), pl.ds((t - 8) % 4 * D, D)]
        return r.w_down.at[l, pl.ds((t - 16) * H, H), :]

    cps = [pltpu.make_async_copy(tiles.at[place[24 * l + t]], spot(l, t), r.sem) for l in range(2) for t in range(24)]
    for cp in cps:
        cp.start()
    for k in range(18):
        r.pb[k // 9, k % 9 * D : k % 9 * D + D, :] = jnp.broadcast_to(pbr[k : k + 1, :], (128, D)).T
    for cp in cps:
        cp.wait()
    for l in range(2):
        for src, dst in ((r.w_qkv, r.wt_qkv), (r.w_o, r.wt_o), (r.w_up, r.wt_up), (r.w_down, r.wt_down)):
            dst[l] = src[l].T
    ki = lax.broadcasted_iota(jnp.int32, (256, 256), 0)
    qi = lax.broadcasted_iota(jnp.int32, (256, 256), 1)
    r.mask[...] = jnp.where(ki <= qi, 0.0, MASKED)
    r.acc[...] = jnp.zeros_like(r.acc)
    r.sg[...] = jnp.zeros_like(r.sg)

    def prompt(p, _):
        count = counts[p]
        cp = pltpu.make_async_copy(emb.at[rows[p]], r.io, r.sem)
        cp.start()
        cp.wait()
        r.embT[...] = r.io[...].T
        r.cur[...] = jnp.zeros_like(r.cur)

        def forward(j):
            r.cur[...] = r.cur[...] + r.embT[...]

            def fl(l, _):
                layer_fwd(r, l, lax.rem(j, S) * 2 + l, T, D)
                return 0

            lax.fori_loop(0, 2, fl, 0)

        def floop(j, _):
            if redo:
                r.hs[j] = r.cur[...]
            forward(j)
            return 0

        lax.fori_loop(0, count, floop, 0)
        r.io[...] = r.cur[...].T
        cp = pltpu.make_async_copy(r.io, fin.at[p], r.sem)
        cp.start()
        cp.wait()
        cp = pltpu.make_async_copy(cot.at[rows[p]], r.io, r.sem)
        cp.start()
        cp.wait()
        r.dcur[...] = r.io[...].T
        r.gsum[...] = jnp.zeros_like(r.gsum)

        def bloop(jj, _):
            j = count - 1 - jj
            if redo:

                @pl.when(jj >= S)
                def _():
                    r.cur[...] = r.hs[j]
                    forward(j)

            def bl(ll, _):
                l = 1 - ll
                layer_bwd(r, l, lax.rem(j, S) * 2 + l, T, D)
                return 0

            lax.fori_loop(0, 2, bl, 0)
            r.gsum[...] = r.gsum[...] + r.dcur[...]
            return 0

        lax.fori_loop(0, count, bloop, 0)
        r.io[...] = r.gsum[...].T
        cp = pltpu.make_async_copy(r.io, eg.at[p], r.sem)
        cp.start()
        cp.wait()
        return 0

    lax.fori_loop(0, nprompts, prompt, 0)


def call(N, counts, place, rows, emb, cot, tiles, pbr, unroll=2):
    S = N if N <= 4 else 2
    n = counts.shape[0]
    _, T, D = emb.shape
    V = pltpu.VMEM
    H = 4 * D
    scr = [
        V((2, 9 * D, 128), F32), V((2, 3 * D, D), BF16), V((2, D, D), BF16), V((2, H, D), BF16), V((2, D, H), BF16),
        V((2, D, 3 * D), BF16), V((2, D, D), BF16), V((2, D, H), BF16), V((2, H, D), BF16),
        V((256, 256), F32),
        V((D, T), F32), V((D, T), F32), V((D, T), F32), V((D, T), F32), V((T, D), F32),
        V((D, T), BF16), V((D, T), BF16), V((D, T), F32), V((H, T), BF16), V((H, T), BF16),
        V((D, T), BF16), V((D, T), BF16), V((D, T), BF16), V((3 * D, T), BF16),
        V((2 * S, D, T), F32), V((2 * S, 3 * D, T), BF16),
        V((2 * S, HEADS, T * (T // 256 + 1) // 2, 256), BF16), V((2 * S, HEADS, T), F32), V((2 * S, D, T), BF16),
        pltpu.SemaphoreType.DMA,
    ]
    if N > S:
        scr.append(V((N, D, T), F32))
    A = pl.BlockSpec(memory_space=pl.ANY)
    VM = pl.BlockSpec(memory_space=pltpu.VMEM)
    SM = pl.BlockSpec(memory_space=pltpu.SMEM)
    return pl.pallas_call(
        functools.partial(kernel, S, N, unroll, n),
        out_shape=(
            jax.ShapeDtypeStruct((n, T, D), F32), jax.ShapeDtypeStruct((n, T, D), F32),
            jax.ShapeDtypeStruct((48, 128, D), F32), jax.ShapeDtypeStruct((2, 9 * D, 128), F32)),
        in_specs=[SM, SM, SM, A, A, A, VM],
        out_specs=(A, A, VM, VM),
        scratch_shapes=scr,
        compiler_params=pltpu.CompilerParams(vmem_limit_bytes=63 * 1024 * 1024),
    )(counts, place, rows, emb, cot, tiles, pbr)


STEP = 10
beta_one = 0.9
beta_two = 0.999
learn_rate = 0.05
small_rate = 0.3
weight_decay = 0.1
adam_eps = 1e-08


def adam_update(gradient, first_old, second_old, weight, decay_rate, rate):
    first_new = beta_one * first_old + (1.0 - beta_one) * gradient
    second_new = beta_two * second_old + (1.0 - beta_two) * gradient * gradient
    corr_one = 1.0 - beta_one**STEP
    corr_two = 1.0 - beta_two**STEP
    update = first_new / corr_one / (jnp.sqrt(second_new / corr_two) + adam_eps)
    return (first_new, second_new, weight - rate * (update + decay_rate * weight))


def ranks(key, falling):
    n = key.shape[0]
    i = jnp.arange(n)
    ahead = (key[None, :] > key[:, None]) if falling else (key[None, :] < key[:, None])
    tie = (key[None, :] == key[:, None]) & (i[None, :] < i[:, None])
    return jnp.sum((ahead | tie).astype(jnp.int32), axis=1)


def shards(embedding, cotangent, counts, owner_list, tiles_owned, first_owned, second_owned,
           small_params, small_first, small_second):
    N = lax.axis_size("section")
    s = lax.axis_index("section")
    P_, T, D = embedding.shape
    place = ranks(owner_list, False)
    tiles = lax.all_gather(tiles_owned.astype(BF16), "dp", axis=0, tiled=True)
    rank = ranks(counts, True)
    nslot = -(-P_ // N)
    want = jnp.stack([k * N + (s if k % 2 == 0 else N - 1 - s) for k in range(nslot)])
    hit = want[:, None] == rank[None, :]
    my_rows = jnp.sum(jnp.where(hit, jnp.arange(P_)[None, :], 0), axis=1).astype(jnp.int32)
    my_counts = jnp.sum(jnp.where(hit, counts[None, :], 0), axis=1).astype(jnp.int32)
    fin, eg, gt, sg = call(N, my_counts, place, my_rows, embedding, cotangent, tiles, small_params, unroll=8)
    k = rank // N
    q = rank % N
    w = jnp.where(k % 2 == 0, q, N - 1 - q)
    at = k * N + w

    def spread(v):
        got = lax.all_to_all(v.reshape(nslot, N, T // N, D), "section", split_axis=1, concat_axis=1, tiled=True)
        got = got.reshape(nslot * N, T // N, D)
        return jnp.concatenate([lax.dynamic_slice_in_dim(got, at[p], 1, 0) for p in range(P_)], axis=0)

    fin, eg = spread(fin), spread(eg)
    tile_grad = lax.psum(lax.psum_scatter(gt, "dp", scatter_dimension=0, tiled=True), "section")
    small_grad = lax.psum(jnp.sum(sg, axis=-1).reshape(18, D), ("section", "dp"))
    tile_first, tile_second, tile_new = adam_update(
        tile_grad, first_owned, second_owned, tiles_owned, weight_decay, learn_rate
    )
    small_first_new, small_second_new, small_new = adam_update(
        small_grad, small_first, small_second, small_params, 0.0, small_rate
    )
    return (fin, eg, tile_grad, tile_first, tile_second, tile_new,
            small_grad, small_first_new, small_second_new, small_new)


def solution(mesh):
    P = jax.sharding.PartitionSpec
    own, rep = P("dp", None, None), P()
    return jax.shard_map(
        shards,
        mesh=mesh,
        in_specs=(own, own, P("dp"), rep, own, own, own, rep, rep, rep),
        out_specs=(P("dp", "section", None),) * 2 + (own,) * 4 + (rep,) * 4,
        check_vma=False,
    )
```

```python
import functools, math
import jax
import jax.numpy as jnp
from jax import lax
from jax.experimental import pallas as pl
from jax.experimental.pallas import tpu as pltpu

F32, BF16 = jnp.float32, jnp.bfloat16
HEADS = 8
EPS = 1e-5
MASKED = -1e30
GC0 = math.sqrt(2.0 / math.pi)
GC1 = 0.044715


def nn(a, b):
    return lax.dot_general(a, b, (((1,), (0,)), ((), ())), preferred_element_type=F32)


def nt(a, b):
    return lax.dot_general(a, b, (((1,), (1,)), ((), ())), preferred_element_type=F32)


def tn(a, b):
    return lax.dot_general(a, b, (((0,), (0,)), ((), ())), preferred_element_type=F32)


def wide(col, n):
    return jnp.concatenate([col] * (n // 128), axis=1)


def fold(a):
    r = a[:, 0:128]
    for i in range(1, a.shape[1] // 128):
        r = r + a[:, 128 * i : 128 * i + 128]
    return r


def normed(x):
    d = x.shape[0]
    mean = jnp.sum(x, axis=0, keepdims=True) * (1.0 / d)
    xc = x - mean
    var = jnp.sum(xc * xc, axis=0, keepdims=True) * (1.0 / d)
    rstd = lax.rsqrt(var + EPS)
    return xc * rstd, rstd


def norm_back(dn, xhat, rstd, gain):
    d = dn.shape[0]
    dx = dn * gain
    a = jnp.sum(dx, axis=0, keepdims=True) * (1.0 / d)
    b = jnp.sum(dx * xhat, axis=0, keepdims=True) * (1.0 / d)
    return rstd * (dx - a - xhat * b)


def staged(jobs, first, second, third):
    a = first(*jobs[0])
    done = None
    for i, job in enumerate(jobs):
        ahead = first(*jobs[i + 1]) if i + 1 < len(jobs) else None
        b = second(*job, a)
        if done is not None:
            third(*done)
        done = job + (b,)
        a = ahead
    third(*done)


class R:
    pass


def layer_fwd(r, l, sl, T, D):
    hd = D // HEADS
    pr = lambda k, n=1: r.pb[l, pl.ds(k * D, n * D), :]
    x = r.cur[...]
    r.xs[sl] = x
    xhat, _ = normed(x)
    r.n1[...] = (xhat * wide(pr(0), T) + wide(pr(1), T)).astype(BF16)
    c2 = hd**-0.5 * math.log2(math.e)
    for i in range(3):
        v = nn(r.wt_qkv[l, pl.ds(i * D, D), :], r.n1[...])
        r.qkv[sl, pl.ds(i * D, D), :] = (v * c2 if i == 0 else v).astype(BF16)
    ones16 = jnp.ones((16, T), BF16)
    jobs = [(h, b) for h in range(HEADS) for b in range(T // 256)]

    def scores(h, b):
        kk = 256 * (b + 1)
        k = r.qkv[sl, pl.ds(D + h * hd, hd), pl.ds(0, kk)]
        return tn(k, r.qkv[sl, pl.ds(h * hd, hd), pl.ds(256 * b, 256)])

    def probs(h, b, s):
        kk = 256 * (b + 1)
        tail = s[kk - 256 :, :] + r.mask[...]
        mx = jnp.max(tail, axis=0, keepdims=True)
        if b == 0:
            e = jnp.exp2(tail - mx).astype(BF16)
        else:
            lead = s[: kk - 256, :]
            mx = jnp.maximum(mx, jnp.max(lead, axis=0, keepdims=True))
            e = jnp.concatenate([jnp.exp2(lead - mx).astype(BF16), jnp.exp2(tail - mx).astype(BF16)], axis=0)
        r.es[sl, h, pl.ds(128 * b * (b + 1), kk), :] = e
        return e

    def context(h, b, e):
        kk = 256 * (b + 1)
        v = r.qkv[sl, pl.ds(2 * D + h * hd, hd), pl.ds(0, kk)]
        o = nn(jnp.concatenate([v, ones16[:, :kk]], axis=0), e)
        linv = 1.0 / o[hd : hd + 1, :]
        r.linv[sl, pl.ds(h, 1), pl.ds(256 * b, 256)] = linv
        r.ctx[sl, pl.ds(h * hd, hd), pl.ds(256 * b, 256)] = (o[:hd, :] * linv).astype(BF16)

    staged(jobs, scores, probs, context)
    m = r.xs[sl] + nn(r.wt_o[l], r.ctx[sl])
    r.cur[...] = m
    mhat, _ = normed(m)
    r.n2[...] = (mhat * wide(pr(2), T) + wide(pr(3), T)).astype(BF16)
    for i in range(4):
        u = nn(r.wt_up[l, pl.ds(i * D, D), :], r.n2[...]) + wide(pr(4 + i), T)
        t = jnp.tanh(u * (GC0 + (GC0 * GC1) * (u * u)))
        hu = 0.5 * u
        r.g[pl.ds(i * D, D), :] = (hu + hu * t).astype(BF16)
    r.cur[...] = r.cur[...] + nn(r.wt_down[l], r.g[...]) + wide(pr(8), T)


def layer_bwd(r, l, sl, T, D):
    hd = D // HEADS
    c = hd**-0.5
    pr = lambda k, n=1: r.pb[l, pl.ds(k * D, n * D), :]

    def add_small(k, v):
        r.sg[l, pl.ds(k * D, D), :] = r.sg[l, pl.ds(k * D, D), :] + fold(v)

    dy = r.dcur[...]
    r.dylow[...] = dy.astype(BF16)
    add_small(8, dy)
    mhat, rstd2 = normed(r.xs[sl] + nn(r.wt_o[l], r.ctx[sl]))
    r.hat[...] = mhat
    r.n2[...] = (mhat * wide(pr(2), T) + wide(pr(3), T)).astype(BF16)
    for i in range(4):
        u = nn(r.wt_up[l, pl.ds(i * D, D), :], r.n2[...]) + wide(pr(4 + i), T)
        u2 = u * u
        t = jnp.tanh(u * (GC0 + (GC0 * GC1) * u2))
        hu = 0.5 * u
        r.g[pl.ds(i * D, D), :] = (hu + hu * t).astype(BF16)
        gp = (0.5 + 0.5 * t) + (hu - hu * t * t) * (GC0 + (3.0 * GC0 * GC1) * u2)
        du = gp * nn(r.w_down[l, pl.ds(i * D, D), :], r.dylow[...])
        add_small(4 + i, du)
        r.du[pl.ds(i * D, D), :] = du.astype(BF16)
    dn2 = nn(r.w_up[l], r.du[...])
    add_small(2, dn2 * r.hat[...])
    add_small(3, dn2)
    dm = r.dcur[...] + norm_back(dn2, r.hat[...], rstd2, wide(pr(2), T))
    r.dcur[...] = dm
    r.dmlow[...] = dm.astype(BF16)

    def add_tiles(t, v, gap=1):
        for a in range(2):
            at = r.place[24 * l + t + gap * a]
            r.acc[at] = r.acc[at] + v[128 * a : 128 * a + 128]

    for i in range(4):
        add_tiles(16 + 2 * i, nt(r.g[pl.ds(i * D, D), :], r.dylow[...]))
    for i in range(4):
        add_tiles(8 + i, nt(r.n2[...], r.du[pl.ds(i * D, D), :]), 4)
    add_tiles(6, nt(r.ctx[sl], r.dmlow[...]))
    dctx = nn(r.w_o[l], r.dmlow[...])
    for h in range(HEADS):
        hs = slice(h * hd, h * hd + hd)
        r.dctx[hs, :] = (dctx[hs, :] * (r.linv[sl, pl.ds(h, 1), :] * c)).astype(BF16)
    c2 = hd**-0.5 * math.log2(math.e)
    nb = T // 256
    row = lax.broadcasted_iota(jnp.int32, (16, T), 0)
    ones3 = jnp.where(row < 3, 1.0, 0.0).astype(BF16)
    dks = [[None] * nb for _ in range(HEADS)]
    dvs = [[None] * nb for _ in range(HEADS)]
    jobs = [(h, b) for h in range(HEADS) for b in range(nb)]

    def back_probs(h, b):
        kk = 256 * (b + 1)
        qs = pl.ds(256 * b, 256)
        dctx = r.dctx[pl.ds(h * hd, hd), qs]
        ctx = r.ctx[sl, pl.ds(h * hd, hd), qs].astype(F32)
        nd = -jnp.sum(dctx.astype(F32) * ctx, axis=0, keepdims=True)
        n0 = nd.astype(BF16).astype(F32)
        n1 = (nd - n0).astype(BF16).astype(F32)
        n2 = nd - n0 - n1
        rw = row[:, :256]
        extra = jnp.where(rw == 0, n0, jnp.where(rw == 1, n1, jnp.where(rw == 2, n2, 0.0))).astype(BF16)
        de = jnp.concatenate([dctx, extra], axis=0)
        ve = jnp.concatenate([r.qkv[sl, pl.ds(2 * D + h * hd, hd), pl.ds(0, kk)], ones3[:, :kk]], axis=0)
        return tn(ve, de)

    def back_scores(h, b, dsr):
        e = r.es[sl, h, pl.ds(128 * b * (b + 1), 256 * (b + 1)), :]
        return (e.astype(F32) * dsr).astype(BF16)

    def back_heads(h, b, ds):
        kk = 256 * (b + 1)
        qs = pl.ds(256 * b, 256)
        e = r.es[sl, h, pl.ds(128 * b * (b + 1), kk), :]
        k = r.qkv[sl, pl.ds(D + h * hd, hd), pl.ds(0, kk)]
        r.dqkv[pl.ds(h * hd, hd), qs] = nn(k, ds).astype(BF16)
        dkb = nt(r.qkv[sl, pl.ds(h * hd, hd), qs], ds)
        dvb = nt(r.dctx[pl.ds(h * hd, hd), qs], e)
        for j in range(b + 1):
            js = slice(256 * j, 256 * j + 256)
            dks[h][j] = dkb[:, js] if dks[h][j] is None else dks[h][j] + dkb[:, js]
            dvs[h][j] = dvb[:, js] if dvs[h][j] is None else dvs[h][j] + dvb[:, js]
        if b == nb - 1:
            for j in range(nb):
                r.dqkv[pl.ds(D + h * hd, hd), pl.ds(256 * j, 256)] = (dks[h][j] * (1.0 / c2)).astype(BF16)
                r.dqkv[pl.ds(2 * D + h * hd, hd), pl.ds(256 * j, 256)] = (dvs[h][j] * (1.0 / c)).astype(BF16)

    staged(jobs, back_probs, back_scores, back_heads)
    xhat, rstd1 = normed(r.xs[sl])
    r.hat[...] = xhat
    r.n1[...] = (xhat * wide(pr(0), T) + wide(pr(1), T)).astype(BF16)
    for i in range(3):
        add_tiles(2 * i, nt(r.n1[...], r.dqkv[pl.ds(i * D, D), :]))
    dn1 = nn(r.w_qkv[l], r.dqkv[...])
    add_small(0, dn1 * r.hat[...])
    add_small(1, dn1)
    r.dcur[...] = r.dcur[...] + norm_back(dn1, r.hat[...], rstd1, wide(pr(0), T))


def kernel(S, N, nprompts, counts, place, src, rows, emb, cot, tiles, pbr, fe, gt, sgo, *scr):
    r = R()
    (r.pb, r.wt_qkv, r.wt_o, r.wt_up, r.wt_down, r.w_qkv, r.w_o, r.w_up, r.w_down, r.mask,
     r.cur, r.dcur, r.embT, r.gsum, r.io, r.n1, r.n2, r.hat, r.g, r.du, r.dylow, r.dmlow, r.dctx, r.dqkv,
     r.xs, r.qkv, r.es, r.linv, r.ctx, r.sg, r.low, r.sem) = scr[:32]
    redo = N > S
    if redo:
        r.hs = scr[32]
    r.acc, r.place = gt, place
    T, D = r.io.shape
    C = T // N

    def spot(l, row, n):
        t, o = row // 128, row % 128
        if t < 6:
            return r.w_qkv.at[l, pl.ds(t % 2 * 128 + o, n), pl.ds(t // 2 * D, D)]
        if t < 8:
            return r.w_o.at[l, pl.ds((t - 6) * 128 + o, n), :]
        if t < 16:
            return r.w_up.at[l, pl.ds((t - 8) // 4 * 128 + o, n), pl.ds((t - 8) % 4 * D, D)]
        return r.w_down.at[l, pl.ds((t - 16) * 128 + o, n), :]

    cps = []
    for l in range(2):
        for i in range(48):
            cps.append(pltpu.make_async_copy(tiles.at[src[48 * l + i]], spot(l, 64 * i, 64), r.sem))
    for cp in cps:
        cp.start()
    for k in range(18):
        r.pb[k // 9, k % 9 * D : k % 9 * D + D, :] = jnp.broadcast_to(pbr[k : k + 1, :], (128, D)).T
    for cp in cps:
        cp.wait()
    for l in range(2):
        for src, dst in ((r.w_qkv, r.wt_qkv), (r.w_o, r.wt_o), (r.w_up, r.wt_up), (r.w_down, r.wt_down)):
            dst[l] = src[l].T
    ki = lax.broadcasted_iota(jnp.int32, (256, 256), 0)
    qi = lax.broadcasted_iota(jnp.int32, (256, 256), 1)
    r.mask[...] = jnp.where(ki <= qi, 0.0, MASKED)
    r.acc[...] = jnp.zeros_like(r.acc)
    r.sg[...] = jnp.zeros_like(r.sg)

    def prompt(p, _):
        count = counts[p]
        cp = pltpu.make_async_copy(emb.at[rows[p]], r.io, r.sem)
        cp.start()
        cp.wait()
        r.embT[...] = r.io[...].T
        r.cur[...] = jnp.zeros_like(r.cur)

        def forward(j):
            r.cur[...] = r.cur[...] + r.embT[...]

            def fl(l, _):
                layer_fwd(r, l, lax.rem(j, S) * 2 + l, T, D)
                return 0

            lax.fori_loop(0, 2, fl, 0)

        def floop(j, _):
            if redo:
                r.hs[j] = r.cur[...]
            forward(j)
            return 0

        lax.fori_loop(0, count, floop, 0)
        r.low[...] = r.cur[...].T.astype(BF16)
        cps = [pltpu.make_async_copy(r.low.at[pl.ds(C * i, C), :], fe.at[i, 0, p], r.sem) for i in range(N)]
        for cp in cps:
            cp.start()
        for cp in cps:
            cp.wait()
        cp = pltpu.make_async_copy(cot.at[rows[p]], r.io, r.sem)
        cp.start()
        cp.wait()
        r.dcur[...] = r.io[...].T
        r.gsum[...] = jnp.zeros_like(r.gsum)

        def bloop(jj, _):
            j = count - 1 - jj
            if redo:

                @pl.when(jj >= S)
                def _():
                    r.cur[...] = r.hs[j]
                    forward(j)

            def bl(ll, _):
                l = 1 - ll
                layer_bwd(r, l, lax.rem(j, S) * 2 + l, T, D)
                return 0

            lax.fori_loop(0, 2, bl, 0)
            r.gsum[...] = r.gsum[...] + r.dcur[...]
            return 0

        lax.fori_loop(0, count, bloop, 0)
        r.low[...] = r.gsum[...].T.astype(BF16)
        cps = [pltpu.make_async_copy(r.low.at[pl.ds(C * i, C), :], fe.at[i, 1, p], r.sem) for i in range(N)]
        for cp in cps:
            cp.start()
        for cp in cps:
            cp.wait()
        return 0

    lax.fori_loop(0, nprompts, prompt, 0)
    for k in range(18):
        part = r.sg[k // 9, k % 9 * D : k % 9 * D + D, :].T
        sgo[k : k + 1, :] = jnp.sum(part, axis=0, keepdims=True)


def call(N, counts, place, src, rows, emb, cot, tiles, pbr):
    S = N if N <= 4 else 2
    n = counts.shape[0]
    _, T, D = emb.shape
    V = pltpu.VMEM
    H = 4 * D
    scr = [
        V((2, 9 * D, 128), F32), V((2, 3 * D, D), BF16), V((2, D, D), BF16), V((2, H, D), BF16), V((2, D, H), BF16),
        V((2, D, 3 * D), BF16), V((2, D, D), BF16), V((2, D, H), BF16), V((2, H, D), BF16),
        V((256, 256), F32),
        V((D, T), F32), V((D, T), F32), V((D, T), F32), V((D, T), F32), V((T, D), F32),
        V((D, T), BF16), V((D, T), BF16), V((D, T), F32), V((H, T), BF16), V((H, T), BF16),
        V((D, T), BF16), V((D, T), BF16), V((D, T), BF16), V((3 * D, T), BF16),
        V((2 * S, D, T), F32), V((2 * S, 3 * D, T), BF16),
        V((2 * S, HEADS, T * (T // 256 + 1) // 2, 256), BF16), V((2 * S, HEADS, T), F32), V((2 * S, D, T), BF16),
        V((2, 9 * D, 128), F32), V((T, D), BF16),
        pltpu.SemaphoreType.DMA,
    ]
    if N > S:
        scr.append(V((N, D, T), F32))
    A = pl.BlockSpec(memory_space=pl.ANY)
    VM = pl.BlockSpec(memory_space=pltpu.VMEM)
    SM = pl.BlockSpec(memory_space=pltpu.SMEM)
    return pl.pallas_call(
        functools.partial(kernel, S, N, n),
        out_shape=(
            jax.ShapeDtypeStruct((N, 2, n, T // N, D), BF16),
            jax.ShapeDtypeStruct((48, 128, D), F32), jax.ShapeDtypeStruct((18, D), F32)),
        in_specs=[SM, SM, SM, SM, A, A, A, VM],
        out_specs=(A, VM, VM),
        scratch_shapes=scr,
        compiler_params=pltpu.CompilerParams(vmem_limit_bytes=63 * 1024 * 1024),
    )(counts, place, src, rows, emb, cot, tiles, pbr)


STEP = 10
beta_one = 0.9
beta_two = 0.999
learn_rate = 0.05
small_rate = 0.3
weight_decay = 0.1
adam_eps = 1e-08


def adam_update(gradient, first_old, second_old, weight, decay_rate, rate):
    first_new = beta_one * first_old + (1.0 - beta_one) * gradient
    second_new = beta_two * second_old + (1.0 - beta_two) * gradient * gradient
    corr_one = 1.0 - beta_one**STEP
    corr_two = 1.0 - beta_two**STEP
    update = first_new / corr_one / (jnp.sqrt(second_new / corr_two) + adam_eps)
    return (first_new, second_new, weight - rate * (update + decay_rate * weight))


def ranks(key, falling):
    n = key.shape[0]
    i = jnp.arange(n)
    ahead = (key[None, :] > key[:, None]) if falling else (key[None, :] < key[:, None])
    tie = (key[None, :] == key[:, None]) & (i[None, :] < i[:, None])
    return jnp.sum((ahead | tie).astype(jnp.int32), axis=1)


def swap(v, axis, k):
    n = lax.axis_size(axis)
    return lax.ppermute(v, axis, [(i, i ^ k) for i in range(n)])


def pick(v, i, axis):
    return lax.dynamic_index_in_dim(v, i, axis, keepdims=False)


def gather_tiles(own, N, Z, s):
    rows, D = own.shape
    part = pick(own.reshape(N, rows // N, D), s, 0)
    zs = jnp.stack([part] + [swap(part, "dp", 2 * k) for k in range(1, Z)])
    near = [zs] + [swap(zs, "section", k) for k in range(1, N)]
    far = [swap(v, "dp", 1) for v in near]
    return jnp.stack(near + far)


def reduce_tiles(gt, N, Z, s, z, own_rows):
    D = gt.shape[-1]
    half = Z * own_rows
    R = own_rows // N
    got = swap(gt[half:].astype(BF16), "dp", 1)
    part = (gt[:half] + got.astype(F32)).reshape(Z, N, R, D)
    got = [swap(pick(part, s ^ k, 1).astype(BF16), "section", k) for k in range(1, N)]
    part = pick(part, s, 1)
    for v in got:
        part = part + v.astype(F32)
    got = [swap(pick(part, z ^ k, 0).astype(BF16), "dp", 2 * k) for k in range(1, Z)]
    part = pick(part, z, 0)
    for v in got:
        part = part + v.astype(F32)
    part = part.astype(BF16)
    every = jnp.stack([part] + [swap(part, "section", k) for k in range(1, N)])
    return jnp.concatenate([pick(every, s ^ j, 0) for j in range(N)], axis=0).astype(F32)


def reduce_small(v, N, DP):
    for axis, n in (("dp", DP), ("section", N)):
        k = 1
        while k < n:
            v = v + swap(v, axis, k)
            k *= 2
    return v


def order_kernel(N, slots, at, *refs):
    ins, fin, eg = refs[:N], refs[N], refs[N + 1]

    def put(p, _):
        w = at[p]
        for k in range(N):
            for j in range(slots):

                @pl.when(w == k * slots + j)
                def _():
                    fin[p] = ins[k][0, j].astype(F32)
                    eg[p] = ins[k][1, j].astype(F32)

        return 0

    lax.fori_loop(0, fin.shape[0], put, 0)


def in_order(pieces, at, prompts):
    _, slots, C, D = pieces[0].shape
    N = len(pieces)
    VM = pl.BlockSpec(memory_space=pltpu.VMEM)
    out = jax.ShapeDtypeStruct((prompts, C, D), F32)
    return pl.pallas_call(
        functools.partial(order_kernel, N, slots),
        out_shape=(out, out),
        in_specs=[pl.BlockSpec(memory_space=pltpu.SMEM)] + [VM] * N,
        out_specs=(VM, VM),
        compiler_params=pltpu.CompilerParams(vmem_limit_bytes=32 * 1024 * 1024),
    )(at, *pieces)


def shards(embedding, cotangent, counts, owner_list, tiles_owned, first_owned, second_owned,
           small_params, small_first, small_second):
    N, DP = lax.axis_size("section"), lax.axis_size("dp")
    Z = DP // 2
    s, dp = lax.axis_index("section"), lax.axis_index("dp")
    z, c = dp // 2, dp % 2
    PR, T, D = embedding.shape
    OWN = tiles_owned.shape[0]
    own_rows = OWN * 128
    R = own_rows // N
    rank = ranks(owner_list, False)
    owner, slot = rank // OWN, rank % OWN
    place = ((owner % 2) ^ c) * (Z * OWN) + owner // 2 * OWN + slot
    low = tiles_owned.astype(BF16)
    halves = 2 * slot[:, None] + jnp.arange(2)[None, :]
    if R % 64 == 0:
        tiles = gather_tiles(low.reshape(own_rows, D), N, Z, s)
        per = R // 64
        src = (((owner % 2) ^ c)[:, None] * N + ((halves // per) ^ s)) * Z + ((owner // 2) ^ z)[:, None]
        src = src * per + halves % per
    else:
        tiles = lax.all_gather(low, "dp", axis=0, tiled=True)
        src = owner[:, None] * (2 * OWN) + halves
    rank = ranks(counts, True)
    nslot = -(-PR // N)
    want = jnp.stack([k * N + (s if k % 2 == 0 else N - 1 - s) for k in range(nslot)])
    hit = want[:, None] == rank[None, :]
    my_rows = jnp.sum(jnp.where(hit, jnp.arange(PR)[None, :], 0), axis=1).astype(jnp.int32)
    my_counts = jnp.sum(jnp.where(hit, counts[None, :], 0), axis=1).astype(jnp.int32)
    fe, gt, sg = call(N, my_counts, place, src.reshape(-1), my_rows, embedding, cotangent,
                      tiles.reshape(-1, 64, D), small_params)
    k = rank // N
    q = rank % N
    w = jnp.where(k % 2 == 0, q, N - 1 - q)
    pieces = [pick(fe, s, 0)] + [swap(pick(fe, s ^ k, 0), "section", k) for k in range(1, N)]
    tile_grad = reduce_tiles(gt.reshape(-1, D), N, Z, s, z, own_rows).reshape(OWN, 128, D)
    small_grad = reduce_small(sg, N, DP)
    fin, eg = in_order(pieces, (w ^ s) * nslot + k, PR)
    tile_first, tile_second, tile_new = adam_update(
        tile_grad, first_owned, second_owned, tiles_owned, weight_decay, learn_rate
    )
    small_first_new, small_second_new, small_new = adam_update(
        small_grad, small_first, small_second, small_params, 0.0, small_rate
    )
    return (fin, eg, tile_grad, tile_first, tile_second, tile_new,
            small_grad, small_first_new, small_second_new, small_new)


def solution(mesh):
    P = jax.sharding.PartitionSpec
    own, rep = P("dp", None, None), P()
    return jax.shard_map(
        shards,
        mesh=mesh,
        in_specs=(own, own, P("dp"), rep, own, own, own, rep, rep, rep),
        out_specs=(P("dp", "section", None),) * 2 + (own,) * 4 + (rep,) * 4,
        check_vma=False,
    )
```

```python
import functools
import itertools
import math

import jax
import jax.numpy as jnp
import numpy as np
from jax import lax
from jax.experimental import pallas as pl
from jax.experimental.pallas import tpu as pltpu

F32, BF16 = jnp.float32, jnp.bfloat16
HEADS = 8
EPS = 1e-5
MASKED = -1e30
GC0 = math.sqrt(2.0 / math.pi)
GC1 = 0.044715


def nn(a, b):
    return lax.dot_general(a, b, (((1,), (0,)), ((), ())), preferred_element_type=F32)


def nt(a, b):
    return lax.dot_general(a, b, (((1,), (1,)), ((), ())), preferred_element_type=F32)


def tn(a, b):
    return lax.dot_general(a, b, (((0,), (0,)), ((), ())), preferred_element_type=F32)


def wide(col, n):
    return jnp.concatenate([col] * (n // 128), axis=1)


def fold(a):
    r = a[:, 0:128]
    for i in range(1, a.shape[1] // 128):
        r = r + a[:, 128 * i : 128 * i + 128]
    return r


def normed(x):
    d = x.shape[0]
    mean = jnp.sum(x, axis=0, keepdims=True) * (1.0 / d)
    xc = x - mean
    var = jnp.sum(xc * xc, axis=0, keepdims=True) * (1.0 / d)
    rstd = lax.rsqrt(var + EPS)
    return xc * rstd, rstd


def norm_back(dn, xhat, rstd, gain):
    d = dn.shape[0]
    dx = dn * gain
    a = jnp.sum(dx, axis=0, keepdims=True) * (1.0 / d)
    b = jnp.sum(dx * xhat, axis=0, keepdims=True) * (1.0 / d)
    return rstd * (dx - a - xhat * b)


def staged(jobs, first, second, third):
    a = first(*jobs[0])
    done = None
    for i, job in enumerate(jobs):
        ahead = first(*jobs[i + 1]) if i + 1 < len(jobs) else None
        b = second(*job, a)
        if done is not None:
            third(*done)
        done = job + (b,)
        a = ahead
    third(*done)


class R:
    pass


def layer_fwd(r, l, sl, T, D):
    hd = D // HEADS
    pr = lambda k, n=1: r.pb[l, pl.ds(k * D, n * D), :]
    x = r.cur[...]
    r.xs[sl] = x
    xhat, _ = normed(x)
    r.n1[...] = (xhat * wide(pr(0), T) + wide(pr(1), T)).astype(BF16)
    c2 = hd**-0.5 * math.log2(math.e)
    for i in range(3):
        v = nn(r.wt_qkv[l, pl.ds(i * D, D), :], r.n1[...])
        r.qkv[sl, pl.ds(i * D, D), :] = (v * c2 if i == 0 else v).astype(BF16)
    ones16 = jnp.ones((16, T), BF16)
    jobs = [(h, b) for h in range(HEADS) for b in range(T // 256)]

    def scores(h, b):
        kk = 256 * (b + 1)
        k = r.qkv[sl, pl.ds(D + h * hd, hd), pl.ds(0, kk)]
        return tn(k, r.qkv[sl, pl.ds(h * hd, hd), pl.ds(256 * b, 256)])

    def probs(h, b, s):
        kk = 256 * (b + 1)
        tail = s[kk - 256 :, :] + r.mask[...]
        mx = jnp.max(tail, axis=0, keepdims=True)
        if b == 0:
            e = jnp.exp2(tail - mx).astype(BF16)
        else:
            lead = s[: kk - 256, :]
            mx = jnp.maximum(mx, jnp.max(lead, axis=0, keepdims=True))
            e = jnp.concatenate([jnp.exp2(lead - mx).astype(BF16), jnp.exp2(tail - mx).astype(BF16)], axis=0)
        r.es[sl, h, pl.ds(128 * b * (b + 1), kk), :] = e
        return e

    def context(h, b, e):
        kk = 256 * (b + 1)
        v = r.qkv[sl, pl.ds(2 * D + h * hd, hd), pl.ds(0, kk)]
        o = nn(jnp.concatenate([v, ones16[:, :kk]], axis=0), e)
        linv = 1.0 / o[hd : hd + 1, :]
        r.linv[sl, pl.ds(h, 1), pl.ds(256 * b, 256)] = linv
        r.ctx[sl, pl.ds(h * hd, hd), pl.ds(256 * b, 256)] = (o[:hd, :] * linv).astype(BF16)

    staged(jobs, scores, probs, context)
    m = r.xs[sl] + nn(r.wt_o[l], r.ctx[sl])
    r.cur[...] = m
    mhat, _ = normed(m)
    r.n2[...] = (mhat * wide(pr(2), T) + wide(pr(3), T)).astype(BF16)
    for i in range(4):
        u = nn(r.wt_up[l, pl.ds(i * D, D), :], r.n2[...]) + wide(pr(4 + i), T)
        t = jnp.tanh(u * (GC0 + (GC0 * GC1) * (u * u)))
        hu = 0.5 * u
        r.g[pl.ds(i * D, D), :] = (hu + hu * t).astype(BF16)
    r.cur[...] = r.cur[...] + nn(r.wt_down[l], r.g[...]) + wide(pr(8), T)


def layer_bwd(r, l, sl, T, D):
    hd = D // HEADS
    c = hd**-0.5
    pr = lambda k, n=1: r.pb[l, pl.ds(k * D, n * D), :]

    def add_small(k, v):
        r.sg[l, pl.ds(k * D, D), :] = r.sg[l, pl.ds(k * D, D), :] + fold(v)

    dy = r.dcur[...]
    r.dylow[...] = dy.astype(BF16)
    add_small(8, dy)
    mhat, rstd2 = normed(r.xs[sl] + nn(r.wt_o[l], r.ctx[sl]))
    r.hat[...] = mhat
    r.n2[...] = (mhat * wide(pr(2), T) + wide(pr(3), T)).astype(BF16)
    for i in range(4):
        u = nn(r.wt_up[l, pl.ds(i * D, D), :], r.n2[...]) + wide(pr(4 + i), T)
        u2 = u * u
        t = jnp.tanh(u * (GC0 + (GC0 * GC1) * u2))
        hu = 0.5 * u
        r.g[pl.ds(i * D, D), :] = (hu + hu * t).astype(BF16)
        gp = (0.5 + 0.5 * t) + (hu - hu * t * t) * (GC0 + (3.0 * GC0 * GC1) * u2)
        du = gp * nn(r.w_down[l, pl.ds(i * D, D), :], r.dylow[...])
        add_small(4 + i, du)
        r.du[pl.ds(i * D, D), :] = du.astype(BF16)
    dn2 = nn(r.w_up[l], r.du[...])
    add_small(2, dn2 * r.hat[...])
    add_small(3, dn2)
    dm = r.dcur[...] + norm_back(dn2, r.hat[...], rstd2, wide(pr(2), T))
    r.dcur[...] = dm
    r.dmlow[...] = dm.astype(BF16)

    def add_tiles(t, v, gap=1):
        for a in range(2):
            at = r.place[24 * l + t + gap * a]
            r.acc[at] = r.acc[at] + v[128 * a : 128 * a + 128]

    for i in range(4):
        add_tiles(16 + 2 * i, nt(r.g[pl.ds(i * D, D), :], r.dylow[...]))
    for i in range(4):
        add_tiles(8 + i, nt(r.n2[...], r.du[pl.ds(i * D, D), :]), 4)
    add_tiles(6, nt(r.ctx[sl], r.dmlow[...]))
    dctx = nn(r.w_o[l], r.dmlow[...])
    for h in range(HEADS):
        hs = slice(h * hd, h * hd + hd)
        r.dctx[hs, :] = (dctx[hs, :] * (r.linv[sl, pl.ds(h, 1), :] * c)).astype(BF16)
    c2 = hd**-0.5 * math.log2(math.e)
    nb = T // 256
    row = lax.broadcasted_iota(jnp.int32, (16, T), 0)
    ones3 = jnp.where(row < 3, 1.0, 0.0).astype(BF16)
    dks = [[None] * nb for _ in range(HEADS)]
    dvs = [[None] * nb for _ in range(HEADS)]
    jobs = [(h, b) for h in range(HEADS) for b in range(nb)]

    def back_probs(h, b):
        kk = 256 * (b + 1)
        qs = pl.ds(256 * b, 256)
        dctx = r.dctx[pl.ds(h * hd, hd), qs]
        ctx = r.ctx[sl, pl.ds(h * hd, hd), qs].astype(F32)
        nd = -jnp.sum(dctx.astype(F32) * ctx, axis=0, keepdims=True)
        n0 = nd.astype(BF16).astype(F32)
        n1 = (nd - n0).astype(BF16).astype(F32)
        n2 = nd - n0 - n1
        rw = row[:, :256]
        extra = jnp.where(rw == 0, n0, jnp.where(rw == 1, n1, jnp.where(rw == 2, n2, 0.0))).astype(BF16)
        de = jnp.concatenate([dctx, extra], axis=0)
        ve = jnp.concatenate([r.qkv[sl, pl.ds(2 * D + h * hd, hd), pl.ds(0, kk)], ones3[:, :kk]], axis=0)
        return tn(ve, de)

    def back_scores(h, b, dsr):
        e = r.es[sl, h, pl.ds(128 * b * (b + 1), 256 * (b + 1)), :]
        return (e.astype(F32) * dsr).astype(BF16)

    def back_heads(h, b, ds):
        kk = 256 * (b + 1)
        qs = pl.ds(256 * b, 256)
        e = r.es[sl, h, pl.ds(128 * b * (b + 1), kk), :]
        k = r.qkv[sl, pl.ds(D + h * hd, hd), pl.ds(0, kk)]
        r.dqkv[pl.ds(h * hd, hd), qs] = nn(k, ds).astype(BF16)
        dkb = nt(r.qkv[sl, pl.ds(h * hd, hd), qs], ds)
        dvb = nt(r.dctx[pl.ds(h * hd, hd), qs], e)
        for j in range(b + 1):
            js = slice(256 * j, 256 * j + 256)
            dks[h][j] = dkb[:, js] if dks[h][j] is None else dks[h][j] + dkb[:, js]
            dvs[h][j] = dvb[:, js] if dvs[h][j] is None else dvs[h][j] + dvb[:, js]
        if b == nb - 1:
            for j in range(nb):
                r.dqkv[pl.ds(D + h * hd, hd), pl.ds(256 * j, 256)] = (dks[h][j] * (1.0 / c2)).astype(BF16)
                r.dqkv[pl.ds(2 * D + h * hd, hd), pl.ds(256 * j, 256)] = (dvs[h][j] * (1.0 / c)).astype(BF16)

    staged(jobs, back_probs, back_scores, back_heads)
    xhat, rstd1 = normed(r.xs[sl])
    r.hat[...] = xhat
    r.n1[...] = (xhat * wide(pr(0), T) + wide(pr(1), T)).astype(BF16)
    for i in range(3):
        add_tiles(2 * i, nt(r.n1[...], r.dqkv[pl.ds(i * D, D), :]))
    dn1 = nn(r.w_qkv[l], r.dqkv[...])
    add_small(0, dn1 * r.hat[...])
    add_small(1, dn1)
    r.dcur[...] = r.dcur[...] + norm_back(dn1, r.hat[...], rstd1, wide(pr(0), T))


def kernel(S, N, nprompts, npieces, counts, place, dst, rows, far, emb, cot, emb_far, cot_far, pbr, *refs):
    pieces = refs[:npieces]
    fe, keep, send, sgo = refs[npieces : npieces + 4]
    scr = refs[npieces + 4 :]
    r = R()
    (r.pb, r.wt_qkv, r.wt_o, r.wt_up, r.wt_down, r.w_qkv, r.w_o, r.w_up, r.w_down, r.mask,
     r.cur, r.dcur, r.embT, r.gsum, r.io, r.n1, r.n2, r.hat, r.g, r.du, r.dylow, r.dmlow, r.dctx, r.dqkv,
     r.xs, r.qkv, r.es, r.linv, r.ctx, r.sg, r.low, r.acc, r.sem, r.sem2) = scr[:34]
    redo = N > S
    if redo:
        r.hs = scr[34]
    r.place = place
    T, D = r.io.shape
    C = T // N

    def load(p, near_ref, far_ref, sem):
        @pl.when(far[p] == 0)
        def _():
            pltpu.make_async_copy(near_ref.at[rows[p]], r.io, sem).start()

        @pl.when(far[p] != 0)
        def _():
            pltpu.make_async_copy(far_ref, r.io, sem).start()

        pltpu.make_async_copy(far_ref, r.io, sem).wait()

    def spot(t):
        per = r.es.shape[2] // 128
        return r.es.at[0, t // per, pl.ds(pl.multiple_of(t % per * 128, 128), 128), :]

    cps = []
    for piece in pieces:
        for i in range(piece.shape[0]):
            cps.append(pltpu.make_async_copy(piece.at[i], spot(dst[len(cps)]), r.sem))
    for cp in cps:
        cp.start()
    r.acc[...] = jnp.zeros_like(r.acc)
    r.sg[...] = jnp.zeros_like(r.sg)
    for k in range(18):
        r.pb[k // 9, k % 9 * D : k % 9 * D + D, :] = jnp.broadcast_to(pbr[k : k + 1, :], (128, D)).T
    for cp in cps:
        cp.wait()
    for l in range(2):
        for t in range(24):
            per = r.es.shape[2] // 128
            u = 24 * l + t
            w = r.es[0, u // per, u % per * 128 : u % per * 128 + 128, :]
            if t < 6:
                r.w_qkv[l, t % 2 * 128 : t % 2 * 128 + 128, t // 2 * D : t // 2 * D + D] = w
            elif t < 8:
                r.w_o[l, (t - 6) * 128 : (t - 5) * 128, :] = w
            elif t < 16:
                o, b = (t - 8) // 4 * 128, (t - 8) % 4 * D
                r.w_up[l, o : o + 128, b : b + D] = w
            else:
                r.w_down[l, (t - 16) * 128 : (t - 15) * 128, :] = w
        for natural, turned in ((r.w_qkv, r.wt_qkv), (r.w_o, r.wt_o), (r.w_up, r.wt_up), (r.w_down, r.wt_down)):
            turned[l] = natural[l].T
    ki = lax.broadcasted_iota(jnp.int32, (256, 256), 0)
    qi = lax.broadcasted_iota(jnp.int32, (256, 256), 1)
    r.mask[...] = jnp.where(ki <= qi, 0.0, MASKED)

    def prompt(p, _):
        count = counts[p]
        load(p, emb, emb_far, r.sem)
        r.embT[...] = r.io[...].T
        r.cur[...] = jnp.zeros_like(r.cur)

        def forward(j):
            r.cur[...] = r.cur[...] + r.embT[...]

            def fl(l, _):
                layer_fwd(r, l, lax.rem(j, S) * 2 + l, T, D)
                return 0

            lax.fori_loop(0, 2, fl, 0)

        def floop(j, _):
            if redo:
                r.hs[j] = r.cur[...]
            forward(j)
            return 0

        lax.fori_loop(0, count, floop, 0)
        r.low[...] = r.cur[...].T.astype(BF16)
        cps = [pltpu.make_async_copy(r.low.at[pl.ds(C * i, C), :], fe.at[i, 0, p], r.sem) for i in range(N)]
        for cp in cps:
            cp.start()
        for cp in cps:
            cp.wait()
        load(p, cot, cot_far, r.sem)
        r.dcur[...] = r.io[...].T
        r.gsum[...] = jnp.zeros_like(r.gsum)

        def bloop(jj, _):
            j = count - 1 - jj
            if redo:

                @pl.when(jj >= S)
                def _():
                    r.cur[...] = r.hs[j]
                    forward(j)

            def bl(ll, _):
                l = 1 - ll
                layer_bwd(r, l, lax.rem(j, S) * 2 + l, T, D)
                return 0

            lax.fori_loop(0, 2, bl, 0)
            r.gsum[...] = r.gsum[...] + r.dcur[...]
            return 0

        lax.fori_loop(0, count, bloop, 0)
        r.low[...] = r.gsum[...].T.astype(BF16)
        cps = [pltpu.make_async_copy(r.low.at[pl.ds(C * i, C), :], fe.at[i, 1, p], r.sem) for i in range(N)]
        for cp in cps:
            cp.start()
        for cp in cps:
            cp.wait()
        return 0

    lax.fori_loop(0, nprompts, prompt, 0)
    out1 = pltpu.make_async_copy(r.acc.at[pl.ds(0, 24)], keep, r.sem)
    out1.start()
    per = r.es.shape[2] // 128
    for t in range(24):
        r.es[0, t // per, t % per * 128 : t % per * 128 + 128, :] = r.acc[24 + t].astype(BF16)
    outs = []
    for t in range(24):
        outs.append(pltpu.make_async_copy(r.es.at[0, t // per, pl.ds(t % per * 128, 128), :], send.at[t], r.sem2))
        outs[-1].start()
    for k in range(18):
        part = r.sg[k // 9, k % 9 * D : k % 9 * D + D, :].T
        sgo[k : k + 1, :] = jnp.sum(part, axis=0, keepdims=True)
    out1.wait()
    for cp in outs:
        cp.wait()


def call(N, counts, place, dst, rows, far, emb, cot, emb_far, cot_far, pbr, pieces):
    S = N if N <= 4 else 2
    n = counts.shape[0]
    _, T, D = emb.shape
    V = pltpu.VMEM
    H = 4 * D
    scr = [
        V((2, 9 * D, 128), F32), V((2, 3 * D, D), BF16), V((2, D, D), BF16), V((2, H, D), BF16), V((2, D, H), BF16),
        V((2, D, 3 * D), BF16), V((2, D, D), BF16), V((2, D, H), BF16), V((2, H, D), BF16),
        V((256, 256), F32),
        V((D, T), F32), V((D, T), F32), V((D, T), F32), V((D, T), F32), V((T, D), F32),
        V((D, T), BF16), V((D, T), BF16), V((D, T), F32), V((H, T), BF16), V((H, T), BF16),
        V((D, T), BF16), V((D, T), BF16), V((D, T), BF16), V((3 * D, T), BF16),
        V((2 * S, D, T), F32), V((2 * S, 3 * D, T), BF16),
        V((2 * S, HEADS, T * (T // 256 + 1) // 2, 256), BF16), V((2 * S, HEADS, T), F32), V((2 * S, D, T), BF16),
        V((2, 9 * D, 128), F32), V((T, D), BF16), V((48, 128, D), F32),
        pltpu.SemaphoreType.DMA, pltpu.SemaphoreType.DMA,
    ]
    if N > S:
        scr.append(V((N, D, T), F32))
    A = pl.BlockSpec(memory_space=pl.ANY)
    VM = pl.BlockSpec(memory_space=pltpu.VMEM)
    SM = pl.BlockSpec(memory_space=pltpu.SMEM)
    return pl.pallas_call(
        functools.partial(kernel, S, N, n, len(pieces)),
        out_shape=(
            jax.ShapeDtypeStruct((N, 2, n, T // N, D), BF16),
            jax.ShapeDtypeStruct((24, 128, D), F32), jax.ShapeDtypeStruct((24, 128, D), BF16),
            jax.ShapeDtypeStruct((18, D), F32)),
        in_specs=[SM] * 5 + [A] * 4 + [VM] + [A] * len(pieces),
        out_specs=(A, A, A, VM),
        scratch_shapes=scr,
        compiler_params=pltpu.CompilerParams(vmem_limit_bytes=63 * 1024 * 1024),
    )(counts, place, dst, rows, far, emb, cot, emb_far, cot_far, pbr, *pieces)


STEP = 10
beta_one = 0.9
beta_two = 0.999
learn_rate = 0.05
small_rate = 0.3
weight_decay = 0.1
adam_eps = 1e-08


def adam_update(gradient, first_old, second_old, weight, decay_rate, rate):
    first_new = beta_one * first_old + (1.0 - beta_one) * gradient
    second_new = beta_two * second_old + (1.0 - beta_two) * gradient * gradient
    corr_one = 1.0 - beta_one**STEP
    corr_two = 1.0 - beta_two**STEP
    update = first_new / corr_one / (jnp.sqrt(second_new / corr_two) + adam_eps)
    return (first_new, second_new, weight - rate * (update + decay_rate * weight))


def ranks(key, falling):
    n = key.shape[0]
    i = jnp.arange(n)
    ahead = (key[None, :] > key[:, None]) if falling else (key[None, :] < key[:, None])
    tie = (key[None, :] == key[:, None]) & (i[None, :] < i[:, None])
    return jnp.sum((ahead | tie).astype(jnp.int32), axis=1)


def swap(v, axis, k):
    n = lax.axis_size(axis)
    return lax.ppermute(v, axis, [(i, i ^ k) for i in range(n)])


def pick(v, i, axis):
    return lax.dynamic_index_in_dim(v, i, axis, keepdims=False)


def gather_tiles(low, N, Z, s, z, c):
    OWN, H, D = low.shape
    E = OWN - N
    line = lambda v: jnp.stack([v] + [swap(v, "dp", 2 * k) for k in range(1, Z)])
    zs = line(pick(low[E:], s, 0))
    near = [zs] + [swap(zs, "section", k) for k in range(1, N)]
    pieces = near + [swap(v, "dp", 1) for v in near]
    zr = jnp.arange(Z) ^ z
    at = [((zr * 2 + cc) * OWN + E + (s ^ k)) for cc in (c, 1 - c) for k in range(N)]
    if E:
        rest = line(low[:E]).reshape(Z * E, H, D)
        pieces += [rest, swap(rest, "dp", 1)]
        at += [((zr[:, None] * 2 + cc) * OWN + jnp.arange(E)[None, :]).reshape(-1) for cc in (c, 1 - c)]
    return pieces, jnp.concatenate(at)


def reduce_mixed(part, N, Z, s, z):
    _, OWN, H, D = part.shape
    E = OWN - N
    add = lambda v, got: functools.reduce(lambda x, y: x + y.astype(F32), got, v)
    split, rest = part[:, E:], part[:, :E]
    got_q = [swap(pick(split, s ^ k, 1).astype(BF16), "section", k) for k in range(1, N)]
    got_d = [swap(pick(rest, z ^ k, 0).astype(BF16), "dp", 2 * k) for k in range(1, Z)]
    q = add(pick(split, s, 1), got_q)
    d = add(pick(rest, z, 0), got_d).reshape(N, E * H // N, D)
    got_q = [swap(pick(q, z ^ k, 0).astype(BF16), "dp", 2 * k) for k in range(1, Z)]
    got_d = [swap(pick(d, s ^ k, 0).astype(BF16), "section", k) for k in range(1, N)]
    q = add(pick(q, z, 0), got_q)
    d = add(pick(d, s, 0), got_d)
    done = jnp.concatenate([d, q], axis=0).astype(BF16)
    every = jnp.stack([done] + [swap(done, "section", k) for k in range(1, N)])
    every = [pick(every, s ^ j, 0) for j in range(N)]
    F = E * H // N
    return jnp.concatenate([v[:F] for v in every] + [v[F:] for v in every], axis=0).astype(F32)


def reduce_even(part, N, Z, s, z):
    _, OWN, H, D = part.shape
    part = part.reshape(Z, N, OWN * H // N, D)
    got = [swap(pick(part, s ^ k, 1).astype(BF16), "section", k) for k in range(1, N)]
    part = pick(part, s, 1)
    for v in got:
        part = part + v.astype(F32)
    got = [swap(pick(part, z ^ k, 0).astype(BF16), "dp", 2 * k) for k in range(1, Z)]
    part = pick(part, z, 0)
    for v in got:
        part = part + v.astype(F32)
    part = part.astype(BF16)
    every = jnp.stack([part] + [swap(part, "section", k) for k in range(1, N)])
    return jnp.concatenate([pick(every, s ^ j, 0) for j in range(N)], axis=0).astype(F32)


def reduce_small(v, N, DP):
    for axis, n in (("dp", DP), ("section", N)):
        k = 1
        while k < n:
            v = v + swap(v, axis, k)
            k *= 2
    return v


def order_kernel(N, slots, at, *refs):
    ins, fin, eg = refs[:N], refs[N], refs[N + 1]

    def put(p, _):
        w = at[p]
        for k in range(N):
            for j in range(slots):

                @pl.when(w == k * slots + j)
                def _():
                    fin[p] = ins[k][0, j].astype(F32)
                    eg[p] = ins[k][1, j].astype(F32)

        return 0

    lax.fori_loop(0, fin.shape[0], put, 0)


def in_order(pieces, at, prompts):
    _, slots, C, D = pieces[0].shape
    N = len(pieces)
    VM = pl.BlockSpec(memory_space=pltpu.VMEM)
    out = jax.ShapeDtypeStruct((prompts, C, D), F32)
    return pl.pallas_call(
        functools.partial(order_kernel, N, slots),
        out_shape=(out, out),
        in_specs=[pl.BlockSpec(memory_space=pltpu.SMEM)] + [VM] * N,
        out_specs=(VM, VM),
        compiler_params=pltpu.CompilerParams(vmem_limit_bytes=32 * 1024 * 1024),
    )(at, *pieces)


def choose(table, i):
    n = table.shape[0]
    return jnp.sum(jnp.where(i[:, None] == jnp.arange(n)[None, :], table[None, :], 0), axis=1)


def share_prompts(counts, N, s, c):
    PR = counts.shape[0]
    jobs = R()
    jobs.shared = PR == 2 * N and N <= 4
    rank = ranks(counts, True)
    slots = -(-PR // N)
    j = jnp.arange(slots)
    if not jobs.shared:
        want = j * N + jnp.where(j % 2 == 0, s, N - 1 - s)
        hit = want[:, None] == rank[None, :]
        jobs.rows = jnp.sum(jnp.where(hit, jnp.arange(PR)[None, :], 0), axis=1).astype(jnp.int32)
        jobs.counts = jnp.sum(jnp.where(hit, counts[None, :], 0), axis=1).astype(jnp.int32)
        jobs.far = jnp.zeros((slots,), jnp.int32)
        k = rank // N
        w = jnp.where(k % 2 == 0, rank % N, N - 1 - rank % N)
        jobs.at = (w ^ s) * slots + k
        return jobs
    def falling(v, r):
        return jnp.sum(jnp.where(r[None, :] == jnp.arange(PR)[:, None], v[None, :], 0), axis=1)
    theirs = swap(counts, "dp", 1)
    mine_sorted = falling(counts, rank)
    theirs_sorted = falling(theirs, ranks(theirs, True))
    first = jnp.where(c == 0, mine_sorted, theirs_sorted)
    second = jnp.where(c == 0, theirs_sorted, mine_sorted)
    hi_a, lo_a = first[:N, None], first[N:][::-1][:, None]
    hi_b, lo_b = second[None, :N], second[N:][::-1][None, :]
    kept = jnp.maximum(hi_a + lo_a, hi_b + lo_b)
    traded = jnp.maximum(hi_a + lo_b, hi_b + lo_a)
    cost = jnp.minimum(kept, traded).reshape(-1)
    perms = np.array(list(itertools.permutations(range(N))), np.int32)
    picks = perms + N * np.arange(N)[None, :]
    onehot = picks[:, :, None] == np.arange(N * N)[None, None, :]
    worst = jnp.max(jnp.sum(jnp.where(onehot, cost[None, None, :], 0), axis=2), axis=1)
    code = jnp.min(worst * perms.shape[0] + jnp.arange(perms.shape[0]))
    best = jnp.arange(perms.shape[0]) == code % perms.shape[0]
    perm = jnp.sum(jnp.where(best[:, None], perms, 0), axis=0)
    back = jnp.sum(jnp.where(perm[None, :] == jnp.arange(N)[:, None], jnp.arange(N)[None, :], 0), axis=1)
    pair = jnp.where(c == 0, s, choose(perm, s[None])[0])
    cell = s * N + choose(perm, s[None])[0]
    trade = choose((traded < kept).reshape(-1).astype(jnp.int32), cell[None])[0]
    other_pair = jnp.where(c == 0, choose(perm, s[None])[0], s)
    want = jnp.stack([pair, PR - 1 - pair])
    hit = want[:, None] == rank[None, :]
    jobs.rows = jnp.sum(jnp.where(hit, jnp.arange(PR)[None, :], 0), axis=1).astype(jnp.int32)
    own = jnp.sum(jnp.where(hit, counts[None, :], 0), axis=1).astype(jnp.int32)
    lent = choose(theirs_sorted, (PR - 1 - other_pair)[None])[0]
    jobs.far = jnp.stack([jnp.zeros((), jnp.int32), trade])
    jobs.counts = jnp.stack([own[0], jnp.where(trade != 0, lent, own[1])]).astype(jnp.int32)
    low = rank >= N
    mypair = jnp.where(low, PR - 1 - rank, rank)
    w = jnp.where(c == 0, mypair, choose(back, mypair))
    jobs.at = (w ^ s) * slots + low.astype(jnp.int32)
    return jobs


def shards(embedding, cotangent, counts, owner_list, tiles_owned, first_owned, second_owned,
           small_params, small_first, small_second):
    N, DP = lax.axis_size("section"), lax.axis_size("dp")
    Z = DP // 2
    s, dp = lax.axis_index("section"), lax.axis_index("dp")
    z, c = dp // 2, dp % 2
    PR, T, D = embedding.shape
    OWN, H, _ = tiles_owned.shape
    TILES = OWN * DP
    rank = ranks(owner_list, False)
    owner, slot = rank // OWN, rank % OWN
    place = ((owner % 2) ^ c) * (Z * OWN) + owner // 2 * OWN + slot
    low = tiles_owned.astype(BF16)
    if OWN >= N and (OWN - N) * H % N == 0:
        pieces, at = gather_tiles(low, N, Z, s, z, c)
        reduce_tiles = reduce_mixed
    else:
        pieces, at = [lax.all_gather(low, "dp", axis=0, tiled=True)], jnp.arange(TILES)
        reduce_tiles = reduce_even
    dst = jnp.sum(jnp.where(at[:, None] == rank[None, :], jnp.arange(TILES)[None, :], 0), axis=1)
    jobs = share_prompts(counts, N, s, c)
    row = jobs.rows[-1]
    emb_far, cot_far = (swap(pick(v, row, 0), "dp", 1) if jobs.shared else v[0] for v in (embedding, cotangent))
    fe, keep, send, sg = call(N, jobs.counts, place, dst, jobs.rows, jobs.far, embedding, cotangent, emb_far, cot_far,
                              small_params, pieces)
    if jobs.shared:
        other = swap(fe[:, :, 1], "dp", 1)
        fe = jnp.stack([fe[:, :, 0], jnp.where(jobs.far[1] != 0, other, fe[:, :, 1])], axis=2)
    done = [pick(fe, s, 0)] + [swap(pick(fe, s ^ k, 0), "section", k) for k in range(1, N)]
    part = (keep + swap(send, "dp", 1).astype(F32)).reshape(Z, OWN, H, D)
    tile_grad = reduce_tiles(part, N, Z, s, z).reshape(OWN, H, D)
    small_grad = reduce_small(sg, N, DP)
    fin, eg = in_order(done, jobs.at, PR)
    tile_first, tile_second, tile_new = adam_update(
        tile_grad, first_owned, second_owned, tiles_owned, weight_decay, learn_rate
    )
    small_first_new, small_second_new, small_new = adam_update(
        small_grad, small_first, small_second, small_params, 0.0, small_rate
    )
    return (fin, eg, tile_grad, tile_first, tile_second, tile_new,
            small_grad, small_first_new, small_second_new, small_new)


def solution(mesh):
    P = jax.sharding.PartitionSpec
    own, rep = P("dp", None, None), P()
    return jax.shard_map(
        shards,
        mesh=mesh,
        in_specs=(own, own, P("dp"), rep, own, own, own, rep, rep, rep),
        out_specs=(P("dp", "section", None),) * 2 + (own,) * 4 + (rep,) * 4,
        check_vma=False,
    )
```

```python
import functools
import itertools
import math

import jax
import jax.numpy as jnp
from jax import lax
from jax.experimental import pallas as pl
from jax.experimental.pallas import tpu as pltpu

F32, BF16 = jnp.float32, jnp.bfloat16
HEADS = 8
EPS = 1e-5
MASKED = -1e30
GC0 = math.sqrt(2.0 / math.pi)
GC1 = 0.044715


def nn(a, b):
    return lax.dot_general(a, b, (((1,), (0,)), ((), ())), preferred_element_type=F32)


def nt(a, b):
    return lax.dot_general(a, b, (((1,), (1,)), ((), ())), preferred_element_type=F32)


def tn(a, b):
    return lax.dot_general(a, b, (((0,), (0,)), ((), ())), preferred_element_type=F32)


def wide(col, n):
    return jnp.concatenate([col] * (n // 128), axis=1)


def fold(a):
    r = a[:, 0:128]
    for i in range(1, a.shape[1] // 128):
        r = r + a[:, 128 * i : 128 * i + 128]
    return r


def normed(x):
    d = x.shape[0]
    mean = jnp.sum(x, axis=0, keepdims=True) * (1.0 / d)
    xc = x - mean
    var = jnp.sum(xc * xc, axis=0, keepdims=True) * (1.0 / d)
    rstd = lax.rsqrt(var + EPS)
    return xc * rstd, rstd


def norm_back(dn, xhat, rstd, gain):
    d = dn.shape[0]
    dx = dn * gain
    a = jnp.sum(dx, axis=0, keepdims=True) * (1.0 / d)
    b = jnp.sum(dx * xhat, axis=0, keepdims=True) * (1.0 / d)
    return rstd * (dx - a - xhat * b)


def staged(jobs, first, second, third, ahead=2, behind=2):
    n = len(jobs)
    a, b = {}, {}
    for i in range(-ahead, n + behind):
        if 0 <= i + ahead < n:
            a[i + ahead] = first(*jobs[i + ahead])
        if 0 <= i < n:
            b[i] = second(*jobs[i], a.pop(i))
        if 0 <= i - behind < n:
            third(*jobs[i - behind], b.pop(i - behind))


class R:
    pass


def layer_fwd(r, l, sl, T, D):
    hd = D // HEADS
    pr = lambda k, n=1: r.pb[l, pl.ds(k * D, n * D), :]
    x = r.cur[...]
    r.xs[sl] = x
    xhat, _ = normed(x)
    r.n1[...] = (xhat * wide(pr(0), T) + wide(pr(1), T)).astype(BF16)
    c2 = hd**-0.5 * math.log2(math.e)
    for i in range(3):
        v = nn(r.wt_qkv[l, pl.ds(i * D, D), :], r.n1[...])
        r.qkv[sl, pl.ds(i * D, D), :] = (v * c2 if i == 0 else v).astype(BF16)
    ones16 = jnp.ones((16, T), BF16)
    jobs = [(h, b) for h in range(HEADS) for b in range(T // 256)]

    def scores(h, b):
        kk = 256 * (b + 1)
        k = r.qkv[sl, pl.ds(D + h * hd, hd), pl.ds(0, kk)]
        return tn(k, r.qkv[sl, pl.ds(h * hd, hd), pl.ds(256 * b, 256)])

    def probs(h, b, s):
        kk = 256 * (b + 1)
        tail = s[kk - 256 :, :] + r.mask[...]
        mx = jnp.max(tail, axis=0, keepdims=True)
        if b == 0:
            e = jnp.exp2(tail - mx).astype(BF16)
        else:
            lead = s[: kk - 256, :]
            mx = jnp.maximum(mx, jnp.max(lead, axis=0, keepdims=True))
            e = jnp.concatenate([jnp.exp2(lead - mx).astype(BF16), jnp.exp2(tail - mx).astype(BF16)], axis=0)
        r.es[sl, h, pl.ds(128 * b * (b + 1), kk), :] = e
        return e

    def context(h, b, e):
        kk = 256 * (b + 1)
        v = r.qkv[sl, pl.ds(2 * D + h * hd, hd), pl.ds(0, kk)]
        o = nn(jnp.concatenate([v, ones16[:, :kk]], axis=0), e)
        linv = 1.0 / o[hd : hd + 1, :]
        r.linv[sl, pl.ds(h, 1), pl.ds(256 * b, 256)] = linv
        r.ctx[sl, pl.ds(h * hd, hd), pl.ds(256 * b, 256)] = (o[:hd, :] * linv).astype(BF16)

    staged(jobs, scores, probs, context)
    m = r.xs[sl] + nn(r.wt_o[l], r.ctx[sl])
    r.cur[...] = m
    mhat, _ = normed(m)
    r.n2[:D, :] = (mhat * wide(pr(2), T) + wide(pr(3), T)).astype(BF16)
    r.cur[...] = r.cur[...] + wide(pr(8), T)

    def up(i):
        return nn(r.wt_up[l, pl.ds(i * D, D), :], r.n2[:D, :]) + wide(pr(4 + i), T)

    def act(i, h):
        t1 = 1.0 + jnp.tanh(h * (2 * GC0 + (8 * GC0 * GC1) * (h * h)))
        return (h * t1).astype(BF16)

    def down(i, g):
        r.cur[...] = r.cur[...] + nn(r.wt_down[l, :, pl.ds(i * D, D)], g)

    staged([(i,) for i in range(4)], up, act, down, 1, 1)


def layer_bwd(r, l, sl, T, D):
    hd = D // HEADS
    c = hd**-0.5
    pr = lambda k, n=1: r.pb[l, pl.ds(k * D, n * D), :]

    def add_small(k, v):
        r.sg[l, pl.ds(k * D, D), :] = r.sg[l, pl.ds(k * D, D), :] + fold(v)

    dy = r.dcur[...]
    r.dylow[...] = dy.astype(BF16)
    add_small(8, dy)
    mhat, rstd2 = normed(r.xs[sl] + nn(r.wt_o[l], r.ctx[sl]))
    r.hat[...] = mhat
    r.n2[:D, :] = (mhat * wide(pr(2), T) + wide(pr(3), T)).astype(BF16)

    def add_tiles(t, v, gap=1):
        for a in range(2):
            at = r.place[24 * l + t + gap * a]
            r.acc[at] = r.acc[at] + v[128 * a : 128 * a + 128]

    def up(i):
        h = nn(r.wt_up[l, pl.ds(i * D, D), :], r.n2[:D, :]) + wide(pr(4 + i), T)
        return h, nn(r.w_down[l, pl.ds(i * D, D), :], r.dylow[...])

    def act(i, both):
        h, dg = both
        h2 = h * h
        t1 = 1.0 + jnp.tanh(h * (2 * GC0 + (8 * GC0 * GC1) * h2))
        g = h * t1
        du = dg * (t1 + g * (2.0 - t1) * (2 * GC0 + (24 * GC0 * GC1) * h2))
        g, du = g.astype(BF16), du.astype(BF16)
        r.du[pl.ds(i * D, D), :] = du
        return g, du

    def grads(i, both):
        g, du = both
        add_tiles(16 + 2 * i, nt(g, r.dylow[...]))
        v = nt(r.n2[...], du)
        add_tiles(8 + i, v, 4)
        r.sgb[l, i : i + 1, :] = r.sgb[l, i : i + 1, :] + v[D : D + 1]

    staged([(i,) for i in range(4)], up, act, grads, 1, 1)
    dn2 = nn(r.w_up[l], r.du[...])
    add_small(2, dn2 * r.hat[...])
    add_small(3, dn2)
    dm = r.dcur[...] + norm_back(dn2, r.hat[...], rstd2, wide(pr(2), T))
    r.dcur[...] = dm
    r.dmlow[...] = dm.astype(BF16)

    add_tiles(6, nt(r.ctx[sl], r.dmlow[...]))
    dctx = nn(r.w_o[l], r.dmlow[...])
    for h in range(HEADS):
        hs = slice(h * hd, h * hd + hd)
        r.dctx[hs, :] = (dctx[hs, :] * (r.linv[sl, pl.ds(h, 1), :] * c)).astype(BF16)
    c2 = hd**-0.5 * math.log2(math.e)
    nb = T // 256
    row = lax.broadcasted_iota(jnp.int32, (16, T), 0)
    ones3 = jnp.where(row < 3, 1.0, 0.0).astype(BF16)
    dks = [[None] * nb for _ in range(HEADS)]
    dvs = [[None] * nb for _ in range(HEADS)]
    jobs = [(h, b) for h in range(HEADS) for b in range(nb)]

    def back_probs(h, b):
        kk = 256 * (b + 1)
        qs = pl.ds(256 * b, 256)
        dctx = r.dctx[pl.ds(h * hd, hd), qs]
        ctx = r.ctx[sl, pl.ds(h * hd, hd), qs].astype(F32)
        nd = -jnp.sum(dctx.astype(F32) * ctx, axis=0, keepdims=True)
        n0 = nd.astype(BF16).astype(F32)
        n1 = (nd - n0).astype(BF16).astype(F32)
        n2 = nd - n0 - n1
        rw = row[:, :256]
        extra = jnp.where(rw == 0, n0, jnp.where(rw == 1, n1, jnp.where(rw == 2, n2, 0.0))).astype(BF16)
        de = jnp.concatenate([dctx, extra], axis=0)
        ve = jnp.concatenate([r.qkv[sl, pl.ds(2 * D + h * hd, hd), pl.ds(0, kk)], ones3[:, :kk]], axis=0)
        return tn(ve, de)

    def back_scores(h, b, dsr):
        e = r.es[sl, h, pl.ds(128 * b * (b + 1), 256 * (b + 1)), :]
        return (e.astype(F32) * dsr).astype(BF16)

    def back_heads(h, b, ds):
        kk = 256 * (b + 1)
        qs = pl.ds(256 * b, 256)
        e = r.es[sl, h, pl.ds(128 * b * (b + 1), kk), :]
        k = r.qkv[sl, pl.ds(D + h * hd, hd), pl.ds(0, kk)]
        r.dqkv[pl.ds(h * hd, hd), qs] = nn(k, ds).astype(BF16)
        dkb = nt(r.qkv[sl, pl.ds(h * hd, hd), qs], ds)
        dvb = nt(r.dctx[pl.ds(h * hd, hd), qs], e)
        for j in range(b + 1):
            js = slice(256 * j, 256 * j + 256)
            dks[h][j] = dkb[:, js] if dks[h][j] is None else dks[h][j] + dkb[:, js]
            dvs[h][j] = dvb[:, js] if dvs[h][j] is None else dvs[h][j] + dvb[:, js]
        if b == nb - 1:
            for j in range(nb):
                r.dqkv[pl.ds(D + h * hd, hd), pl.ds(256 * j, 256)] = (dks[h][j] * (1.0 / c2)).astype(BF16)
                r.dqkv[pl.ds(2 * D + h * hd, hd), pl.ds(256 * j, 256)] = (dvs[h][j] * (1.0 / c)).astype(BF16)

    staged(jobs, back_probs, back_scores, back_heads)
    xhat, rstd1 = normed(r.xs[sl])
    r.hat[...] = xhat
    r.n1[...] = (xhat * wide(pr(0), T) + wide(pr(1), T)).astype(BF16)
    for i in range(3):
        add_tiles(2 * i, nt(r.n1[...], r.dqkv[pl.ds(i * D, D), :]))
    dn1 = nn(r.w_qkv[l], r.dqkv[...])
    add_small(0, dn1 * r.hat[...])
    add_small(1, dn1)
    r.dcur[...] = r.dcur[...] + norm_back(dn1, r.hat[...], rstd1, wide(pr(0), T))


def kernel(S, N, nprompts, npieces, counts, place, dst, rows, far, emb, cot, emb_far, cot_far, pbr, *refs):
    pieces = refs[:npieces]
    fe, keep, send, sgo = refs[npieces : npieces + 4]
    scr = refs[npieces + 4 :]
    r = R()
    (r.pb, r.wt_qkv, r.wt_o, r.wt_up, r.wt_down, r.w_qkv, r.w_o, r.w_up, r.w_down, r.mask,
     r.cur, r.dcur, r.embT, r.gsum, r.io, r.n1, r.n2, r.hat, r.du, r.dylow, r.dmlow, r.dctx, r.dqkv,
     r.xs, r.qkv, r.es, r.linv, r.ctx, r.sg, r.low, r.acc, r.io2, r.low2, r.sgb,
     r.sem, r.sem2, r.sem_e, r.sem_c) = scr[:38]
    redo = N > S
    if redo:
        r.hs = scr[38]
    r.place = place
    T, D = r.io.shape
    C = T // N

    def load(p, near_ref, far_ref, to, sem):
        @pl.when(far[p] == 0)
        def _():
            pltpu.make_async_copy(near_ref.at[rows[p]], to, sem).start()

        @pl.when(far[p] != 0)
        def _():
            pltpu.make_async_copy(far_ref, to, sem).start()

    load(0, emb, emb_far, r.io, r.sem_e)
    load(0, cot, cot_far, r.io2, r.sem_c)

    def give(p, which, v, low, sem):
        cps = [pltpu.make_async_copy(low.at[pl.ds(C * i, C), :], fe.at[i, which, p], sem) for i in range(N)]

        @pl.when(p > 0)
        def _():
            for cp in cps:
                cp.wait()

        low[...] = v.T.astype(BF16)
        for cp in cps:
            cp.start()

    def spot(t):
        per = r.es.shape[2] // 64
        return r.es.at[0, t // per, pl.ds(pl.multiple_of(t % per * 64, 64), 64), :]

    cps = []
    for piece in pieces:
        for i in range(piece.shape[0]):
            cps.append(pltpu.make_async_copy(piece.at[i], spot(dst[len(cps)]), r.sem))
    for cp in cps:
        cp.start()
    r.acc[...] = jnp.zeros_like(r.acc)
    r.sg[...] = jnp.zeros_like(r.sg)
    r.sgb[...] = jnp.zeros_like(r.sgb)
    r.n2[D:, :] = jnp.where(lax.broadcasted_iota(jnp.int32, (16, T), 0) == 0, 1.0, 0.0).astype(BF16)
    for k in range(18):
        half = 0.5 if 4 <= k % 9 < 8 else 1.0
        r.pb[k // 9, k % 9 * D : k % 9 * D + D, :] = jnp.broadcast_to(pbr[k : k + 1, :] * half, (128, D)).T
    for cp in cps:
        cp.wait()
    for l in range(2):
        for t in range(24):
            per = r.es.shape[2] // 128
            u = 24 * l + t
            w = r.es[0, u // per, u % per * 128 : u % per * 128 + 128, :]
            if t < 6:
                r.w_qkv[l, t % 2 * 128 : t % 2 * 128 + 128, t // 2 * D : t // 2 * D + D] = w
            elif t < 8:
                r.w_o[l, (t - 6) * 128 : (t - 5) * 128, :] = w
            elif t < 16:
                o, b = (t - 8) // 4 * 128, (t - 8) % 4 * D
                r.w_up[l, o : o + 128, b : b + D] = w
            else:
                r.w_down[l, (t - 16) * 128 : (t - 15) * 128, :] = w
        for natural, turned in ((r.w_qkv, r.wt_qkv), (r.w_o, r.wt_o), (r.w_up, r.wt_up), (r.w_down, r.wt_down)):
            turned[l] = natural[l].T
        r.wt_up[l] = r.wt_up[l] * 0.5
        r.w_down[l] = r.w_down[l] * 0.5
    ki = lax.broadcasted_iota(jnp.int32, (256, 256), 0)
    qi = lax.broadcasted_iota(jnp.int32, (256, 256), 1)
    r.mask[...] = jnp.where(ki <= qi, 0.0, MASKED)

    def prompt(p, _):
        count = counts[p]
        pltpu.make_async_copy(emb_far, r.io, r.sem_e).wait()
        r.embT[...] = r.io[...].T

        @pl.when(p + 1 < nprompts)
        def _():
            load(p + 1, emb, emb_far, r.io, r.sem_e)

        r.cur[...] = jnp.zeros_like(r.cur)

        def forward(j):
            r.cur[...] = r.cur[...] + r.embT[...]

            def fl(l, _):
                layer_fwd(r, l, lax.rem(j, S) * 2 + l, T, D)
                return 0

            lax.fori_loop(0, 2, fl, 0)

        def floop(j, _):
            if redo:
                r.hs[j] = r.cur[...]
            forward(j)
            return 0

        lax.fori_loop(0, count, floop, 0)
        give(p, 0, r.cur[...], r.low, r.sem)
        pltpu.make_async_copy(cot_far, r.io2, r.sem_c).wait()
        r.dcur[...] = r.io2[...].T

        @pl.when(p + 1 < nprompts)
        def _():
            load(p + 1, cot, cot_far, r.io2, r.sem_c)

        r.gsum[...] = jnp.zeros_like(r.gsum)

        def bloop(jj, _):
            j = count - 1 - jj
            if redo:

                @pl.when(jj >= S)
                def _():
                    r.cur[...] = r.hs[j]
                    forward(j)

            def bl(ll, _):
                l = 1 - ll
                layer_bwd(r, l, lax.rem(j, S) * 2 + l, T, D)
                return 0

            lax.fori_loop(0, 2, bl, 0)
            r.gsum[...] = r.gsum[...] + r.dcur[...]
            return 0

        lax.fori_loop(0, count, bloop, 0)
        give(p, 1, r.gsum[...], r.low2, r.sem2)
        return 0

    lax.fori_loop(0, nprompts, prompt, 0)
    for which, low, sem in ((0, r.low, r.sem), (1, r.low2, r.sem2)):
        for i in range(N):
            pltpu.make_async_copy(low.at[pl.ds(C * i, C), :], fe.at[i, which, nprompts - 1], sem).wait()
    out1 = pltpu.make_async_copy(r.acc.at[pl.ds(0, 24)], keep, r.sem)
    out1.start()
    per = r.es.shape[2] // 128
    for t in range(24):
        r.es[0, t // per, t % per * 128 : t % per * 128 + 128, :] = r.acc[24 + t].astype(BF16)
    outs = []
    for t in range(24):
        outs.append(pltpu.make_async_copy(r.es.at[0, t // per, pl.ds(t % per * 128, 128), :], send.at[t], r.sem2))
        outs[-1].start()
    for k in range(18):
        if 4 <= k % 9 < 8:
            sgo[k : k + 1, :] = r.sgb[k // 9, k % 9 - 4 : k % 9 - 3, :]
        else:
            part = r.sg[k // 9, k % 9 * D : k % 9 * D + D, :].T
            sgo[k : k + 1, :] = jnp.sum(part, axis=0, keepdims=True)
    out1.wait()
    for cp in outs:
        cp.wait()


def call(N, counts, place, dst, rows, far, emb, cot, emb_far, cot_far, pbr, pieces):
    S = N if N <= 4 else 2
    n = counts.shape[0]
    _, T, D = emb.shape
    V = pltpu.VMEM
    H = 4 * D
    scr = [
        V((2, 9 * D, 128), F32), V((2, 3 * D, D), BF16), V((2, D, D), BF16), V((2, H, D), BF16), V((2, D, H), BF16),
        V((2, D, 3 * D), BF16), V((2, D, D), BF16), V((2, D, H), BF16), V((2, H, D), BF16),
        V((256, 256), F32),
        V((D, T), F32), V((D, T), F32), V((D, T), F32), V((D, T), F32), V((T, D), F32),
        V((D, T), BF16), V((D + 16, T), BF16), V((D, T), F32), V((H, T), BF16),
        V((D, T), BF16), V((D, T), BF16), V((D, T), BF16), V((3 * D, T), BF16),
        V((2 * S, D, T), F32), V((2 * S, 3 * D, T), BF16),
        V((2 * S, HEADS, T * (T // 256 + 1) // 2, 256), BF16), V((2 * S, HEADS, T), F32), V((2 * S, D, T), BF16),
        V((2, 9 * D, 128), F32), V((T, D), BF16), V((48, 128, D), F32),
        V((T, D), F32), V((T, D), BF16), V((2, 8, D), F32),
        pltpu.SemaphoreType.DMA, pltpu.SemaphoreType.DMA, pltpu.SemaphoreType.DMA, pltpu.SemaphoreType.DMA,
    ]
    if N > S:
        scr.append(V((N, D, T), F32))
    A = pl.BlockSpec(memory_space=pl.ANY)
    VM = pl.BlockSpec(memory_space=pltpu.VMEM)
    SM = pl.BlockSpec(memory_space=pltpu.SMEM)
    return pl.pallas_call(
        functools.partial(kernel, S, N, n, len(pieces)),
        out_shape=(
            jax.ShapeDtypeStruct((N, 2, n, T // N, D), BF16),
            jax.ShapeDtypeStruct((24, 128, D), F32), jax.ShapeDtypeStruct((24, 128, D), BF16),
            jax.ShapeDtypeStruct((18, D), F32)),
        in_specs=[SM] * 5 + [A] * 4 + [VM] + [A] * len(pieces),
        out_specs=(A, A, A, VM),
        scratch_shapes=scr,
        compiler_params=pltpu.CompilerParams(vmem_limit_bytes=63 * 1024 * 1024),
    )(counts, place, dst, rows, far, emb, cot, emb_far, cot_far, pbr, *pieces)


STEP = 10
beta_one = 0.9
beta_two = 0.999
learn_rate = 0.05
small_rate = 0.3
weight_decay = 0.1
adam_eps = 1e-08


def adam_update(gradient, first_old, second_old, weight, decay_rate, rate):
    first_new = beta_one * first_old + (1.0 - beta_one) * gradient
    second_new = beta_two * second_old + (1.0 - beta_two) * gradient * gradient
    corr_one = 1.0 - beta_one**STEP
    corr_two = 1.0 - beta_two**STEP
    update = first_new / corr_one / (jnp.sqrt(second_new / corr_two) + adam_eps)
    return (first_new, second_new, weight - rate * (update + decay_rate * weight))


def ranks(key, falling):
    n = key.shape[0]
    i = jnp.arange(n)
    ahead = (key[None, :] > key[:, None]) if falling else (key[None, :] < key[:, None])
    tie = (key[None, :] == key[:, None]) & (i[None, :] < i[:, None])
    return jnp.sum((ahead | tie).astype(jnp.int32), axis=1)


def swap(v, axis, k):
    n = lax.axis_size(axis)
    return lax.ppermute(v, axis, [(i, i ^ k) for i in range(n)])


def pick(v, i, axis):
    return lax.dynamic_index_in_dim(v, i, axis, keepdims=False)


def gather_tiles(low, N, Z, s):
    OWN, H, D = low.shape
    R = OWN * H // N
    part = pick(low.reshape(N, R, D), s, 0)
    zs = jnp.stack([part] + [swap(part, "dp", 2 * k) for k in range(1, Z)])
    near = [zs] + [swap(zs, "section", k) for k in range(1, N)]
    pieces = near + [swap(v, "dp", 1) for v in near]
    where = [(cc, zz, k, h) for cc in (0, 1) for k in range(N) for zz in range(Z) for h in range(R // 64)]
    return [v.reshape(-1, 64, D) for v in pieces], where, near[1]


def tree(v):
    return v[0] if len(v) == 1 else tree([v[i] + v[i + 1] for i in range(0, len(v), 2)])


def reduce_all(part, small, N, Z, s, z):
    _, rows, D = part.shape
    R = rows // N
    part = part.reshape(Z, N, R, D)
    n = small.shape[0]
    small = jnp.concatenate([small, jnp.zeros((-n % 8, D), F32)])

    def step(v, axis, ks, me, dim, small):
        low = small.astype(BF16)
        shape = pick(v, me, dim).shape
        flat = lambda k: pick(v, me ^ k, dim).reshape(-1, D).astype(BF16)
        got = [swap(jnp.concatenate([flat(k), low]), axis, f * k) for f, k in ks]
        total = pick(v, me, dim).reshape(-1, D)
        m = total.shape[0]
        for g in got:
            total = total + g[:m].astype(F32)
        return total.reshape(shape), tree([low.astype(F32)] + [g[m:].astype(F32) for g in got])

    part, small = step(part, "section", [(1, k) for k in range(1, N)], s, 1, small)
    part, small = step(part, "dp", [(2, k) for k in range(1, Z)], z, 0, small)
    part = part.astype(BF16)
    every = jnp.stack([part] + [swap(part, "section", k) for k in range(1, N)])
    return jnp.concatenate([pick(every, s ^ j, 0) for j in range(N)], axis=0).astype(F32), small[:n]


def order_kernel(N, slots, at, *refs):
    ins, fin, eg = refs[:N], refs[N], refs[N + 1]

    def put(p, _):
        w = at[p]
        for k in range(N):
            for j in range(slots):

                @pl.when(w == k * slots + j)
                def _():
                    fin[p] = ins[k][0, j].astype(F32)
                    eg[p] = ins[k][1, j].astype(F32)

        return 0

    lax.fori_loop(0, fin.shape[0], put, 0)


def in_order(pieces, at, prompts):
    _, slots, C, D = pieces[0].shape
    N = len(pieces)
    VM = pl.BlockSpec(memory_space=pltpu.VMEM)
    out = jax.ShapeDtypeStruct((prompts, C, D), F32)
    return pl.pallas_call(
        functools.partial(order_kernel, N, slots),
        out_shape=(out, out),
        in_specs=[pl.BlockSpec(memory_space=pltpu.SMEM)] + [VM] * N,
        out_specs=(VM, VM),
        compiler_params=pltpu.CompilerParams(vmem_limit_bytes=32 * 1024 * 1024),
    )(at, *pieces)


def plain_jobs(owner_list, counts, N, Z, OWN, s, c):
    PR = counts.shape[0]
    jobs = R()
    pos = ranks(owner_list, False)
    owner, slot = pos // OWN, pos % OWN
    jobs.place = ((owner % 2) ^ c) * (Z * OWN) + owner // 2 * OWN + slot
    tiles = jnp.arange(pos.shape[0])
    order = jnp.sum(jnp.where(tiles[:, None] == pos[None, :], tiles[None, :], 0), axis=1)
    jobs.dst = (2 * order[:, None] + jnp.arange(2)[None, :]).reshape(-1)
    rank = ranks(counts, True)
    slots = -(-PR // N)
    j = jnp.arange(slots)
    want = j * N + jnp.where(j % 2 == 0, s, N - 1 - s)
    hit = want[:, None] == rank[None, :]
    jobs.rows = jnp.sum(jnp.where(hit, jnp.arange(PR)[None, :], 0), axis=1).astype(jnp.int32)
    jobs.counts = jnp.sum(jnp.where(hit, counts[None, :], 0), axis=1).astype(jnp.int32)
    jobs.far = jnp.zeros((slots,), jnp.int32)
    k = rank // N
    w = jnp.where(k % 2 == 0, rank % N, N - 1 - rank % N)
    jobs.at = (w ^ s) * slots + k
    return jobs


def plan_kernel(N, Z, OWN, where, owner, mine, theirs, ids, place, dst, rows, cnts, far, at, order, used, srt, prm):
    s, z, c = ids[0], ids[1], ids[2]
    PR = 2 * N
    for o in range(2 * Z):
        used[o] = 0
    for t in range(place.shape[0]):
        o = owner[t]
        i = used[o]
        used[o] = i + 1
        order[o * OWN + i] = t
        place[t] = ((o & 1) ^ c) * (Z * OWN) + (o >> 1) * OWN + i
    for i, (cc, zz, k, h) in enumerate(where):
        half = (s ^ k) * (2 * OWN // N) + h
        dst[i] = 2 * order[((z ^ zz) * 2 + (c ^ cc)) * OWN + (half >> 1)] + (half & 1)

    def ranked(ref, base, keep):
        v = [ref[i] for i in range(PR)]
        got = []
        for i in range(PR):
            r = 0
            for j in range(PR):
                if j != i:
                    r = r + jnp.where(v[j] >= v[i] if j < i else v[j] > v[i], 1, 0)
            srt[base + r] = v[i]
            if keep:
                srt[2 * PR + r] = i
            got.append(r)
        return got

    rank = ranked(mine, c * PR, True)
    ranked(theirs, (1 - c) * PR, False)
    a = [srt[i] for i in range(PR)]
    b = [srt[PR + i] for i in range(PR)]
    kept, traded = {}, {}
    for i in range(N):
        for j in range(N):
            kept[i, j] = jnp.maximum(a[i] + a[PR - 1 - i], b[j] + b[PR - 1 - j])
            traded[i, j] = jnp.maximum(a[i] + b[PR - 1 - j], b[j] + a[PR - 1 - i])
    best = None
    for p in itertools.permutations(range(N)):
        worst = functools.reduce(jnp.maximum, [jnp.minimum(kept[i, p[i]], traded[i, p[i]]) for i in range(N)])
        if best is None:
            best, perm = worst, [jnp.int32(v) for v in p]
        else:
            less = worst < best
            best = jnp.where(less, worst, best)
            perm = [jnp.where(less, jnp.int32(v), u) for u, v in zip(perm, p)]
    for i in range(N):
        prm[i] = perm[i]
        prm[N + perm[i]] = i
    trade = jnp.int32(0)
    for i in range(N):
        for j in range(N):
            cell = (s == i) & (prm[i] == j)
            trade = jnp.where(cell & (traded[i, j] < kept[i, j]), 1, trade)
    pair = jnp.where(c == 0, s, prm[s])
    other = jnp.where(c == 0, prm[s], s)
    rows[0] = srt[2 * PR + pair]
    rows[1] = srt[2 * PR + PR - 1 - pair]
    far[0] = 0
    far[1] = trade
    cnts[0] = srt[c * PR + pair]
    cnts[1] = srt[jnp.where(trade != 0, (1 - c) * PR + PR - 1 - other, c * PR + PR - 1 - pair)]
    for p in range(PR):
        low = rank[p] >= N
        j = jnp.where(low, PR - 1 - rank[p], rank[p])
        w = jnp.where(c == 0, j, prm[N + j])
        at[p] = (w ^ s) * 2 + jnp.where(low, 1, 0)


def plan(owner_list, mine, theirs, ids, where, N, Z, OWN):
    SM = pl.BlockSpec(memory_space=pltpu.SMEM)
    tiles, PR = owner_list.shape[0], mine.shape[0]
    sizes = (tiles, 2 * tiles, 2, 2, 2, PR)
    jobs = R()
    jobs.place, jobs.dst, jobs.rows, jobs.counts, jobs.far, jobs.at = pl.pallas_call(
        functools.partial(plan_kernel, N, Z, OWN, where),
        out_shape=[jax.ShapeDtypeStruct((n,), jnp.int32) for n in sizes],
        in_specs=[SM] * 4,
        out_specs=[SM] * 6,
        scratch_shapes=[pltpu.SMEM((n,), jnp.int32) for n in (tiles, 2 * Z, 3 * PR, 2 * N)],
    )(owner_list, mine, theirs, ids)
    return jobs


def shards(embedding, cotangent, counts, owner_list, tiles_owned, first_owned, second_owned,
           small_params, small_first, small_second):
    N, DP = lax.axis_size("section"), lax.axis_size("dp")
    Z = DP // 2
    s, dp = lax.axis_index("section"), lax.axis_index("dp")
    z, c = dp // 2, dp % 2
    PR, T, D = embedding.shape
    OWN, H, _ = tiles_owned.shape
    low = tiles_owned.astype(BF16)
    shared = PR == 2 * N and OWN * H % (64 * N) == 0
    if shared:
        pieces, where, early = gather_tiles(low, N, Z, s)
        jobs = plan(owner_list, counts, swap(counts, "dp", 1), jnp.stack([s, z, c]), where, N, Z, OWN)
        row, _ = lax.optimization_barrier((jobs.rows[1], early))
        emb_far, cot_far = (swap(pick(v, row, 0), "dp", 1) for v in (embedding, cotangent))
    else:
        pieces = [lax.all_gather(low, "dp", axis=0, tiled=True).reshape(-1, 64, D)]
        jobs = plain_jobs(owner_list, counts, N, Z, OWN, s, c)
        emb_far, cot_far = embedding[0], cotangent[0]
    fe, keep, send, sg = call(N, jobs.counts, jobs.place, jobs.dst, jobs.rows, jobs.far, embedding, cotangent,
                              emb_far, cot_far, small_params, pieces)
    if shared:
        other = swap(fe[:, :, 1], "dp", 1)
        fe = jnp.stack([fe[:, :, 0], jnp.where(jobs.far[1] != 0, other, fe[:, :, 1])], axis=2)
    done = [pick(fe, s, 0)] + [swap(pick(fe, s ^ k, 0), "section", k) for k in range(1, N)]
    part = (keep + swap(send, "dp", 1).astype(F32)).reshape(Z, OWN * H, D)
    tile_grad, small_grad = reduce_all(part, sg + swap(sg, "dp", 1), N, Z, s, z)
    tile_grad = tile_grad.reshape(OWN, H, D)
    fin, eg = in_order(done, jobs.at, PR)
    tile_first, tile_second, tile_new = adam_update(
        tile_grad, first_owned, second_owned, tiles_owned, weight_decay, learn_rate
    )
    small_first_new, small_second_new, small_new = adam_update(
        small_grad, small_first, small_second, small_params, 0.0, small_rate
    )
    return (fin, eg, tile_grad, tile_first, tile_second, tile_new,
            small_grad, small_first_new, small_second_new, small_new)


def solution(mesh):
    P = jax.sharding.PartitionSpec
    own, rep = P("dp", None, None), P()
    return jax.shard_map(
        shards,
        mesh=mesh,
        in_specs=(own, own, P("dp"), rep, own, own, own, rep, rep, rep),
        out_specs=(P("dp", "section", None),) * 2 + (own,) * 4 + (rep,) * 4,
        check_vma=False,
    )
```

```python
import functools
import itertools
import math

import jax
import jax.numpy as jnp
from jax import lax
from jax.experimental import pallas as pl
from jax.experimental.pallas import tpu as pltpu

F32, BF16 = jnp.float32, jnp.bfloat16
HEADS = 8
EPS = 1e-5
MASKED = -1e30
GC0 = math.sqrt(2.0 / math.pi)
GC1 = 0.044715


def nn(a, b):
    return lax.dot_general(a, b, (((1,), (0,)), ((), ())), preferred_element_type=F32)


def nt(a, b):
    return lax.dot_general(a, b, (((1,), (1,)), ((), ())), preferred_element_type=F32)


def tn(a, b):
    return lax.dot_general(a, b, (((0,), (0,)), ((), ())), preferred_element_type=F32)


def wide(col, n):
    return jnp.concatenate([col] * (n // 128), axis=1)


def fold(a):
    r = a[:, 0:128]
    for i in range(1, a.shape[1] // 128):
        r = r + a[:, 128 * i : 128 * i + 128]
    return r


def normed(x):
    d = x.shape[0]
    mean = jnp.sum(x, axis=0, keepdims=True) * (1.0 / d)
    xc = x - mean
    var = jnp.sum(xc * xc, axis=0, keepdims=True) * (1.0 / d)
    rstd = lax.rsqrt(var + EPS)
    return xc * rstd, mean, rstd


def norm_back(dn, xhat, rstd, gain):
    d = dn.shape[0]
    dx = dn * gain
    a = jnp.sum(dx, axis=0, keepdims=True) * (1.0 / d)
    b = jnp.sum(dx * xhat, axis=0, keepdims=True) * (1.0 / d)
    return rstd * (dx - a - xhat * b)


def staged(jobs, *stages):
    state = [{} for _ in jobs]
    low = min(k for _, k in stages)
    high = max(k for _, k in stages)
    for i in range(-high, len(jobs) - low):
        for f, k in stages:
            if 0 <= i + k < len(jobs):
                f(state[i + k], *jobs[i + k])


class R:
    pass


def layer_fwd(r, l, sl, T, D):
    hd = D // HEADS
    pr = lambda k, n=1: r.pb[l, pl.ds(k * D, n * D), :]
    x = r.cur[...]
    r.xs[sl] = x
    xhat, r.stats[sl, 0:1, :], r.stats[sl, 1:2, :] = normed(x)
    r.n1[...] = (xhat * wide(pr(0), T) + wide(pr(1), T)).astype(BF16)
    c2 = hd**-0.5 * math.log2(math.e)
    for i in range(3):
        v = nn(r.wt_qkv[l, pl.ds(i * D, D), :], r.n1[...])
        r.qkv[sl, pl.ds(i * D, D), :] = (v * c2 if i == 0 else v).astype(BF16)
    ones16 = jnp.ones((16, T), BF16)
    jobs = [(h, b) for h in range(HEADS) for b in range(T // 256)]

    def scores(d, h, b):
        kk = 256 * (b + 1)
        k = r.qkv[sl, pl.ds(D + h * hd, hd), pl.ds(0, kk)]
        d[0] = tn(k, r.qkv[sl, pl.ds(h * hd, hd), pl.ds(256 * b, 256)])

    def probs(d, h, b):
        s = d.pop(0)
        kk = 256 * (b + 1)
        tail = s[kk - 256 :, :] + r.mask[...]
        mx = jnp.max(tail, axis=0, keepdims=True)
        if b == 0:
            e = jnp.exp2(tail - mx).astype(BF16)
        else:
            lead = s[: kk - 256, :]
            mx = jnp.maximum(mx, jnp.max(lead, axis=0, keepdims=True))
            e = jnp.concatenate([jnp.exp2(lead - mx).astype(BF16), jnp.exp2(tail - mx).astype(BF16)], axis=0)
        r.es[sl, h, pl.ds(128 * b * (b + 1), kk), :] = e
        d[1] = e

    def context(d, h, b):
        e = d.pop(1)
        kk = 256 * (b + 1)
        v = r.qkv[sl, pl.ds(2 * D + h * hd, hd), pl.ds(0, kk)]
        o = nn(jnp.concatenate([v, ones16[:, :kk]], axis=0), e)
        linv = 1.0 / o[hd : hd + 1, :]
        r.linv[sl, pl.ds(h, 1), pl.ds(256 * b, 256)] = linv
        r.ctx[sl, pl.ds(h * hd, hd), pl.ds(256 * b, 256)] = (o[:hd, :] * linv).astype(BF16)

    staged(jobs, (scores, 2), (probs, 0), (context, -2))
    m = r.xs[sl] + nn(r.wt_o[l], r.ctx[sl])
    r.cur[...] = m
    mhat, r.stats[sl, 2:3, :], r.stats[sl, 3:4, :] = normed(m)
    r.n2[:D, :] = (mhat * wide(pr(2), T) + wide(pr(3), T)).astype(BF16)
    r.cur[...] = r.cur[...] + wide(pr(8), T)

    def up(d, i):
        d[0] = nn(r.wt_up[l, pl.ds(i * D, D), :], r.n2[:D, :]) + wide(pr(4 + i), T)

    def act(d, i):
        h = d.pop(0)
        t1 = 1.0 + jnp.tanh(h * (2 * GC0 + (8 * GC0 * GC1) * (h * h)))
        d[1] = (h * t1).astype(BF16)

    def down(d, i):
        r.cur[...] = r.cur[...] + nn(r.wt_down[l, :, pl.ds(i * D, D)], d.pop(1))

    staged([(i,) for i in range(4)], (up, 1), (act, 0), (down, -1))


def layer_bwd(r, l, sl, T, D):
    hd = D // HEADS
    c = hd**-0.5
    pr = lambda k, n=1: r.pb[l, pl.ds(k * D, n * D), :]

    def add_small(k, v):
        r.sg[l, pl.ds(k * D, D), :] = r.sg[l, pl.ds(k * D, D), :] + fold(v)

    dy = r.dcur[...]
    r.dylow[...] = dy.astype(BF16)
    add_small(8, dy)
    rstd2 = r.stats[sl, 3:4, :]
    mhat = (r.xs[sl] + nn(r.wt_o[l], r.ctx[sl]) - r.stats[sl, 2:3, :]) * rstd2
    r.hat[...] = mhat
    r.n2[:D, :] = (mhat * wide(pr(2), T) + wide(pr(3), T)).astype(BF16)

    def add_tiles(t, v, gap=1):
        for a in range(2):
            at = r.place[24 * l + t + gap * a]
            r.acc[at] = r.acc[at] + v[128 * a : 128 * a + 128]

    def up(d, i):
        h = nn(r.wt_up[l, pl.ds(i * D, D), :], r.n2[:D, :]) + wide(pr(4 + i), T)
        d[0] = h, nn(r.w_down[l, pl.ds(i * D, D), :], r.dylow[...])

    def act(d, i):
        h, dg = d.pop(0)
        h2 = h * h
        t1 = 1.0 + jnp.tanh(h * (2 * GC0 + (8 * GC0 * GC1) * h2))
        g = h * t1
        du = dg * (t1 + g * (2.0 - t1) * (2 * GC0 + (24 * GC0 * GC1) * h2))
        g, du = g.astype(BF16), du.astype(BF16)
        r.du[pl.ds(i * D, D), :] = du
        d[1] = g, du

    def grads(d, i):
        g, du = d.pop(1)
        add_tiles(16 + 2 * i, nt(g, r.dylow[...]))
        v = nt(r.n2[...], du)
        add_tiles(8 + i, v, 4)
        r.sgb[l, i : i + 1, :] = r.sgb[l, i : i + 1, :] + v[D : D + 1]

    staged([(i,) for i in range(4)], (up, 0), (act, 0), (grads, -1))
    dn2 = nn(r.w_up[l], r.du[...])
    add_small(2, dn2 * r.hat[...])
    add_small(3, dn2)
    dm = r.dcur[...] + norm_back(dn2, r.hat[...], rstd2, wide(pr(2), T))
    r.dcur[...] = dm
    r.dmlow[...] = dm.astype(BF16)

    add_tiles(6, nt(r.ctx[sl], r.dmlow[...]))
    dctx = nn(r.w_o[l], r.dmlow[...])
    for h in range(HEADS):
        hs = slice(h * hd, h * hd + hd)
        r.dctx[hs, :] = (dctx[hs, :] * (r.linv[sl, pl.ds(h, 1), :] * c)).astype(BF16)
    c2 = hd**-0.5 * math.log2(math.e)
    nb = T // 256
    row = lax.broadcasted_iota(jnp.int32, (16, T), 0)
    ones3 = jnp.where(row < 3, 1.0, 0.0).astype(BF16)
    blk = lambda j: slice(256 * j, 256 * j + 256)

    def back_probs(d, h):
        dctx = r.dctx[pl.ds(h * hd, hd), :]
        ctx = r.ctx[sl, pl.ds(h * hd, hd), :].astype(F32)
        nd = -jnp.sum(dctx.astype(F32) * ctx, axis=0, keepdims=True)
        n0 = nd.astype(BF16).astype(F32)
        n1 = (nd - n0).astype(BF16).astype(F32)
        n2 = nd - n0 - n1
        extra = jnp.where(row == 0, n0, jnp.where(row == 1, n1, jnp.where(row == 2, n2, 0.0))).astype(BF16)
        de = jnp.concatenate([dctx, extra], axis=0)
        ve = jnp.concatenate([r.qkv[sl, pl.ds(2 * D + h * hd, hd), :], ones3], axis=0)
        d["dsr"] = [tn(ve[:, : 256 * (b + 1)], de[:, blk(b)]) for b in range(nb)]

    def probs_of(h, b):
        return r.es[sl, h, pl.ds(128 * b * (b + 1), 256 * (b + 1)), :]

    def back_scores(d, h):
        dsr = d.pop("dsr")
        d["ds"] = [(probs_of(h, b).astype(F32) * dsr[b]).astype(BF16) for b in range(nb)]

    def by_key(parts, j):
        return jnp.concatenate([parts[b][blk(j)] for b in range(j, nb)], axis=1)

    def back_v(d, h):
        e = [probs_of(h, b) for b in range(nb)]
        for j in range(nb):
            dv = nt(r.dctx[pl.ds(h * hd, hd), pl.ds(256 * j, T - 256 * j)], by_key(e, j))
            r.dqkv[pl.ds(2 * D + h * hd, hd), pl.ds(256 * j, 256)] = (dv * (1.0 / c)).astype(BF16)

    def back_k(d, h):
        ds = d["ds"]
        for j in range(nb):
            dk = nt(r.qkv[sl, pl.ds(h * hd, hd), pl.ds(256 * j, T - 256 * j)], by_key(ds, j))
            r.dqkv[pl.ds(D + h * hd, hd), pl.ds(256 * j, 256)] = (dk * (1.0 / c2)).astype(BF16)

    def back_q(d, h):
        ds = d["ds"]
        for b in range(nb):
            k = r.qkv[sl, pl.ds(D + h * hd, hd), pl.ds(0, 256 * (b + 1))]
            r.dqkv[pl.ds(h * hd, hd), pl.ds(256 * b, 256)] = nn(k, ds[b]).astype(BF16)

    staged([(h,) for h in range(HEADS)], (back_probs, 1), (back_v, 1), (back_scores, 0), (back_q, -1), (back_k, -1))
    rstd1 = r.stats[sl, 1:2, :]
    xhat = (r.xs[sl] - r.stats[sl, 0:1, :]) * rstd1
    r.hat[...] = xhat
    r.n1[...] = (xhat * wide(pr(0), T) + wide(pr(1), T)).astype(BF16)
    for i in range(3):
        add_tiles(2 * i, nt(r.n1[...], r.dqkv[pl.ds(i * D, D), :]))
    dn1 = nn(r.w_qkv[l], r.dqkv[...])
    add_small(0, dn1 * r.hat[...])
    add_small(1, dn1)
    r.dcur[...] = r.dcur[...] + norm_back(dn1, r.hat[...], rstd1, wide(pr(0), T))


def kernel(S, N, nprompts, npieces, counts, place, dst, rows, far, emb, cot, emb_far, cot_far, pbr, *refs):
    pieces = refs[:npieces]
    fe, keep, send, sgo = refs[npieces : npieces + 4]
    scr = refs[npieces + 4 :]
    r = R()
    (r.pb, r.wt_qkv, r.wt_o, r.wt_up, r.wt_down, r.w_qkv, r.w_o, r.w_up, r.w_down, r.mask,
     r.cur, r.dcur, r.embT, r.gsum, r.io, r.n1, r.n2, r.hat, r.du, r.dylow, r.dmlow, r.dctx, r.dqkv,
     r.xs, r.qkv, r.es, r.linv, r.ctx, r.sg, r.low, r.acc, r.io2, r.low2, r.sgb, r.stats,
     r.sem, r.sem2, r.sem_e, r.sem_c) = scr[:39]
    redo = N > S
    if redo:
        r.hs = scr[39]
    r.place = place
    T, D = r.io.shape
    C = T // N

    def load(p, near_ref, far_ref, to, sem):
        @pl.when(far[p] == 0)
        def _():
            pltpu.make_async_copy(near_ref.at[rows[p]], to, sem).start()

        @pl.when(far[p] != 0)
        def _():
            pltpu.make_async_copy(far_ref, to, sem).start()

    load(0, emb, emb_far, r.io, r.sem_e)
    load(0, cot, cot_far, r.io2, r.sem_c)

    def give(p, which, v, low, sem):
        cps = [pltpu.make_async_copy(low.at[pl.ds(C * i, C), :], fe.at[i, which, p], sem) for i in range(N)]

        @pl.when(p > 0)
        def _():
            for cp in cps:
                cp.wait()

        low[...] = v.T.astype(BF16)
        for cp in cps:
            cp.start()

    def spot(t):
        per = r.es.shape[2] // 64
        return r.es.at[0, t // per, pl.ds(pl.multiple_of(t % per * 64, 64), 64), :]

    cps = []
    for piece in pieces:
        for i in range(piece.shape[0]):
            cps.append(pltpu.make_async_copy(piece.at[i], spot(dst[len(cps)]), r.sem))
    for cp in cps:
        cp.start()
    r.acc[...] = jnp.zeros_like(r.acc)
    r.sg[...] = jnp.zeros_like(r.sg)
    r.sgb[...] = jnp.zeros_like(r.sgb)
    r.n2[D:, :] = jnp.where(lax.broadcasted_iota(jnp.int32, (16, T), 0) == 0, 1.0, 0.0).astype(BF16)
    for k in range(18):
        half = 0.5 if 4 <= k % 9 < 8 else 1.0
        r.pb[k // 9, k % 9 * D : k % 9 * D + D, :] = jnp.broadcast_to(pbr[k : k + 1, :] * half, (128, D)).T
    for cp in cps:
        cp.wait()
    for l in range(2):
        for t in range(24):
            per = r.es.shape[2] // 128
            u = 24 * l + t
            w = r.es[0, u // per, u % per * 128 : u % per * 128 + 128, :]
            if t < 6:
                r.w_qkv[l, t % 2 * 128 : t % 2 * 128 + 128, t // 2 * D : t // 2 * D + D] = w
            elif t < 8:
                r.w_o[l, (t - 6) * 128 : (t - 5) * 128, :] = w
            elif t < 16:
                o, b = (t - 8) // 4 * 128, (t - 8) % 4 * D
                r.w_up[l, o : o + 128, b : b + D] = w
            else:
                r.w_down[l, (t - 16) * 128 : (t - 15) * 128, :] = w
        for natural, turned in ((r.w_qkv, r.wt_qkv), (r.w_o, r.wt_o), (r.w_up, r.wt_up), (r.w_down, r.wt_down)):
            turned[l] = natural[l].T
        r.wt_up[l] = r.wt_up[l] * 0.5
        r.w_down[l] = r.w_down[l] * 0.5
    ki = lax.broadcasted_iota(jnp.int32, (256, 256), 0)
    qi = lax.broadcasted_iota(jnp.int32, (256, 256), 1)
    r.mask[...] = jnp.where(ki <= qi, 0.0, MASKED)

    def prompt(p, _):
        count = counts[p]
        pltpu.make_async_copy(emb_far, r.io, r.sem_e).wait()
        r.embT[...] = r.io[...].T

        @pl.when(p + 1 < nprompts)
        def _():
            load(p + 1, emb, emb_far, r.io, r.sem_e)

        r.cur[...] = jnp.zeros_like(r.cur)

        def forward(j):
            r.cur[...] = r.cur[...] + r.embT[...]

            def fl(l, _):
                layer_fwd(r, l, lax.rem(j, S) * 2 + l, T, D)
                return 0

            lax.fori_loop(0, 2, fl, 0)

        def floop(j, _):
            if redo:
                r.hs[j] = r.cur[...]
            forward(j)
            return 0

        lax.fori_loop(0, count, floop, 0)
        give(p, 0, r.cur[...], r.low, r.sem)
        pltpu.make_async_copy(cot_far, r.io2, r.sem_c).wait()
        r.dcur[...] = r.io2[...].T

        @pl.when(p + 1 < nprompts)
        def _():
            load(p + 1, cot, cot_far, r.io2, r.sem_c)

        r.gsum[...] = jnp.zeros_like(r.gsum)

        def bloop(jj, _):
            j = count - 1 - jj
            if redo:

                @pl.when(jj >= S)
                def _():
                    r.cur[...] = r.hs[j]
                    forward(j)

            def bl(ll, _):
                l = 1 - ll
                layer_bwd(r, l, lax.rem(j, S) * 2 + l, T, D)
                return 0

            lax.fori_loop(0, 2, bl, 0)
            r.gsum[...] = r.gsum[...] + r.dcur[...]
            return 0

        lax.fori_loop(0, count, bloop, 0)
        give(p, 1, r.gsum[...], r.low2, r.sem2)
        return 0

    lax.fori_loop(0, nprompts, prompt, 0)
    for which, low, sem in ((0, r.low, r.sem), (1, r.low2, r.sem2)):
        for i in range(N):
            pltpu.make_async_copy(low.at[pl.ds(C * i, C), :], fe.at[i, which, nprompts - 1], sem).wait()
    parts, Z, span, _ = keep.shape
    half = parts * Z * span // 128
    outs = []

    def put(src, dst, sem):
        for row in range(0, 128 * half, 64):
            o, w = row // (parts * span), row % (parts * span)
            at = dst.at[w // span, o, pl.ds(w % span, 64), :]
            outs.append(pltpu.make_async_copy(src(row), at, sem))
            outs[-1].start()

    put(lambda row: r.acc.at[row // 128, pl.ds(row % 128, 64), :], keep, r.sem)
    per = r.es.shape[2] // 128
    for t in range(half):
        r.es[0, t // per, t % per * 128 : t % per * 128 + 128, :] = r.acc[half + t].astype(BF16)
    put(lambda row: r.es.at[0, row // (128 * per), pl.ds(row % (128 * per), 64), :], send, r.sem2)
    for k in range(18):
        if 4 <= k % 9 < 8:
            sgo[k : k + 1, :] = r.sgb[k // 9, k % 9 - 4 : k % 9 - 3, :]
        else:
            part = r.sg[k // 9, k % 9 * D : k % 9 * D + D, :].T
            sgo[k : k + 1, :] = jnp.sum(part, axis=0, keepdims=True)
    for cp in outs:
        cp.wait()


def call(N, parts, OWN, counts, place, dst, rows, far, emb, cot, emb_far, cot_far, pbr, pieces):
    S = N if N <= 4 else 2
    n = counts.shape[0]
    _, T, D = emb.shape
    V = pltpu.VMEM
    H = 4 * D
    scr = [
        V((2, 9 * D, 128), F32), V((2, 3 * D, D), BF16), V((2, D, D), BF16), V((2, H, D), BF16), V((2, D, H), BF16),
        V((2, D, 3 * D), BF16), V((2, D, D), BF16), V((2, D, H), BF16), V((2, H, D), BF16),
        V((256, 256), F32),
        V((D, T), F32), V((D, T), F32), V((D, T), F32), V((D, T), F32), V((T, D), F32),
        V((D, T), BF16), V((D + 16, T), BF16), V((D, T), F32), V((H, T), BF16),
        V((D, T), BF16), V((D, T), BF16), V((D, T), BF16), V((3 * D, T), BF16),
        V((2 * S, D, T), F32), V((2 * S, 3 * D, T), BF16),
        V((2 * S, HEADS, T * (T // 256 + 1) // 2, 256), BF16), V((2 * S, HEADS, T), F32), V((2 * S, D, T), BF16),
        V((2, 9 * D, 128), F32), V((T, D), BF16), V((48, 128, D), F32),
        V((T, D), F32), V((T, D), BF16), V((2, 8, D), F32), V((2 * S, 8, T), F32),
        pltpu.SemaphoreType.DMA, pltpu.SemaphoreType.DMA, pltpu.SemaphoreType.DMA, pltpu.SemaphoreType.DMA,
    ]
    if N > S:
        scr.append(V((N, D, T), F32))
    half = (parts, 24 // OWN, OWN * 128 // parts, D)
    A = pl.BlockSpec(memory_space=pl.ANY)
    VM = pl.BlockSpec(memory_space=pltpu.VMEM)
    SM = pl.BlockSpec(memory_space=pltpu.SMEM)
    return pl.pallas_call(
        functools.partial(kernel, S, N, n, len(pieces)),
        out_shape=(
            jax.ShapeDtypeStruct((N, 2, n, T // N, D), BF16),
            jax.ShapeDtypeStruct(half, F32), jax.ShapeDtypeStruct(half, BF16),
            jax.ShapeDtypeStruct((18, D), F32)),
        in_specs=[SM] * 5 + [A] * 4 + [VM] + [A] * len(pieces),
        out_specs=(A, A, A, VM),
        scratch_shapes=scr,
        compiler_params=pltpu.CompilerParams(vmem_limit_bytes=63 * 1024 * 1024),
    )(counts, place, dst, rows, far, emb, cot, emb_far, cot_far, pbr, *pieces)


STEP = 10
beta_one = 0.9
beta_two = 0.999
learn_rate = 0.05
small_rate = 0.3
weight_decay = 0.1
adam_eps = 1e-08


def adam_update(gradient, first_old, second_old, weight, decay_rate, rate):
    first_new = beta_one * first_old + (1.0 - beta_one) * gradient
    second_new = beta_two * second_old + (1.0 - beta_two) * gradient * gradient
    corr_one = 1.0 - beta_one**STEP
    corr_two = 1.0 - beta_two**STEP
    update = first_new / corr_one / (jnp.sqrt(second_new / corr_two) + adam_eps)
    return (first_new, second_new, weight - rate * (update + decay_rate * weight))


def ranks(key, falling):
    n = key.shape[0]
    i = jnp.arange(n)
    ahead = (key[None, :] > key[:, None]) if falling else (key[None, :] < key[:, None])
    tie = (key[None, :] == key[:, None]) & (i[None, :] < i[:, None])
    return jnp.sum((ahead | tie).astype(jnp.int32), axis=1)


def swap(v, axis, k):
    n = lax.axis_size(axis)
    return lax.ppermute(v, axis, [(i, i ^ k) for i in range(n)])


def pick(v, i, axis):
    return lax.dynamic_index_in_dim(v, i, axis, keepdims=False)


def gather_tiles(low, N, Z, s):
    OWN, H, D = low.shape
    R = OWN * H // N
    part = pick(low.reshape(N, R, D), s, 0)
    zs = jnp.stack([part] + [swap(part, "dp", 2 * k) for k in range(1, Z)])
    near = [zs] + [swap(zs, "section", k) for k in range(1, N)]
    pieces = near + [swap(v, "dp", 1) for v in near]
    where = [(cc, zz, k, h) for cc in (0, 1) for k in range(N) for zz in range(Z) for h in range(R // 64)]
    return [v.reshape(-1, 64, D) for v in pieces], where, near[1]


def tree(v):
    return v[0] if len(v) == 1 else tree([v[i] + v[i + 1] for i in range(0, len(v), 2)])


def reduce_all(keep, send, small, N, Z, s, z):
    if keep.shape[0] != N:
        keep, send = (v.reshape(Z, N, -1, v.shape[-1]).swapaxes(0, 1) for v in (keep, send))
    _, _, R, D = keep.shape
    n = small.shape[0]
    small = small + swap(small, "dp", 1)
    low = jnp.concatenate([small, jnp.zeros((-n % 8, D), F32)]).astype(BF16)
    ks = list(range(1, N)) + [0]
    got = {k: swap(pick(send, s ^ k, 0), "dp", 1) for k in ks}
    both = {k: (pick(keep, s ^ k, 0) + got[k].astype(F32)).reshape(Z * R, D) for k in ks}
    far = [swap(jnp.concatenate([both[k].astype(BF16), low]), "section", k) for k in range(1, N)]
    part = functools.reduce(lambda x, v: x + v[: Z * R].astype(F32), far, both[0]).reshape(Z, R, D)
    low = tree([low.astype(F32)] + [v[Z * R :].astype(F32) for v in far]).astype(BF16)
    far = [swap(jnp.concatenate([pick(part, z ^ k, 0).astype(BF16), low]), "dp", 2 * k) for k in range(1, Z)]
    done = functools.reduce(lambda x, v: x + v[:R].astype(F32), far, pick(part, z, 0)).astype(BF16)
    low = tree([low.astype(F32)] + [v[R:].astype(F32) for v in far])
    every = jnp.stack([done] + [swap(done, "section", k) for k in range(1, N)])
    return jnp.concatenate([pick(every, s ^ j, 0) for j in range(N)], axis=0).astype(F32), low[:n], part


def order_kernel(N, slots, at, *refs):
    ins, fin, eg = refs[:N], refs[N], refs[N + 1]

    def put(p, _):
        w = at[p]
        for k in range(N):
            for j in range(slots):

                @pl.when(w == k * slots + j)
                def _():
                    fin[p] = ins[k][0, j].astype(F32)
                    eg[p] = ins[k][1, j].astype(F32)

        return 0

    lax.fori_loop(0, fin.shape[0], put, 0)


def in_order(pieces, at, prompts):
    _, slots, C, D = pieces[0].shape
    N = len(pieces)
    VM = pl.BlockSpec(memory_space=pltpu.VMEM)
    out = jax.ShapeDtypeStruct((prompts, C, D), F32)
    return pl.pallas_call(
        functools.partial(order_kernel, N, slots),
        out_shape=(out, out),
        in_specs=[pl.BlockSpec(memory_space=pltpu.SMEM)] + [VM] * N,
        out_specs=(VM, VM),
        compiler_params=pltpu.CompilerParams(vmem_limit_bytes=32 * 1024 * 1024),
    )(at, *pieces)


def plain_jobs(owner_list, counts, N, Z, OWN, s, c):
    PR = counts.shape[0]
    jobs = R()
    pos = ranks(owner_list, False)
    owner, slot = pos // OWN, pos % OWN
    jobs.place = ((owner % 2) ^ c) * (Z * OWN) + owner // 2 * OWN + slot
    tiles = jnp.arange(pos.shape[0])
    order = jnp.sum(jnp.where(tiles[:, None] == pos[None, :], tiles[None, :], 0), axis=1)
    jobs.dst = (2 * order[:, None] + jnp.arange(2)[None, :]).reshape(-1)
    rank = ranks(counts, True)
    slots = -(-PR // N)
    j = jnp.arange(slots)
    want = j * N + jnp.where(j % 2 == 0, s, N - 1 - s)
    hit = want[:, None] == rank[None, :]
    jobs.rows = jnp.sum(jnp.where(hit, jnp.arange(PR)[None, :], 0), axis=1).astype(jnp.int32)
    jobs.counts = jnp.sum(jnp.where(hit, counts[None, :], 0), axis=1).astype(jnp.int32)
    jobs.far = jnp.zeros((slots,), jnp.int32)
    k = rank // N
    w = jnp.where(k % 2 == 0, rank % N, N - 1 - rank % N)
    jobs.at = (w ^ s) * slots + k
    return jobs


def plan_kernel(N, Z, OWN, where, owner, mine, theirs, ids, place, dst, rows, cnts, far, at, order, used, srt, prm):
    s, z, c = ids[0], ids[1], ids[2]
    PR = 2 * N
    for o in range(2 * Z):
        used[o] = 0
    for t in range(place.shape[0]):
        o = owner[t]
        i = used[o]
        used[o] = i + 1
        order[o * OWN + i] = t
        place[t] = ((o & 1) ^ c) * (Z * OWN) + (o >> 1) * OWN + i
    for i, (cc, zz, k, h) in enumerate(where):
        half = (s ^ k) * (2 * OWN // N) + h
        dst[i] = 2 * order[((z ^ zz) * 2 + (c ^ cc)) * OWN + (half >> 1)] + (half & 1)

    def ranked(ref, base, keep):
        v = [ref[i] for i in range(PR)]
        got = []
        for i in range(PR):
            r = 0
            for j in range(PR):
                if j != i:
                    r = r + jnp.where(v[j] >= v[i] if j < i else v[j] > v[i], 1, 0)
            srt[base + r] = v[i]
            if keep:
                srt[2 * PR + r] = i
            got.append(r)
        return got

    rank = ranked(mine, c * PR, True)
    ranked(theirs, (1 - c) * PR, False)
    a = [srt[i] for i in range(PR)]
    b = [srt[PR + i] for i in range(PR)]
    kept, traded = {}, {}
    for i in range(N):
        for j in range(N):
            kept[i, j] = jnp.maximum(a[i] + a[PR - 1 - i], b[j] + b[PR - 1 - j])
            traded[i, j] = jnp.maximum(a[i] + b[PR - 1 - j], b[j] + a[PR - 1 - i])
    best = None
    for p in itertools.permutations(range(N)):
        worst = functools.reduce(jnp.maximum, [jnp.minimum(kept[i, p[i]], traded[i, p[i]]) for i in range(N)])
        if best is None:
            best, perm = worst, [jnp.int32(v) for v in p]
        else:
            less = worst < best
            best = jnp.where(less, worst, best)
            perm = [jnp.where(less, jnp.int32(v), u) for u, v in zip(perm, p)]
    for i in range(N):
        prm[i] = perm[i]
        prm[N + perm[i]] = i
    trade = jnp.int32(0)
    for i in range(N):
        for j in range(N):
            cell = (s == i) & (prm[i] == j)
            trade = jnp.where(cell & (traded[i, j] < kept[i, j]), 1, trade)
    pair = jnp.where(c == 0, s, prm[s])
    other = jnp.where(c == 0, prm[s], s)
    rows[0] = srt[2 * PR + pair]
    rows[1] = srt[2 * PR + PR - 1 - pair]
    far[0] = 0
    far[1] = trade
    cnts[0] = srt[c * PR + pair]
    cnts[1] = srt[jnp.where(trade != 0, (1 - c) * PR + PR - 1 - other, c * PR + PR - 1 - pair)]
    for p in range(PR):
        low = rank[p] >= N
        j = jnp.where(low, PR - 1 - rank[p], rank[p])
        w = jnp.where(c == 0, j, prm[N + j])
        at[p] = (w ^ s) * 2 + jnp.where(low, 1, 0)


def plan(owner_list, mine, theirs, ids, where, N, Z, OWN):
    SM = pl.BlockSpec(memory_space=pltpu.SMEM)
    tiles, PR = owner_list.shape[0], mine.shape[0]
    sizes = (tiles, 2 * tiles, 2, 2, 2, PR)
    jobs = R()
    jobs.place, jobs.dst, jobs.rows, jobs.counts, jobs.far, jobs.at = pl.pallas_call(
        functools.partial(plan_kernel, N, Z, OWN, where),
        out_shape=[jax.ShapeDtypeStruct((n,), jnp.int32) for n in sizes],
        in_specs=[SM] * 4,
        out_specs=[SM] * 6,
        scratch_shapes=[pltpu.SMEM((n,), jnp.int32) for n in (tiles, 2 * Z, 3 * PR, 2 * N)],
    )(owner_list, mine, theirs, ids)
    return jobs


def shards(embedding, cotangent, counts, owner_list, tiles_owned, first_owned, second_owned,
           small_params, small_first, small_second):
    N, DP = lax.axis_size("section"), lax.axis_size("dp")
    Z = DP // 2
    s, dp = lax.axis_index("section"), lax.axis_index("dp")
    z, c = dp // 2, dp % 2
    PR, T, D = embedding.shape
    OWN, H, _ = tiles_owned.shape
    low = tiles_owned.astype(BF16)
    shared = PR == 2 * N and OWN * H % (64 * N) == 0
    if shared:
        pieces, where, early = gather_tiles(low, N, Z, s)
        jobs = plan(owner_list, counts, swap(counts, "dp", 1), jnp.stack([s, z, c]), where, N, Z, OWN)
        row, _ = lax.optimization_barrier((jobs.rows[1], early))
        emb_far, cot_far = (swap(pick(v, row, 0), "dp", 1) for v in (embedding, cotangent))
    else:
        pieces = [lax.all_gather(low, "dp", axis=0, tiled=True).reshape(-1, 64, D)]
        jobs = plain_jobs(owner_list, counts, N, Z, OWN, s, c)
        emb_far, cot_far = embedding[0], cotangent[0]
    fe, keep, send, sg = call(N, N if shared else 1, OWN, jobs.counts, jobs.place, jobs.dst, jobs.rows, jobs.far, embedding, cotangent,
                              emb_far, cot_far, small_params, pieces)
    if shared:
        other = swap(fe[:, :, 1], "dp", 1)
        fe = jnp.stack([fe[:, :, 0], jnp.where(jobs.far[1] != 0, other, fe[:, :, 1])], axis=2)
    tile_grad, small_grad, halfway = reduce_all(keep, send, sg, N, Z, s, z)
    tile_grad = tile_grad.reshape(OWN, H, D)
    fe, _ = lax.optimization_barrier((fe, halfway))
    done = [pick(fe, s, 0)] + [swap(pick(fe, s ^ k, 0), "section", k) for k in range(1, N)]
    fin, eg = in_order(done, jobs.at, PR)
    tile_first, tile_second, tile_new = adam_update(
        tile_grad, first_owned, second_owned, tiles_owned, weight_decay, learn_rate
    )
    small_first_new, small_second_new, small_new = adam_update(
        small_grad, small_first, small_second, small_params, 0.0, small_rate
    )
    return (fin, eg, tile_grad, tile_first, tile_second, tile_new,
            small_grad, small_first_new, small_second_new, small_new)


def solution(mesh):
    P = jax.sharding.PartitionSpec
    own, rep = P("dp", None, None), P()
    return jax.shard_map(
        shards,
        mesh=mesh,
        in_specs=(own, own, P("dp"), rep, own, own, own, rep, rep, rep),
        out_specs=(P("dp", "section", None),) * 2 + (own,) * 4 + (rep,) * 4,
        check_vma=False,
    )
```

```python
import functools
import itertools
import math

import jax
import jax.numpy as jnp
from jax import lax
from jax.experimental import pallas as pl
from jax.experimental.pallas import tpu as pltpu

F32, BF16 = jnp.float32, jnp.bfloat16
HEADS = 8
EPS = 1e-5
MASKED = -1e30
GC0 = math.sqrt(2.0 / math.pi)
GC1 = 0.044715


def nn(a, b):
    return lax.dot_general(a, b, (((1,), (0,)), ((), ())), preferred_element_type=F32)


def nt(a, b):
    return lax.dot_general(a, b, (((1,), (1,)), ((), ())), preferred_element_type=F32)


def tn(a, b):
    return lax.dot_general(a, b, (((0,), (0,)), ((), ())), preferred_element_type=F32)


def wide(col, n):
    return jnp.concatenate([col] * (n // 128), axis=1)


def fold(a):
    r = a[:, 0:128]
    for i in range(1, a.shape[1] // 128):
        r = r + a[:, 128 * i : 128 * i + 128]
    return r


def normed(x):
    d = x.shape[0]
    mean = jnp.sum(x, axis=0, keepdims=True) * (1.0 / d)
    xc = x - mean
    var = jnp.sum(xc * xc, axis=0, keepdims=True) * (1.0 / d)
    rstd = lax.rsqrt(var + EPS)
    return xc * rstd, mean, rstd


def norm_back(dn, xhat, rstd, gain):
    d = dn.shape[0]
    dx = dn * gain
    a = jnp.sum(dx, axis=0, keepdims=True) * (1.0 / d)
    b = jnp.sum(dx * xhat, axis=0, keepdims=True) * (1.0 / d)
    return rstd * (dx - a - xhat * b)


def staged(jobs, *stages):
    state = [{} for _ in jobs]
    low = min(k for _, k in stages)
    high = max(k for _, k in stages)
    for i in range(-high, len(jobs) - low):
        for f, k in stages:
            if 0 <= i + k < len(jobs):
                f(state[i + k], *jobs[i + k])


class R:
    pass


def layer_fwd(r, l, sl, T, D):
    hd = D // HEADS
    pr = lambda k, n=1: r.pb[l, pl.ds(k * D, n * D), :]
    x = r.cur[...]
    r.xs[sl] = x
    xhat, r.stats[sl, 0:1, :], r.stats[sl, 1:2, :] = normed(x)
    r.n1[...] = (xhat * wide(pr(0), T) + wide(pr(1), T)).astype(BF16)
    c2 = hd**-0.5 * math.log2(math.e)
    for i in range(3):
        v = nn(r.wt_qkv[l, pl.ds(i * D, D), :], r.n1[...])
        r.qkv[sl, pl.ds(i * D, D), :] = (v * c2 if i == 0 else v).astype(BF16)
    ones16 = jnp.ones((16, T), BF16)
    jobs = [(h, b) for h in range(HEADS) for b in range(T // 256)]

    def scores(d, h, b):
        kk = 256 * (b + 1)
        k = r.qkv[sl, pl.ds(D + h * hd, hd), pl.ds(0, kk)]
        d[0] = tn(k, r.qkv[sl, pl.ds(h * hd, hd), pl.ds(256 * b, 256)])

    def probs(d, h, b):
        s = d.pop(0)
        kk = 256 * (b + 1)
        halves = []
        for i in range(2):
            part = s[:, 128 * i : 128 * i + 128]
            near = kk - 256 + 128 * i
            seen = [part[:near, :]] if near else []
            seen.append(part[near : near + 128, :] + r.mask[...])
            mx = functools.reduce(jnp.maximum, [jnp.max(v, axis=0, keepdims=True) for v in seen])
            e = [jnp.exp2(v - mx).astype(BF16) for v in seen]
            if i == 0:
                e.append(jnp.zeros((128, 128), BF16))
            halves.append(jnp.concatenate(e, axis=0))
        e = jnp.concatenate(halves, axis=1)
        r.es[sl, h, pl.ds(128 * b * (b + 1), kk), :] = e
        d[1] = e

    def context(d, h, b):
        e = d.pop(1)
        kk = 256 * (b + 1)
        v = r.qkv[sl, pl.ds(2 * D + h * hd, hd), pl.ds(0, kk)]
        o = nn(jnp.concatenate([v, ones16[:, :kk]], axis=0), e)
        linv = 1.0 / o[hd : hd + 1, :]
        r.linv[sl, pl.ds(h, 1), pl.ds(256 * b, 256)] = linv
        r.ctx[sl, pl.ds(h * hd, hd), pl.ds(256 * b, 256)] = (o[:hd, :] * linv).astype(BF16)

    staged(jobs, (scores, 3), (probs, 0), (context, -2))
    m = r.xs[sl] + nn(r.wt_o[l], r.ctx[sl])
    r.cur[...] = m
    mhat, r.stats[sl, 2:3, :], r.stats[sl, 3:4, :] = normed(m)
    r.n2[:D, :] = (mhat * wide(pr(2), T) + wide(pr(3), T)).astype(BF16)
    r.cur[...] = r.cur[...] + wide(pr(8), T)

    def up(d, i):
        d[0] = nn(r.wt_up[l, pl.ds(i * D, D), :], r.n2[:D, :]) + wide(pr(4 + i), T)

    def act(d, i):
        h = d.pop(0)
        t1 = 1.0 + jnp.tanh(h * (2 * GC0 + (8 * GC0 * GC1) * (h * h)))
        d[1] = (h * t1).astype(BF16)

    def down(d, i):
        r.cur[...] = r.cur[...] + nn(r.wt_down[l, :, pl.ds(i * D, D)], d.pop(1))

    staged([(i,) for i in range(4)], (up, 1), (act, 0), (down, -1))


def layer_bwd(r, l, sl, T, D):
    hd = D // HEADS
    c = hd**-0.5
    pr = lambda k, n=1: r.pb[l, pl.ds(k * D, n * D), :]

    def add_small(k, v):
        r.sg[l, pl.ds(k * D, D), :] = r.sg[l, pl.ds(k * D, D), :] + fold(v)

    dy = r.dcur[...]
    r.dylow[...] = dy.astype(BF16)
    add_small(8, dy)
    rstd2 = r.stats[sl, 3:4, :]
    mhat = (r.xs[sl] + nn(r.wt_o[l], r.ctx[sl]) - r.stats[sl, 2:3, :]) * rstd2
    r.hat[...] = mhat
    r.n2[:D, :] = (mhat * wide(pr(2), T) + wide(pr(3), T)).astype(BF16)

    def add_tiles(t, v, gap=1):
        for a in range(2):
            at = r.place[24 * l + t + gap * a]
            r.acc[at] = r.acc[at] + v[128 * a : 128 * a + 128]

    def up(d, i):
        h = nn(r.wt_up[l, pl.ds(i * D, D), :], r.n2[:D, :]) + wide(pr(4 + i), T)
        d[0] = h, nn(r.w_down[l, pl.ds(i * D, D), :], r.dylow[...])

    def act(d, i):
        h, dg = d.pop(0)
        h2 = h * h
        t1 = 1.0 + jnp.tanh(h * (2 * GC0 + (8 * GC0 * GC1) * h2))
        g = h * t1
        du = dg * (t1 + g * (2.0 - t1) * (2 * GC0 + (24 * GC0 * GC1) * h2))
        g, du = g.astype(BF16), du.astype(BF16)
        r.du[pl.ds(i * D, D), :] = du
        d[1] = g, du

    def grads(d, i):
        g, du = d.pop(1)
        add_tiles(16 + 2 * i, nt(g, r.dylow[...]))
        v = nt(r.n2[...], du)
        add_tiles(8 + i, v, 4)
        r.sgb[l, i : i + 1, :] = r.sgb[l, i : i + 1, :] + v[D : D + 1]

    staged([(i,) for i in range(4)], (up, 0), (act, 0), (grads, -1))
    dn2 = nn(r.w_up[l], r.du[...])
    add_small(2, dn2 * r.hat[...])
    add_small(3, dn2)
    dm = r.dcur[...] + norm_back(dn2, r.hat[...], rstd2, wide(pr(2), T))
    r.dcur[...] = dm
    r.dmlow[...] = dm.astype(BF16)

    add_tiles(6, nt(r.ctx[sl], r.dmlow[...]))
    dctx = nn(r.w_o[l], r.dmlow[...])
    for h in range(HEADS):
        hs = slice(h * hd, h * hd + hd)
        r.dctx[hs, :] = (dctx[hs, :] * (r.linv[sl, pl.ds(h, 1), :] * c)).astype(BF16)
    c2 = hd**-0.5 * math.log2(math.e)
    nb = T // 256
    row = lax.broadcasted_iota(jnp.int32, (16, T), 0)
    ones3 = jnp.where(row < 3, 1.0, 0.0).astype(BF16)
    blk = lambda j: slice(256 * j, 256 * j + 256)

    def back_probs(d, h):
        dctx = r.dctx[pl.ds(h * hd, hd), :]
        ctx = r.ctx[sl, pl.ds(h * hd, hd), :].astype(F32)
        nd = -jnp.sum(dctx.astype(F32) * ctx, axis=0, keepdims=True)
        n0 = nd.astype(BF16).astype(F32)
        n1 = (nd - n0).astype(BF16).astype(F32)
        n2 = nd - n0 - n1
        extra = jnp.where(row == 0, n0, jnp.where(row == 1, n1, jnp.where(row == 2, n2, 0.0))).astype(BF16)
        de = jnp.concatenate([dctx, extra], axis=0)
        ve = jnp.concatenate([r.qkv[sl, pl.ds(2 * D + h * hd, hd), :], ones3], axis=0)
        d["dsr"] = [tn(ve[:, : 256 * (b + 1)], de[:, blk(b)]) for b in range(nb)]

    def probs_of(h, b):
        return r.es[sl, h, pl.ds(128 * b * (b + 1), 256 * (b + 1)), :]

    def back_scores(d, h):
        dsr = d.pop("dsr")
        d["ds"] = [(probs_of(h, b).astype(F32) * dsr[b]).astype(BF16) for b in range(nb)]

    def by_key(parts, j):
        return jnp.concatenate([parts[b][blk(j)] for b in range(j, nb)], axis=1)

    def back_v(d, h):
        e = [probs_of(h, b) for b in range(nb)]
        for j in range(nb):
            dv = nt(r.dctx[pl.ds(h * hd, hd), pl.ds(256 * j, T - 256 * j)], by_key(e, j))
            r.dqkv[pl.ds(2 * D + h * hd, hd), pl.ds(256 * j, 256)] = (dv * (1.0 / c)).astype(BF16)

    def back_k(d, h):
        ds = d["ds"]
        for j in range(nb):
            dk = nt(r.qkv[sl, pl.ds(h * hd, hd), pl.ds(256 * j, T - 256 * j)], by_key(ds, j))
            r.dqkv[pl.ds(D + h * hd, hd), pl.ds(256 * j, 256)] = (dk * (1.0 / c2)).astype(BF16)

    def back_q(d, h):
        ds = d["ds"]
        for b in range(nb):
            k = r.qkv[sl, pl.ds(D + h * hd, hd), pl.ds(0, 256 * (b + 1))]
            r.dqkv[pl.ds(h * hd, hd), pl.ds(256 * b, 256)] = nn(k, ds[b]).astype(BF16)

    staged([(h,) for h in range(HEADS)], (back_probs, 1), (back_v, 1), (back_scores, 0), (back_q, -1), (back_k, -1))
    rstd1 = r.stats[sl, 1:2, :]
    xhat = (r.xs[sl] - r.stats[sl, 0:1, :]) * rstd1
    r.hat[...] = xhat
    r.n1[...] = (xhat * wide(pr(0), T) + wide(pr(1), T)).astype(BF16)
    for i in range(3):
        add_tiles(2 * i, nt(r.n1[...], r.dqkv[pl.ds(i * D, D), :]))
    dn1 = nn(r.w_qkv[l], r.dqkv[...])
    add_small(0, dn1 * r.hat[...])
    add_small(1, dn1)
    r.dcur[...] = r.dcur[...] + norm_back(dn1, r.hat[...], rstd1, wide(pr(0), T))


def kernel(S, N, nprompts, npieces, counts, place, dst, rows, far, emb, cot, emb_far, cot_far, pbr, *refs):
    pieces = refs[:npieces]
    fe, keep, send, sgo = refs[npieces : npieces + 4]
    scr = refs[npieces + 4 :]
    r = R()
    (r.pb, r.wt_qkv, r.wt_o, r.wt_up, r.wt_down, r.w_qkv, r.w_o, r.w_up, r.w_down, r.mask,
     r.cur, r.dcur, r.embT, r.gsum, r.io, r.n1, r.n2, r.hat, r.du, r.dylow, r.dmlow, r.dctx, r.dqkv,
     r.xs, r.qkv, r.es, r.linv, r.ctx, r.sg, r.low, r.acc, r.io2, r.low2, r.sgb, r.stats,
     r.sem, r.sem2, r.sem_e, r.sem_c) = scr[:39]
    redo = N > S
    if redo:
        r.hs = scr[39]
    r.place = place
    T, D = r.io.shape
    C = T // N

    def load(p, near_ref, far_ref, to, sem):
        @pl.when(far[p] == 0)
        def _():
            pltpu.make_async_copy(near_ref.at[rows[p]], to, sem).start()

        @pl.when(far[p] != 0)
        def _():
            pltpu.make_async_copy(far_ref, to, sem).start()

    load(0, emb, emb_far, r.io, r.sem_e)
    load(0, cot, cot_far, r.io2, r.sem_c)

    def give(p, which, v, low, sem):
        cps = [pltpu.make_async_copy(low.at[pl.ds(C * i, C), :], fe.at[p, i, which], sem) for i in range(N)]

        @pl.when(p > 0)
        def _():
            for cp in cps:
                cp.wait()

        low[...] = v.T.astype(BF16)
        for cp in cps:
            cp.start()

    def spot(t):
        per = r.es.shape[2] // 64
        return r.es.at[0, t // per, pl.ds(pl.multiple_of(t % per * 64, 64), 64), :]

    cps = []
    for piece in pieces:
        for i in range(piece.shape[0]):
            cps.append(pltpu.make_async_copy(piece.at[i], spot(dst[len(cps)]), r.sem))
    for cp in cps:
        cp.start()
    r.acc[...] = jnp.zeros_like(r.acc)
    r.sg[...] = jnp.zeros_like(r.sg)
    r.sgb[...] = jnp.zeros_like(r.sgb)
    r.n2[D:, :] = jnp.where(lax.broadcasted_iota(jnp.int32, (16, T), 0) == 0, 1.0, 0.0).astype(BF16)
    for k in range(18):
        half = 0.5 if 4 <= k % 9 < 8 else 1.0
        r.pb[k // 9, k % 9 * D : k % 9 * D + D, :] = jnp.broadcast_to(pbr[k : k + 1, :] * half, (128, D)).T
    for cp in cps:
        cp.wait()
    for l in range(2):
        for t in range(24):
            per = r.es.shape[2] // 128
            u = 24 * l + t
            w = r.es[0, u // per, u % per * 128 : u % per * 128 + 128, :]
            if t < 6:
                r.w_qkv[l, t % 2 * 128 : t % 2 * 128 + 128, t // 2 * D : t // 2 * D + D] = w
            elif t < 8:
                r.w_o[l, (t - 6) * 128 : (t - 5) * 128, :] = w
            elif t < 16:
                o, b = (t - 8) // 4 * 128, (t - 8) % 4 * D
                r.w_up[l, o : o + 128, b : b + D] = w
            else:
                r.w_down[l, (t - 16) * 128 : (t - 15) * 128, :] = w
        for natural, turned in ((r.w_qkv, r.wt_qkv), (r.w_o, r.wt_o), (r.w_up, r.wt_up), (r.w_down, r.wt_down)):
            turned[l] = natural[l].T
        r.wt_up[l] = r.wt_up[l] * 0.5
        r.w_down[l] = r.w_down[l] * 0.5
    ki = lax.broadcasted_iota(jnp.int32, (128, 128), 0)
    qi = lax.broadcasted_iota(jnp.int32, (128, 128), 1)
    r.mask[...] = jnp.where(ki <= qi, 0.0, MASKED)

    def prompt(p, _):
        count = counts[p]
        pltpu.make_async_copy(emb_far, r.io, r.sem_e).wait()
        r.embT[...] = r.io[...].T

        @pl.when(p + 1 < nprompts)
        def _():
            load(p + 1, emb, emb_far, r.io, r.sem_e)

        r.cur[...] = jnp.zeros_like(r.cur)

        def forward(j):
            r.cur[...] = r.cur[...] + r.embT[...]

            def fl(l, _):
                layer_fwd(r, l, lax.rem(j, S) * 2 + l, T, D)
                return 0

            lax.fori_loop(0, 2, fl, 0)

        def floop(j, _):
            if redo:
                r.hs[j] = r.cur[...]
            forward(j)
            return 0

        lax.fori_loop(0, count, floop, 0)
        give(p, 0, r.cur[...], r.low, r.sem)
        pltpu.make_async_copy(cot_far, r.io2, r.sem_c).wait()
        r.dcur[...] = r.io2[...].T

        @pl.when(p + 1 < nprompts)
        def _():
            load(p + 1, cot, cot_far, r.io2, r.sem_c)

        r.gsum[...] = jnp.zeros_like(r.gsum)

        def bloop(jj, _):
            j = count - 1 - jj
            if redo:

                @pl.when(jj >= S)
                def _():
                    r.cur[...] = r.hs[j]
                    forward(j)

            def bl(ll, _):
                l = 1 - ll
                layer_bwd(r, l, lax.rem(j, S) * 2 + l, T, D)
                return 0

            lax.fori_loop(0, 2, bl, 0)
            r.gsum[...] = r.gsum[...] + r.dcur[...]
            return 0

        lax.fori_loop(0, count, bloop, 0)
        give(p, 1, r.gsum[...], r.low2, r.sem2)
        return 0

    lax.fori_loop(0, nprompts, prompt, 0)
    for which, low, sem in ((0, r.low, r.sem), (1, r.low2, r.sem2)):
        for i in range(N):
            pltpu.make_async_copy(low.at[pl.ds(C * i, C), :], fe.at[nprompts - 1, i, which], sem).wait()
    parts, Z, span, _ = keep.shape
    half = parts * Z * span // 128
    outs = []

    def put(src, dst, sem):
        for row in range(0, 128 * half, 64):
            o, w = row // (parts * span), row % (parts * span)
            at = dst.at[w // span, o, pl.ds(w % span, 64), :]
            outs.append(pltpu.make_async_copy(src(row), at, sem))
            outs[-1].start()

    put(lambda row: r.acc.at[row // 128, pl.ds(row % 128, 64), :], keep, r.sem)
    per = r.es.shape[2] // 128
    for t in range(half):
        r.es[0, t // per, t % per * 128 : t % per * 128 + 128, :] = r.acc[half + t].astype(BF16)
    put(lambda row: r.es.at[0, row // (128 * per), pl.ds(row % (128 * per), 64), :], send, r.sem2)
    for k in range(18):
        if 4 <= k % 9 < 8:
            sgo[k : k + 1, :] = r.sgb[k // 9, k % 9 - 4 : k % 9 - 3, :]
        else:
            part = r.sg[k // 9, k % 9 * D : k % 9 * D + D, :].T
            sgo[k : k + 1, :] = jnp.sum(part, axis=0, keepdims=True)
    for cp in outs:
        cp.wait()


def call(N, parts, OWN, counts, place, dst, rows, far, emb, cot, emb_far, cot_far, pbr, pieces):
    S = N if N <= 4 else 2
    n = counts.shape[0]
    _, T, D = emb.shape
    V = pltpu.VMEM
    H = 4 * D
    scr = [
        V((2, 9 * D, 128), F32), V((2, 3 * D, D), BF16), V((2, D, D), BF16), V((2, H, D), BF16), V((2, D, H), BF16),
        V((2, D, 3 * D), BF16), V((2, D, D), BF16), V((2, D, H), BF16), V((2, H, D), BF16),
        V((128, 128), F32),
        V((D, T), F32), V((D, T), F32), V((D, T), F32), V((D, T), F32), V((T, D), F32),
        V((D, T), BF16), V((D + 16, T), BF16), V((D, T), F32), V((H, T), BF16),
        V((D, T), BF16), V((D, T), BF16), V((D, T), BF16), V((3 * D, T), BF16),
        V((2 * S, D, T), F32), V((2 * S, 3 * D, T), BF16),
        V((2 * S, HEADS, T * (T // 256 + 1) // 2, 256), BF16), V((2 * S, HEADS, T), F32), V((2 * S, D, T), BF16),
        V((2, 9 * D, 128), F32), V((T, D), BF16), V((48, 128, D), F32),
        V((T, D), F32), V((T, D), BF16), V((2, 8, D), F32), V((2 * S, 8, T), F32),
        pltpu.SemaphoreType.DMA, pltpu.SemaphoreType.DMA, pltpu.SemaphoreType.DMA, pltpu.SemaphoreType.DMA,
    ]
    if N > S:
        scr.append(V((N, D, T), F32))
    half = (parts, 24 // OWN, OWN * 128 // parts, D)
    A = pl.BlockSpec(memory_space=pl.ANY)
    VM = pl.BlockSpec(memory_space=pltpu.VMEM)
    SM = pl.BlockSpec(memory_space=pltpu.SMEM)
    return pl.pallas_call(
        functools.partial(kernel, S, N, n, len(pieces)),
        out_shape=(
            jax.ShapeDtypeStruct((n, N, 2, T // N, D), BF16),
            jax.ShapeDtypeStruct(half, F32), jax.ShapeDtypeStruct(half, BF16),
            jax.ShapeDtypeStruct((18, D), F32)),
        in_specs=[SM] * 5 + [A] * 4 + [VM] + [A] * len(pieces),
        out_specs=(A, A, A, VM),
        scratch_shapes=scr,
        compiler_params=pltpu.CompilerParams(vmem_limit_bytes=63 * 1024 * 1024),
    )(counts, place, dst, rows, far, emb, cot, emb_far, cot_far, pbr, *pieces)


STEP = 10
beta_one = 0.9
beta_two = 0.999
learn_rate = 0.05
small_rate = 0.3
weight_decay = 0.1
adam_eps = 1e-08


def adam_update(gradient, first_old, second_old, weight, decay_rate, rate):
    first_new = beta_one * first_old + (1.0 - beta_one) * gradient
    second_new = beta_two * second_old + (1.0 - beta_two) * gradient * gradient
    corr_one = 1.0 - beta_one**STEP
    corr_two = 1.0 - beta_two**STEP
    update = first_new / corr_one / (jnp.sqrt(second_new / corr_two) + adam_eps)
    return (first_new, second_new, weight - rate * (update + decay_rate * weight))


def ranks(key, falling):
    n = key.shape[0]
    i = jnp.arange(n)
    ahead = (key[None, :] > key[:, None]) if falling else (key[None, :] < key[:, None])
    tie = (key[None, :] == key[:, None]) & (i[None, :] < i[:, None])
    return jnp.sum((ahead | tie).astype(jnp.int32), axis=1)


def swap(v, axis, k):
    n = lax.axis_size(axis)
    return lax.ppermute(v, axis, [(i, i ^ k) for i in range(n)])


def pick(v, i, axis):
    return lax.dynamic_index_in_dim(v, i, axis, keepdims=False)


def gather_tiles(low, N, Z, s):
    OWN, H, D = low.shape
    R = OWN * H // N
    part = pick(low.reshape(N, R, D), s, 0)
    zs = jnp.stack([part] + [swap(part, "dp", 2 * k) for k in range(1, Z)])
    near = [zs] + [swap(zs, "section", k) for k in range(1, N)]
    pieces = near + [swap(v, "dp", 1) for v in near]
    where = [(cc, zz, k, h) for cc in (0, 1) for k in range(N) for zz in range(Z) for h in range(R // 64)]
    return [v.reshape(-1, 64, D) for v in pieces], where, near[1]


def tree(v):
    return v[0] if len(v) == 1 else tree([v[i] + v[i + 1] for i in range(0, len(v), 2)])


def reduce_all(keep, send, small, N, Z, s, z):
    if keep.shape[0] != N:
        keep, send = (v.reshape(Z, N, -1, v.shape[-1]).swapaxes(0, 1) for v in (keep, send))
    _, _, R, D = keep.shape
    n = small.shape[0]
    small = small + swap(small, "dp", 1)
    low = jnp.concatenate([small, jnp.zeros((-n % 8, D), F32)]).astype(BF16)
    ks = list(range(1, N)) + [0]
    got = {k: swap(pick(send, s ^ k, 0), "dp", 1) for k in ks}
    both = {k: (pick(keep, s ^ k, 0) + got[k].astype(F32)).reshape(Z * R, D) for k in ks}
    far = [swap(jnp.concatenate([both[k].astype(BF16), low]), "section", k) for k in range(1, N)]
    part = functools.reduce(lambda x, v: x + v[: Z * R].astype(F32), far, both[0]).reshape(Z, R, D)
    low = tree([low.astype(F32)] + [v[Z * R :].astype(F32) for v in far]).astype(BF16)
    far = [swap(jnp.concatenate([pick(part, z ^ k, 0).astype(BF16), low]), "dp", 2 * k) for k in range(1, Z)]
    done = functools.reduce(lambda x, v: x + v[:R].astype(F32), far, pick(part, z, 0)).astype(BF16)
    low = tree([low.astype(F32)] + [v[R:].astype(F32) for v in far])
    every = jnp.stack([done] + [swap(done, "section", k) for k in range(1, N)])
    return jnp.concatenate([pick(every, s ^ j, 0) for j in range(N)], axis=0).astype(F32), low[:n], part


def order_kernel(N, slots, at, *refs):
    ins, fin, eg = refs[:-2], refs[-2], refs[-1]

    def put(p, _):
        w = at[p]
        for k in range(N):
            for j in range(slots):

                @pl.when(w == k * slots + j)
                def _():
                    fin[p] = ins[k * slots + j][0].astype(F32)
                    eg[p] = ins[k * slots + j][1].astype(F32)

        return 0

    lax.fori_loop(0, fin.shape[0], put, 0)


def in_order(pieces, slots, at, prompts):
    _, C, D = pieces[0].shape
    N = len(pieces) // slots
    VM = pl.BlockSpec(memory_space=pltpu.VMEM)
    out = jax.ShapeDtypeStruct((prompts, C, D), F32)
    return pl.pallas_call(
        functools.partial(order_kernel, N, slots),
        out_shape=(out, out),
        in_specs=[pl.BlockSpec(memory_space=pltpu.SMEM)] + [VM] * len(pieces),
        out_specs=(VM, VM),
        compiler_params=pltpu.CompilerParams(vmem_limit_bytes=32 * 1024 * 1024),
    )(at, *pieces)


def plain_jobs(owner_list, counts, N, Z, OWN, s, c):
    PR = counts.shape[0]
    jobs = R()
    pos = ranks(owner_list, False)
    owner, slot = pos // OWN, pos % OWN
    jobs.place = ((owner % 2) ^ c) * (Z * OWN) + owner // 2 * OWN + slot
    tiles = jnp.arange(pos.shape[0])
    order = jnp.sum(jnp.where(tiles[:, None] == pos[None, :], tiles[None, :], 0), axis=1)
    jobs.dst = (2 * order[:, None] + jnp.arange(2)[None, :]).reshape(-1)
    rank = ranks(counts, True)
    slots = -(-PR // N)
    j = jnp.arange(slots)
    want = j * N + jnp.where(j % 2 == 0, s, N - 1 - s)
    hit = want[:, None] == rank[None, :]
    jobs.rows = jnp.sum(jnp.where(hit, jnp.arange(PR)[None, :], 0), axis=1).astype(jnp.int32)
    jobs.counts = jnp.sum(jnp.where(hit, counts[None, :], 0), axis=1).astype(jnp.int32)
    jobs.far = jnp.zeros((slots,), jnp.int32)
    k = rank // N
    w = jnp.where(k % 2 == 0, rank % N, N - 1 - rank % N)
    jobs.at = (w ^ s) * slots + k
    return jobs


def plan_kernel(N, Z, OWN, where, owner, mine, theirs, ids, place, dst, rows, cnts, far, at, order, used, srt, prm):
    s, z, c = ids[0], ids[1], ids[2]
    PR = 2 * N
    for o in range(2 * Z):
        used[o] = 0
    for t in range(place.shape[0]):
        o = owner[t]
        i = used[o]
        used[o] = i + 1
        order[o * OWN + i] = t
        place[t] = ((o & 1) ^ c) * (Z * OWN) + (o >> 1) * OWN + i
    for i, (cc, zz, k, h) in enumerate(where):
        half = (s ^ k) * (2 * OWN // N) + h
        dst[i] = 2 * order[((z ^ zz) * 2 + (c ^ cc)) * OWN + (half >> 1)] + (half & 1)

    def ranked(ref, base, keep):
        v = [ref[i] for i in range(PR)]
        got = []
        for i in range(PR):
            r = 0
            for j in range(PR):
                if j != i:
                    r = r + jnp.where(v[j] >= v[i] if j < i else v[j] > v[i], 1, 0)
            srt[base + r] = v[i]
            if keep:
                srt[2 * PR + r] = i
            got.append(r)
        return got

    rank = ranked(mine, c * PR, True)
    ranked(theirs, (1 - c) * PR, False)
    a = [srt[i] for i in range(PR)]
    b = [srt[PR + i] for i in range(PR)]
    kept, traded = {}, {}
    for i in range(N):
        for j in range(N):
            kept[i, j] = jnp.maximum(a[i] + a[PR - 1 - i], b[j] + b[PR - 1 - j])
            traded[i, j] = jnp.maximum(a[i] + b[PR - 1 - j], b[j] + a[PR - 1 - i])
    best = None
    for p in itertools.permutations(range(N)):
        worst = functools.reduce(jnp.maximum, [jnp.minimum(kept[i, p[i]], traded[i, p[i]]) for i in range(N)])
        if best is None:
            best, perm = worst, [jnp.int32(v) for v in p]
        else:
            less = worst < best
            best = jnp.where(less, worst, best)
            perm = [jnp.where(less, jnp.int32(v), u) for u, v in zip(perm, p)]
    for i in range(N):
        prm[i] = perm[i]
        prm[N + perm[i]] = i
    trade = jnp.int32(0)
    for i in range(N):
        for j in range(N):
            cell = (s == i) & (prm[i] == j)
            trade = jnp.where(cell & (traded[i, j] < kept[i, j]), 1, trade)
    pair = jnp.where(c == 0, s, prm[s])
    other = jnp.where(c == 0, prm[s], s)
    rows[0] = srt[2 * PR + pair]
    rows[1] = srt[2 * PR + PR - 1 - pair]
    far[0] = 0
    far[1] = trade
    cnts[0] = srt[c * PR + pair]
    cnts[1] = srt[jnp.where(trade != 0, (1 - c) * PR + PR - 1 - other, c * PR + PR - 1 - pair)]
    for p in range(PR):
        low = rank[p] >= N
        j = jnp.where(low, PR - 1 - rank[p], rank[p])
        w = jnp.where(c == 0, j, prm[N + j])
        at[p] = (w ^ s) * 2 + jnp.where(low, 1, 0)


def plan(owner_list, mine, theirs, ids, where, N, Z, OWN):
    SM = pl.BlockSpec(memory_space=pltpu.SMEM)
    tiles, PR = owner_list.shape[0], mine.shape[0]
    sizes = (tiles, 2 * tiles, 2, 2, 2, PR)
    jobs = R()
    jobs.place, jobs.dst, jobs.rows, jobs.counts, jobs.far, jobs.at = pl.pallas_call(
        functools.partial(plan_kernel, N, Z, OWN, where),
        out_shape=[jax.ShapeDtypeStruct((n,), jnp.int32) for n in sizes],
        in_specs=[SM] * 4,
        out_specs=[SM] * 6,
        scratch_shapes=[pltpu.SMEM((n,), jnp.int32) for n in (tiles, 2 * Z, 3 * PR, 2 * N)],
    )(owner_list, mine, theirs, ids)
    return jobs


def shards(embedding, cotangent, counts, owner_list, tiles_owned, first_owned, second_owned,
           small_params, small_first, small_second):
    N, DP = lax.axis_size("section"), lax.axis_size("dp")
    Z = DP // 2
    s, dp = lax.axis_index("section"), lax.axis_index("dp")
    z, c = dp // 2, dp % 2
    PR, T, D = embedding.shape
    OWN, H, _ = tiles_owned.shape
    low = tiles_owned.astype(BF16)
    shared = PR == 2 * N and OWN * H % (64 * N) == 0
    if shared:
        pieces, where, early = gather_tiles(low, N, Z, s)
        jobs = plan(owner_list, counts, swap(counts, "dp", 1), jnp.stack([s, z, c]), where, N, Z, OWN)
        row, _ = lax.optimization_barrier((jobs.rows[1], early))
        emb_far, cot_far = (swap(pick(v, row, 0), "dp", 1) for v in (embedding, cotangent))
    else:
        pieces = [lax.all_gather(low, "dp", axis=0, tiled=True).reshape(-1, 64, D)]
        jobs = plain_jobs(owner_list, counts, N, Z, OWN, s, c)
        emb_far, cot_far = embedding[0], cotangent[0]
    fe, keep, send, sg = call(N, N if shared else 1, OWN, jobs.counts, jobs.place, jobs.dst, jobs.rows, jobs.far, embedding, cotangent,
                              emb_far, cot_far, small_params, pieces)
    slots = [fe[j] for j in range(fe.shape[0])]
    tile_grad, small_grad, halfway = reduce_all(keep, send, sg, N, Z, s, z)
    tile_grad = tile_grad.reshape(OWN, H, D)
    if shared:
        other = swap(slots[1], "dp", 1)
        mine = jnp.where(jobs.far[1] != 0, other, slots[1])
        slots[1], _ = lax.optimization_barrier((mine, halfway))
    done = [pick(v, s, 0) for v in slots]
    for k in range(1, N):
        done += [swap(pick(v, s ^ k, 0), "section", k) for v in slots]
    fin, eg = in_order(done, len(slots), jobs.at, PR)
    tile_first, tile_second, tile_new = adam_update(
        tile_grad, first_owned, second_owned, tiles_owned, weight_decay, learn_rate
    )
    small_first_new, small_second_new, small_new = adam_update(
        small_grad, small_first, small_second, small_params, 0.0, small_rate
    )
    return (fin, eg, tile_grad, tile_first, tile_second, tile_new,
            small_grad, small_first_new, small_second_new, small_new)


def solution(mesh):
    P = jax.sharding.PartitionSpec
    own, rep = P("dp", None, None), P()
    return jax.shard_map(
        shards,
        mesh=mesh,
        in_specs=(own, own, P("dp"), rep, own, own, own, rep, rep, rep),
        out_specs=(P("dp", "section", None),) * 2 + (own,) * 4 + (rep,) * 4,
        check_vma=False,
    )
```

```python
import functools
import itertools
import math

import jax
import jax.numpy as jnp
from jax import lax
from jax.experimental import pallas as pl
from jax.experimental.pallas import tpu as pltpu

F32, BF16 = jnp.float32, jnp.bfloat16
HEADS = 8
EPS = 1e-5
MASKED = -1e30
GC0 = math.sqrt(2.0 / math.pi)
GC1 = 0.044715


def nn(a, b):
    return lax.dot_general(a, b, (((1,), (0,)), ((), ())), preferred_element_type=F32)


def nt(a, b):
    return lax.dot_general(a, b, (((1,), (1,)), ((), ())), preferred_element_type=F32)


def tn(a, b):
    return lax.dot_general(a, b, (((0,), (0,)), ((), ())), preferred_element_type=F32)


def wide(col, n):
    return jnp.concatenate([col] * (n // 128), axis=1)


def fold(a):
    r = a[:, 0:128]
    for i in range(1, a.shape[1] // 128):
        r = r + a[:, 128 * i : 128 * i + 128]
    return r


def normed(x):
    d = x.shape[0]
    mean = jnp.sum(x, axis=0, keepdims=True) * (1.0 / d)
    xc = x - mean
    var = jnp.sum(xc * xc, axis=0, keepdims=True) * (1.0 / d)
    rstd = lax.rsqrt(var + EPS)
    return xc * rstd, mean, rstd


def norm_back(dn, xhat, rstd, gain):
    d = dn.shape[0]
    dx = dn * gain
    a = jnp.sum(dx, axis=0, keepdims=True) * (1.0 / d)
    b = jnp.sum(dx * xhat, axis=0, keepdims=True) * (1.0 / d)
    return rstd * (dx - a - xhat * b)


def staged(jobs, *stages):
    state = [{} for _ in jobs]
    low = min(k for _, k in stages)
    high = max(k for _, k in stages)
    for i in range(-high, len(jobs) - low):
        for f, k in stages:
            if 0 <= i + k < len(jobs):
                f(state[i + k], *jobs[i + k])


class R:
    pass


def layer_fwd(r, l, sl, T, D):
    hd = D // HEADS
    pr = lambda k, n=1: r.pb[l, pl.ds(k * D, n * D), :]
    x = r.cur[...]
    r.xs[sl] = x
    xhat, r.stats[sl, 0:1, :], r.stats[sl, 1:2, :] = normed(x)
    r.n1[...] = (xhat * wide(pr(0), T) + wide(pr(1), T)).astype(BF16)
    c2 = hd**-0.5 * math.log2(math.e)
    for i in range(3):
        v = nn(r.wt_qkv[l, pl.ds(i * D, D), :], r.n1[...])
        r.qkv[sl, pl.ds(i * D, D), :] = (v * c2 if i == 0 else v).astype(BF16)
    ones16 = jnp.ones((16, T), BF16)
    jobs = [(h, b) for h in range(HEADS) for b in range(T // 256)]

    def scores(d, h, b):
        kk = 256 * (b + 1)
        k = r.qkv[sl, pl.ds(D + h * hd, hd), pl.ds(0, kk)]
        d[0] = tn(k, r.qkv[sl, pl.ds(h * hd, hd), pl.ds(256 * b, 256)])

    def probs(d, h, b):
        s = d.pop(0)
        kk = 256 * (b + 1)
        halves = []
        for i in range(2):
            part = s[:, 128 * i : 128 * i + 128]
            near = kk - 256 + 128 * i
            seen = [part[:near, :]] if near else []
            seen.append(part[near : near + 128, :] + r.mask[...])
            mx = functools.reduce(jnp.maximum, [jnp.max(v, axis=0, keepdims=True) for v in seen])
            e = [jnp.exp2(v - mx).astype(BF16) for v in seen]
            if i == 0:
                e.append(jnp.zeros((128, 128), BF16))
            halves.append(jnp.concatenate(e, axis=0))
        e = jnp.concatenate(halves, axis=1)
        r.es[sl, h, pl.ds(128 * b * (b + 1), kk), :] = e
        d[1] = e

    def context(d, h, b):
        e = d.pop(1)
        kk = 256 * (b + 1)
        v = r.qkv[sl, pl.ds(2 * D + h * hd, hd), pl.ds(0, kk)]
        o = nn(jnp.concatenate([v, ones16[:, :kk]], axis=0), e)
        linv = 1.0 / o[hd : hd + 1, :]
        r.linv[sl, pl.ds(h, 1), pl.ds(256 * b, 256)] = linv
        r.ctx[sl, pl.ds(h * hd, hd), pl.ds(256 * b, 256)] = (o[:hd, :] * linv).astype(BF16)

    staged(jobs, (scores, 3), (probs, 0), (context, -2))
    m = r.xs[sl] + nn(r.wt_o[l], r.ctx[sl])
    r.cur[...] = m
    mhat, r.stats[sl, 2:3, :], r.stats[sl, 3:4, :] = normed(m)
    r.n2[:D, :] = (mhat * wide(pr(2), T) + wide(pr(3), T)).astype(BF16)
    r.cur[...] = r.cur[...] + wide(pr(8), T)

    def up(d, i):
        d[0] = nn(r.wt_up[l, pl.ds(i * D, D), :], r.n2[:D, :]) + wide(pr(4 + i), T)

    def act(d, i):
        h = d.pop(0)
        t1 = 1.0 + jnp.tanh(h * (2 * GC0 + (8 * GC0 * GC1) * (h * h)))
        d[1] = (h * t1).astype(BF16)

    def down(d, i):
        r.cur[...] = r.cur[...] + nn(r.wt_down[l, :, pl.ds(i * D, D)], d.pop(1))

    staged([(i,) for i in range(4)], (up, 1), (act, 0), (down, -1))


def layer_bwd(r, l, sl, T, D):
    hd = D // HEADS
    c = hd**-0.5
    pr = lambda k, n=1: r.pb[l, pl.ds(k * D, n * D), :]

    def add_small(k, v):
        r.sg[l, pl.ds(k * D, D), :] = r.sg[l, pl.ds(k * D, D), :] + fold(v)

    dy = r.dcur[...]
    r.dylow[...] = dy.astype(BF16)
    add_small(8, dy)
    rstd2 = r.stats[sl, 3:4, :]
    mhat = (r.xs[sl] + nn(r.wt_o[l], r.ctx[sl]) - r.stats[sl, 2:3, :]) * rstd2
    r.hat[...] = mhat
    r.n2[:D, :] = (mhat * wide(pr(2), T) + wide(pr(3), T)).astype(BF16)

    def add_tiles(t, v, gap=1):
        for a in range(2):
            at = r.place[24 * l + t + gap * a]
            r.acc[at] = r.acc[at] + v[128 * a : 128 * a + 128]

    def up(d, i):
        h = nn(r.wt_up[l, pl.ds(i * D, D), :], r.n2[:D, :]) + wide(pr(4 + i), T)
        d[0] = h, nn(r.w_down[l, pl.ds(i * D, D), :], r.dylow[...])

    def act(d, i):
        h, dg = d.pop(0)
        h2 = h * h
        t1 = 1.0 + jnp.tanh(h * (2 * GC0 + (8 * GC0 * GC1) * h2))
        g = h * t1
        du = dg * (t1 + g * (2.0 - t1) * (2 * GC0 + (24 * GC0 * GC1) * h2))
        g, du = g.astype(BF16), du.astype(BF16)
        r.du[pl.ds(i * D, D), :] = du
        d[1] = g, du

    def grads(d, i):
        g, du = d.pop(1)
        add_tiles(16 + 2 * i, nt(g, r.dylow[...]))
        v = nt(r.n2[...], du)
        add_tiles(8 + i, v, 4)
        r.sgb[l, i : i + 1, :] = r.sgb[l, i : i + 1, :] + v[D : D + 1]

    staged([(i,) for i in range(4)], (up, 0), (act, 0), (grads, -1))
    dn2 = nn(r.w_up[l], r.du[...])
    add_small(2, dn2 * r.hat[...])
    add_small(3, dn2)
    dm = r.dcur[...] + norm_back(dn2, r.hat[...], rstd2, wide(pr(2), T))
    r.dcur[...] = dm
    r.dmlow[...] = dm.astype(BF16)

    add_tiles(6, nt(r.ctx[sl], r.dmlow[...]))
    dctx = nn(r.w_o[l], r.dmlow[...])
    for h in range(HEADS):
        hs = slice(h * hd, h * hd + hd)
        r.dctx[hs, :] = (dctx[hs, :] * (r.linv[sl, pl.ds(h, 1), :] * c)).astype(BF16)
    c2 = hd**-0.5 * math.log2(math.e)
    nb = T // 256
    row = lax.broadcasted_iota(jnp.int32, (16, T), 0)
    ones3 = jnp.where(row < 3, 1.0, 0.0).astype(BF16)
    blk = lambda j: slice(256 * j, 256 * j + 256)

    def back_probs(d, h):
        dctx = r.dctx[pl.ds(h * hd, hd), :]
        ctx = r.ctx[sl, pl.ds(h * hd, hd), :].astype(F32)
        nd = -jnp.sum(dctx.astype(F32) * ctx, axis=0, keepdims=True)
        n0 = nd.astype(BF16).astype(F32)
        n1 = (nd - n0).astype(BF16).astype(F32)
        n2 = nd - n0 - n1
        extra = jnp.where(row == 0, n0, jnp.where(row == 1, n1, jnp.where(row == 2, n2, 0.0))).astype(BF16)
        de = jnp.concatenate([dctx, extra], axis=0)
        ve = jnp.concatenate([r.qkv[sl, pl.ds(2 * D + h * hd, hd), :], ones3], axis=0)
        d["dsr"] = [tn(ve[:, : 256 * (b + 1)], de[:, blk(b)]) for b in range(nb)]

    def probs_of(h, b):
        return r.es[sl, h, pl.ds(128 * b * (b + 1), 256 * (b + 1)), :]

    def back_scores(d, h):
        dsr = d.pop("dsr")
        d["ds"] = [(probs_of(h, b).astype(F32) * dsr[b]).astype(BF16) for b in range(nb)]

    def by_key(parts, j):
        return jnp.concatenate([parts[b][blk(j)] for b in range(j, nb)], axis=1)

    def back_v(d, h):
        e = [probs_of(h, b) for b in range(nb)]
        for j in range(nb):
            dv = nt(r.dctx[pl.ds(h * hd, hd), pl.ds(256 * j, T - 256 * j)], by_key(e, j))
            r.dqkv[pl.ds(2 * D + h * hd, hd), pl.ds(256 * j, 256)] = (dv * (1.0 / c)).astype(BF16)

    def back_k(d, h):
        ds = d["ds"]
        for j in range(nb):
            dk = nt(r.qkv[sl, pl.ds(h * hd, hd), pl.ds(256 * j, T - 256 * j)], by_key(ds, j))
            r.dqkv[pl.ds(D + h * hd, hd), pl.ds(256 * j, 256)] = (dk * (1.0 / c2)).astype(BF16)

    def back_q(d, h):
        ds = d["ds"]
        for b in range(nb):
            k = r.qkv[sl, pl.ds(D + h * hd, hd), pl.ds(0, 256 * (b + 1))]
            r.dqkv[pl.ds(h * hd, hd), pl.ds(256 * b, 256)] = nn(k, ds[b]).astype(BF16)

    staged([(h,) for h in range(HEADS)], (back_probs, 1), (back_v, 1), (back_scores, 0), (back_q, -1), (back_k, -1))
    rstd1 = r.stats[sl, 1:2, :]
    xhat = (r.xs[sl] - r.stats[sl, 0:1, :]) * rstd1
    r.hat[...] = xhat
    r.n1[...] = (xhat * wide(pr(0), T) + wide(pr(1), T)).astype(BF16)
    for i in range(3):
        add_tiles(2 * i, nt(r.n1[...], r.dqkv[pl.ds(i * D, D), :]))
    dn1 = nn(r.w_qkv[l], r.dqkv[...])
    add_small(0, dn1 * r.hat[...])
    add_small(1, dn1)
    r.dcur[...] = r.dcur[...] + norm_back(dn1, r.hat[...], rstd1, wide(pr(0), T))


def kernel(S, N, nprompts, npieces, counts, place, dst, rows, far, emb, cot, emb_far, cot_far, pbr, *refs):
    pieces = refs[:npieces]
    fe, keep, send, sgo = refs[npieces : npieces + 4]
    scr = refs[npieces + 4 :]
    r = R()
    (r.pb, r.wt_qkv, r.wt_o, r.wt_up, r.wt_down, r.w_qkv, r.w_o, r.w_up, r.w_down, r.mask,
     r.cur, r.dcur, r.embT, r.gsum, r.io, r.n1, r.n2, r.hat, r.du, r.dylow, r.dmlow, r.dctx, r.dqkv,
     r.xs, r.qkv, r.es, r.linv, r.ctx, r.sg, r.low, r.acc, r.io2, r.low2, r.sgb, r.stats,
     r.sem, r.sem2, r.sem_e, r.sem_c) = scr[:39]
    redo = N > S
    if redo:
        r.hs = scr[39]
    r.place = place
    T, D = r.io.shape
    C = T // N

    def load(p, near_ref, far_ref, to, sem):
        @pl.when(far[p] == 0)
        def _():
            pltpu.make_async_copy(near_ref.at[rows[p]], to, sem).start()

        @pl.when(far[p] != 0)
        def _():
            pltpu.make_async_copy(far_ref, to, sem).start()

    load(0, emb, emb_far, r.io, r.sem_e)
    load(0, cot, cot_far, r.io2, r.sem_c)

    def give(p, which, v, low, sem):
        cps = [pltpu.make_async_copy(low.at[pl.ds(C * i, C), :], fe.at[p, i, which], sem) for i in range(N)]

        @pl.when(p > 0)
        def _():
            for cp in cps:
                cp.wait()

        low[...] = v.T.astype(BF16)
        for cp in cps:
            cp.start()

    def spot(t):
        per = r.es.shape[2] // 64
        return r.es.at[0, t // per, pl.ds(pl.multiple_of(t % per * 64, 64), 64), :]

    cps = []
    for piece in pieces:
        for i in range(piece.shape[0]):
            cps.append(pltpu.make_async_copy(piece.at[i], spot(dst[len(cps)]), r.sem))
    for cp in cps:
        cp.start()
    r.acc[...] = jnp.zeros_like(r.acc)
    r.sg[...] = jnp.zeros_like(r.sg)
    r.sgb[...] = jnp.zeros_like(r.sgb)
    r.n2[D:, :] = jnp.where(lax.broadcasted_iota(jnp.int32, (16, T), 0) == 0, 1.0, 0.0).astype(BF16)
    for k in range(18):
        half = 0.5 if 4 <= k % 9 < 8 else 1.0
        r.pb[k // 9, k % 9 * D : k % 9 * D + D, :] = jnp.broadcast_to(pbr[k : k + 1, :] * half, (128, D)).T
    for cp in cps:
        cp.wait()
    for l in range(2):
        for t in range(24):
            per = r.es.shape[2] // 128
            u = 24 * l + t
            w = r.es[0, u // per, u % per * 128 : u % per * 128 + 128, :]
            if t < 6:
                r.w_qkv[l, t % 2 * 128 : t % 2 * 128 + 128, t // 2 * D : t // 2 * D + D] = w
            elif t < 8:
                r.w_o[l, (t - 6) * 128 : (t - 5) * 128, :] = w
            elif t < 16:
                o, b = (t - 8) // 4 * 128, (t - 8) % 4 * D
                r.w_up[l, o : o + 128, b : b + D] = w
            else:
                r.w_down[l, (t - 16) * 128 : (t - 15) * 128, :] = w
        for natural, turned in ((r.w_qkv, r.wt_qkv), (r.w_o, r.wt_o), (r.w_up, r.wt_up), (r.w_down, r.wt_down)):
            turned[l] = natural[l].T
        r.wt_up[l] = r.wt_up[l] * 0.5
        r.w_down[l] = r.w_down[l] * 0.5
    ki = lax.broadcasted_iota(jnp.int32, (128, 128), 0)
    qi = lax.broadcasted_iota(jnp.int32, (128, 128), 1)
    r.mask[...] = jnp.where(ki <= qi, 0.0, MASKED)

    def prompt(p, _):
        count = counts[p]
        pltpu.make_async_copy(emb_far, r.io, r.sem_e).wait()
        r.embT[...] = r.io[...].T

        @pl.when(p + 1 < nprompts)
        def _():
            load(p + 1, emb, emb_far, r.io, r.sem_e)

        r.cur[...] = jnp.zeros_like(r.cur)

        def forward(j):
            r.cur[...] = r.cur[...] + r.embT[...]

            def fl(l, _):
                layer_fwd(r, l, lax.rem(j, S) * 2 + l, T, D)
                return 0

            lax.fori_loop(0, 2, fl, 0)

        def floop(j, _):
            if redo:
                r.hs[j] = r.cur[...]
            forward(j)
            return 0

        lax.fori_loop(0, count, floop, 0)
        give(p, 0, r.cur[...], r.low, r.sem)
        pltpu.make_async_copy(cot_far, r.io2, r.sem_c).wait()
        r.dcur[...] = r.io2[...].T

        @pl.when(p + 1 < nprompts)
        def _():
            load(p + 1, cot, cot_far, r.io2, r.sem_c)

        r.gsum[...] = jnp.zeros_like(r.gsum)

        def bloop(jj, _):
            j = count - 1 - jj
            if redo:

                @pl.when(jj >= S)
                def _():
                    r.cur[...] = r.hs[j]
                    forward(j)

            def bl(ll, _):
                l = 1 - ll
                layer_bwd(r, l, lax.rem(j, S) * 2 + l, T, D)
                return 0

            lax.fori_loop(0, 2, bl, 0)
            r.gsum[...] = r.gsum[...] + r.dcur[...]
            return 0

        lax.fori_loop(0, count, bloop, 0)
        give(p, 1, r.gsum[...], r.low2, r.sem2)
        return 0

    lax.fori_loop(0, nprompts, prompt, 0)
    for which, low, sem in ((0, r.low, r.sem), (1, r.low2, r.sem2)):
        for i in range(N):
            pltpu.make_async_copy(low.at[pl.ds(C * i, C), :], fe.at[nprompts - 1, i, which], sem).wait()
    parts, Z, span, _ = keep.shape
    half = parts * Z * span // 128
    outs = []

    def put(src, dst, sem):
        for row in range(0, 128 * half, 64):
            o, w = row // (parts * span), row % (parts * span)
            at = dst.at[w // span, o, pl.ds(w % span, 64), :]
            outs.append(pltpu.make_async_copy(src(row), at, sem))
            outs[-1].start()

    put(lambda row: r.acc.at[row // 128, pl.ds(row % 128, 64), :], keep, r.sem)
    per = r.es.shape[2] // 128
    for t in range(half):
        r.es[0, t // per, t % per * 128 : t % per * 128 + 128, :] = r.acc[half + t].astype(BF16)
    put(lambda row: r.es.at[0, row // (128 * per), pl.ds(row % (128 * per), 64), :], send, r.sem2)
    for k in range(18):
        if 4 <= k % 9 < 8:
            sgo[k : k + 1, :] = r.sgb[k // 9, k % 9 - 4 : k % 9 - 3, :]
        else:
            part = r.sg[k // 9, k % 9 * D : k % 9 * D + D, :].T
            sgo[k : k + 1, :] = jnp.sum(part, axis=0, keepdims=True)
    for cp in outs:
        cp.wait()


def call(N, parts, OWN, counts, place, dst, rows, far, emb, cot, emb_far, cot_far, pbr, pieces):
    S = N if N <= 4 else 2
    n = counts.shape[0]
    _, T, D = emb.shape
    V = pltpu.VMEM
    H = 4 * D
    scr = [
        V((2, 9 * D, 128), F32), V((2, 3 * D, D), BF16), V((2, D, D), BF16), V((2, H, D), BF16), V((2, D, H), BF16),
        V((2, D, 3 * D), BF16), V((2, D, D), BF16), V((2, D, H), BF16), V((2, H, D), BF16),
        V((128, 128), F32),
        V((D, T), F32), V((D, T), F32), V((D, T), F32), V((D, T), F32), V((T, D), F32),
        V((D, T), BF16), V((D + 16, T), BF16), V((D, T), F32), V((H, T), BF16),
        V((D, T), BF16), V((D, T), BF16), V((D, T), BF16), V((3 * D, T), BF16),
        V((2 * S, D, T), F32), V((2 * S, 3 * D, T), BF16),
        V((2 * S, HEADS, T * (T // 256 + 1) // 2, 256), BF16), V((2 * S, HEADS, T), F32), V((2 * S, D, T), BF16),
        V((2, 9 * D, 128), F32), V((T, D), BF16), V((48, 128, D), F32),
        V((T, D), F32), V((T, D), BF16), V((2, 8, D), F32), V((2 * S, 8, T), F32),
        pltpu.SemaphoreType.DMA, pltpu.SemaphoreType.DMA, pltpu.SemaphoreType.DMA, pltpu.SemaphoreType.DMA,
    ]
    if N > S:
        scr.append(V((N, D, T), F32))
    half = (parts, 24 // OWN, OWN * 128 // parts, D)
    A = pl.BlockSpec(memory_space=pl.ANY)
    VM = pl.BlockSpec(memory_space=pltpu.VMEM)
    SM = pl.BlockSpec(memory_space=pltpu.SMEM)
    return pl.pallas_call(
        functools.partial(kernel, S, N, n, len(pieces)),
        out_shape=(
            jax.ShapeDtypeStruct((n, N, 2, T // N, D), BF16),
            jax.ShapeDtypeStruct(half, F32), jax.ShapeDtypeStruct(half, BF16),
            jax.ShapeDtypeStruct((18, D), F32)),
        in_specs=[SM] * 5 + [A] * 4 + [VM] + [A] * len(pieces),
        out_specs=(A, A, A, VM),
        scratch_shapes=scr,
        compiler_params=pltpu.CompilerParams(vmem_limit_bytes=63 * 1024 * 1024),
    )(counts, place, dst, rows, far, emb, cot, emb_far, cot_far, pbr, *pieces)


STEP = 10
beta_one = 0.9
beta_two = 0.999
learn_rate = 0.05
small_rate = 0.3
weight_decay = 0.1
adam_eps = 1e-08


def adam_update(gradient, first_old, second_old, weight, decay_rate, rate):
    first_new = beta_one * first_old + (1.0 - beta_one) * gradient
    second_new = beta_two * second_old + (1.0 - beta_two) * gradient * gradient
    corr_one = 1.0 - beta_one**STEP
    corr_two = 1.0 - beta_two**STEP
    update = first_new / corr_one / (jnp.sqrt(second_new / corr_two) + adam_eps)
    return (first_new, second_new, weight - rate * (update + decay_rate * weight))


def ranks(key, falling):
    n = key.shape[0]
    i = jnp.arange(n)
    ahead = (key[None, :] > key[:, None]) if falling else (key[None, :] < key[:, None])
    tie = (key[None, :] == key[:, None]) & (i[None, :] < i[:, None])
    return jnp.sum((ahead | tie).astype(jnp.int32), axis=1)


def swap(v, axis, k):
    n = lax.axis_size(axis)
    return lax.ppermute(v, axis, [(i, i ^ k) for i in range(n)])


def pick(v, i, axis):
    return lax.dynamic_index_in_dim(v, i, axis, keepdims=False)


def gather_tiles(own, N, Z, s):
    OWN, H, D = own.shape
    R = OWN * H // N
    part = pick(own.reshape(N, R, D), s, 0).astype(BF16)
    zs = jnp.stack([part] + [swap(part, "dp", 2 * k) for k in range(1, Z)])
    near = [zs] + [swap(zs, "section", k) for k in range(1, N)]
    pieces = near + [swap(v, "dp", 1) for v in near]
    where = [(cc, zz, k, h) for cc in (0, 1) for k in range(N) for zz in range(Z) for h in range(R // 64)]
    return [v.reshape(-1, 64, D) for v in pieces], where, near[1]


def tree(v):
    return v[0] if len(v) == 1 else tree([v[i] + v[i + 1] for i in range(0, len(v), 2)])


def reduce_all(keep, send, small, N, Z, s, z):
    if keep.shape[0] != N:
        keep, send = (v.reshape(Z, N, -1, v.shape[-1]).swapaxes(0, 1) for v in (keep, send))
    _, _, R, D = keep.shape
    n = small.shape[0]
    small = small + swap(small, "dp", 1)
    low = jnp.concatenate([small, jnp.zeros((-n % 8, D), F32)]).astype(BF16)
    ks = list(range(1, N)) + [0]
    got = {k: swap(pick(send, s ^ k, 0), "dp", 1) for k in ks}
    both = {k: (pick(keep, s ^ k, 0) + got[k].astype(F32)).reshape(Z * R, D) for k in ks}
    far = [swap(jnp.concatenate([both[k].astype(BF16), low]), "section", k) for k in range(1, N)]
    part = functools.reduce(lambda x, v: x + v[: Z * R].astype(F32), far, both[0]).reshape(Z, R, D)
    low = tree([low.astype(F32)] + [v[Z * R :].astype(F32) for v in far]).astype(BF16)
    far = [swap(jnp.concatenate([pick(part, z ^ k, 0).astype(BF16), low]), "dp", 2 * k) for k in range(1, Z)]
    done = functools.reduce(lambda x, v: x + v[:R].astype(F32), far, pick(part, z, 0)).astype(BF16)
    low = tree([low.astype(F32)] + [v[R:].astype(F32) for v in far])
    every = jnp.stack([done] + [swap(done, "section", k) for k in range(1, N)])
    return jnp.concatenate([pick(every, s ^ j, 0) for j in range(N)], axis=0).astype(F32), low[:n], part


def order_kernel(N, slots, at, *refs):
    ins, fin, eg = refs[:-2], refs[-2], refs[-1]

    def put(p, _):
        w = at[p]
        for k in range(N):
            for j in range(slots):

                @pl.when(w == k * slots + j)
                def _():
                    fin[p] = ins[k * slots + j][0].astype(F32)
                    eg[p] = ins[k * slots + j][1].astype(F32)

        return 0

    lax.fori_loop(0, fin.shape[0], put, 0)


def in_order(pieces, slots, at, prompts):
    _, C, D = pieces[0].shape
    N = len(pieces) // slots
    VM = pl.BlockSpec(memory_space=pltpu.VMEM)
    out = jax.ShapeDtypeStruct((prompts, C, D), F32)
    return pl.pallas_call(
        functools.partial(order_kernel, N, slots),
        out_shape=(out, out),
        in_specs=[pl.BlockSpec(memory_space=pltpu.SMEM)] + [VM] * len(pieces),
        out_specs=(VM, VM),
        compiler_params=pltpu.CompilerParams(vmem_limit_bytes=32 * 1024 * 1024),
    )(at, *pieces)


def plain_jobs(owner_list, counts, N, Z, OWN, s, c):
    PR = counts.shape[0]
    jobs = R()
    pos = ranks(owner_list, False)
    owner, slot = pos // OWN, pos % OWN
    jobs.place = ((owner % 2) ^ c) * (Z * OWN) + owner // 2 * OWN + slot
    tiles = jnp.arange(pos.shape[0])
    order = jnp.sum(jnp.where(tiles[:, None] == pos[None, :], tiles[None, :], 0), axis=1)
    jobs.dst = (2 * order[:, None] + jnp.arange(2)[None, :]).reshape(-1)
    rank = ranks(counts, True)
    slots = -(-PR // N)
    j = jnp.arange(slots)
    want = j * N + jnp.where(j % 2 == 0, s, N - 1 - s)
    hit = want[:, None] == rank[None, :]
    jobs.rows = jnp.sum(jnp.where(hit, jnp.arange(PR)[None, :], 0), axis=1).astype(jnp.int32)
    jobs.counts = jnp.sum(jnp.where(hit, counts[None, :], 0), axis=1).astype(jnp.int32)
    jobs.far = jnp.zeros((slots,), jnp.int32)
    k = rank // N
    w = jnp.where(k % 2 == 0, rank % N, N - 1 - rank % N)
    jobs.at = (w ^ s) * slots + k
    return jobs


def plan_kernel(N, Z, OWN, where, owner, mine, theirs, ids, place, dst, rows, cnts, far, at, order, used, srt, prm):
    s, z, c = ids[0], ids[1], ids[2]
    PR = 2 * N
    for o in range(2 * Z):
        used[o] = 0
    for t in range(place.shape[0]):
        o = owner[t]
        i = used[o]
        used[o] = i + 1
        order[o * OWN + i] = t
        place[t] = ((o & 1) ^ c) * (Z * OWN) + (o >> 1) * OWN + i
    for i, (cc, zz, k, h) in enumerate(where):
        half = (s ^ k) * (2 * OWN // N) + h
        dst[i] = 2 * order[((z ^ zz) * 2 + (c ^ cc)) * OWN + (half >> 1)] + (half & 1)

    def ranked(ref, base, keep):
        v = [ref[i] for i in range(PR)]
        got = []
        for i in range(PR):
            r = 0
            for j in range(PR):
                if j != i:
                    r = r + jnp.where(v[j] >= v[i] if j < i else v[j] > v[i], 1, 0)
            srt[base + r] = v[i]
            if keep:
                srt[2 * PR + r] = i
            got.append(r)
        return got

    rank = ranked(mine, c * PR, True)
    ranked(theirs, (1 - c) * PR, False)
    a = [srt[i] for i in range(PR)]
    b = [srt[PR + i] for i in range(PR)]
    kept, traded = {}, {}
    for i in range(N):
        for j in range(N):
            kept[i, j] = jnp.maximum(a[i] + a[PR - 1 - i], b[j] + b[PR - 1 - j])
            traded[i, j] = jnp.maximum(a[i] + b[PR - 1 - j], b[j] + a[PR - 1 - i])
    best = None
    for p in itertools.permutations(range(N)):
        worst = functools.reduce(jnp.maximum, [jnp.minimum(kept[i, p[i]], traded[i, p[i]]) for i in range(N)])
        if best is None:
            best, perm = worst, [jnp.int32(v) for v in p]
        else:
            less = worst < best
            best = jnp.where(less, worst, best)
            perm = [jnp.where(less, jnp.int32(v), u) for u, v in zip(perm, p)]
    for i in range(N):
        prm[i] = perm[i]
        prm[N + perm[i]] = i
    trade = jnp.int32(0)
    for i in range(N):
        for j in range(N):
            cell = (s == i) & (prm[i] == j)
            trade = jnp.where(cell & (traded[i, j] < kept[i, j]), 1, trade)
    pair = jnp.where(c == 0, s, prm[s])
    other = jnp.where(c == 0, prm[s], s)
    rows[0] = srt[2 * PR + pair]
    rows[1] = srt[2 * PR + PR - 1 - pair]
    far[0] = 0
    far[1] = trade
    cnts[0] = srt[c * PR + pair]
    cnts[1] = srt[jnp.where(trade != 0, (1 - c) * PR + PR - 1 - other, c * PR + PR - 1 - pair)]
    for p in range(PR):
        low = rank[p] >= N
        j = jnp.where(low, PR - 1 - rank[p], rank[p])
        w = jnp.where(c == 0, j, prm[N + j])
        at[p] = (w ^ s) * 2 + jnp.where(low, 1, 0)


def plan(owner_list, mine, theirs, ids, where, N, Z, OWN):
    SM = pl.BlockSpec(memory_space=pltpu.SMEM)
    tiles, PR = owner_list.shape[0], mine.shape[0]
    sizes = (tiles, 2 * tiles, 2, 2, 2, PR)
    jobs = R()
    jobs.place, jobs.dst, jobs.rows, jobs.counts, jobs.far, jobs.at = pl.pallas_call(
        functools.partial(plan_kernel, N, Z, OWN, where),
        out_shape=[jax.ShapeDtypeStruct((n,), jnp.int32) for n in sizes],
        in_specs=[SM] * 4,
        out_specs=[SM] * 6,
        scratch_shapes=[pltpu.SMEM((n,), jnp.int32) for n in (tiles, 2 * Z, 3 * PR, 2 * N)],
    )(owner_list, mine, theirs, ids)
    return jobs


def shards(embedding, cotangent, counts, owner_list, tiles_owned, first_owned, second_owned,
           small_params, small_first, small_second):
    N, DP = lax.axis_size("section"), lax.axis_size("dp")
    Z = DP // 2
    s, dp = lax.axis_index("section"), lax.axis_index("dp")
    z, c = dp // 2, dp % 2
    PR, T, D = embedding.shape
    OWN, H, _ = tiles_owned.shape
    shared = PR == 2 * N and OWN * H % (64 * N) == 0
    if shared:
        pieces, where, early = gather_tiles(tiles_owned, N, Z, s)
        jobs = plan(owner_list, counts, swap(counts, "dp", 1), jnp.stack([s, z, c]), where, N, Z, OWN)
        row, _ = lax.optimization_barrier((jobs.rows[1], early))
        emb_far, cot_far = (swap(pick(v, row, 0), "dp", 1) for v in (embedding, cotangent))
    else:
        pieces = [lax.all_gather(tiles_owned.astype(BF16), "dp", axis=0, tiled=True).reshape(-1, 64, D)]
        jobs = plain_jobs(owner_list, counts, N, Z, OWN, s, c)
        emb_far, cot_far = embedding[0], cotangent[0]
    fe, keep, send, sg = call(N, N if shared else 1, OWN, jobs.counts, jobs.place, jobs.dst, jobs.rows, jobs.far, embedding, cotangent,
                              emb_far, cot_far, small_params, pieces)
    slots = [fe[j] for j in range(fe.shape[0])]
    tile_grad, small_grad, halfway = reduce_all(keep, send, sg, N, Z, s, z)
    tile_grad = tile_grad.reshape(OWN, H, D)
    if shared:
        other = swap(slots[1], "dp", 1)
        mine = jnp.where(jobs.far[1] != 0, other, slots[1])
        slots[1] = mine
    done = [pick(v, s, 0) for v in slots]
    for k in range(1, N):
        done += [swap(pick(v, s ^ k, 0), "section", k) for v in slots]
    fin, eg = in_order(done, len(slots), jobs.at, PR)
    tile_first, tile_second, tile_new = adam_update(
        tile_grad, first_owned, second_owned, tiles_owned, weight_decay, learn_rate
    )
    small_first_new, small_second_new, small_new = adam_update(
        small_grad, small_first, small_second, small_params, 0.0, small_rate
    )
    return (fin, eg, tile_grad, tile_first, tile_second, tile_new,
            small_grad, small_first_new, small_second_new, small_new)


def solution(mesh):
    P = jax.sharding.PartitionSpec
    own, rep = P("dp", None, None), P()
    return jax.shard_map(
        shards,
        mesh=mesh,
        in_specs=(own, own, P("dp"), rep, own, own, own, rep, rep, rep),
        out_specs=(P("dp", "section", None),) * 2 + (own,) * 4 + (rep,) * 4,
        check_vma=False,
    )
```

```python
import functools
import itertools
import math

import jax
import jax.numpy as jnp
from jax import lax
from jax.experimental import pallas as pl
from jax.experimental.pallas import tpu as pltpu

F32, BF16 = jnp.float32, jnp.bfloat16
HEADS = 8
EPS = 1e-5
MASKED = -1e30
GC0 = math.sqrt(2.0 / math.pi)
GC1 = 0.044715


def nn(a, b):
    return lax.dot_general(a, b, (((1,), (0,)), ((), ())), preferred_element_type=F32)


def nt(a, b):
    return lax.dot_general(a, b, (((1,), (1,)), ((), ())), preferred_element_type=F32)


def tn(a, b):
    return lax.dot_general(a, b, (((0,), (0,)), ((), ())), preferred_element_type=F32)


def wide(col, n):
    return jnp.concatenate([col] * (n // 128), axis=1)


def fold(a):
    r = a[:, 0:128]
    for i in range(1, a.shape[1] // 128):
        r = r + a[:, 128 * i : 128 * i + 128]
    return r


def normed(x):
    d = x.shape[0]
    mean = jnp.sum(x, axis=0, keepdims=True) * (1.0 / d)
    xc = x - mean
    var = jnp.sum(xc * xc, axis=0, keepdims=True) * (1.0 / d)
    rstd = lax.rsqrt(var + EPS)
    return xc * rstd, mean, rstd


def norm_back(dn, xhat, rstd, gain):
    d = dn.shape[0]
    dx = dn * gain
    a = jnp.sum(dx, axis=0, keepdims=True) * (1.0 / d)
    b = jnp.sum(dx * xhat, axis=0, keepdims=True) * (1.0 / d)
    return rstd * (dx - a - xhat * b)


def staged(jobs, *stages):
    state = [{} for _ in jobs]
    low = min(k for _, k in stages)
    high = max(k for _, k in stages)
    for i in range(-high, len(jobs) - low):
        for f, k in stages:
            if 0 <= i + k < len(jobs):
                f(state[i + k], *jobs[i + k])


class R:
    pass


def layer_fwd(r, l, sl, T, D):
    hd = D // HEADS
    pr = lambda k, n=1: r.pb[l, pl.ds(k * D, n * D), :]
    x = r.cur[...]
    r.xs[sl] = x
    xhat, r.stats[sl, 0:1, :], r.stats[sl, 1:2, :] = normed(x)
    r.n1[...] = (xhat * wide(pr(0), T) + wide(pr(1), T)).astype(BF16)
    c2 = hd**-0.5 * math.log2(math.e)
    for i in range(3):
        v = nn(r.wt_qkv[l, pl.ds(i * D, D), :], r.n1[...])
        r.qkv[sl, pl.ds(i * D, D), :] = (v * c2 if i == 0 else v).astype(BF16)
    ones16 = jnp.ones((16, T), BF16)
    jobs = [(h, b) for h in range(HEADS) for b in range(T // 256)]

    def scores(d, h, b):
        kk = 256 * (b + 1)
        k = r.qkv[sl, pl.ds(D + h * hd, hd), pl.ds(0, kk)]
        d[0] = tn(k, r.qkv[sl, pl.ds(h * hd, hd), pl.ds(256 * b, 256)])

    def probs(d, h, b):
        s = d.pop(0)
        kk = 256 * (b + 1)
        halves = []
        for i in range(2):
            part = s[:, 128 * i : 128 * i + 128]
            near = kk - 256 + 128 * i
            seen = [part[:near, :]] if near else []
            seen.append(part[near : near + 128, :] + r.mask[...])
            mx = functools.reduce(jnp.maximum, [jnp.max(v, axis=0, keepdims=True) for v in seen])
            e = [jnp.exp2(v - mx).astype(BF16) for v in seen]
            if i == 0:
                e.append(jnp.zeros((128, 128), BF16))
            halves.append(jnp.concatenate(e, axis=0))
        e = jnp.concatenate(halves, axis=1)
        r.es[sl, h, pl.ds(128 * b * (b + 1), kk), :] = e
        d[1] = e

    def context(d, h, b):
        e = d.pop(1)
        kk = 256 * (b + 1)
        v = r.qkv[sl, pl.ds(2 * D + h * hd, hd), pl.ds(0, kk)]
        o = nn(jnp.concatenate([v, ones16[:, :kk]], axis=0), e)
        linv = 1.0 / o[hd : hd + 1, :]
        r.linv[sl, pl.ds(h, 1), pl.ds(256 * b, 256)] = linv
        r.ctx[sl, pl.ds(h * hd, hd), pl.ds(256 * b, 256)] = (o[:hd, :] * linv).astype(BF16)

    staged(jobs, (scores, 3), (probs, 0), (context, -2))
    m = r.xs[sl] + nn(r.wt_o[l], r.ctx[sl])
    r.cur[...] = m
    mhat, r.stats[sl, 2:3, :], r.stats[sl, 3:4, :] = normed(m)
    r.n2[:D, :] = (mhat * wide(pr(2), T) + wide(pr(3), T)).astype(BF16)
    r.cur[...] = r.cur[...] + wide(pr(8), T)

    def up(d, i):
        d[0] = nn(r.wt_up[l, pl.ds(i * D, D), :], r.n2[:D, :]) + wide(pr(4 + i), T)

    def act(d, i):
        h = d.pop(0)
        t1 = 1.0 + jnp.tanh(h * (2 * GC0 + (8 * GC0 * GC1) * (h * h)))
        d[1] = (h * t1).astype(BF16)

    def down(d, i):
        r.cur[...] = r.cur[...] + nn(r.wt_down[l, :, pl.ds(i * D, D)], d.pop(1))

    staged([(i,) for i in range(4)], (up, 1), (act, 0), (down, -1))


def layer_bwd(r, l, sl, T, D):
    hd = D // HEADS
    c = hd**-0.5
    pr = lambda k, n=1: r.pb[l, pl.ds(k * D, n * D), :]

    def add_small(k, v):
        r.sg[l, pl.ds(k * D, D), :] = r.sg[l, pl.ds(k * D, D), :] + fold(v)

    dy = r.dcur[...]
    r.dylow[...] = dy.astype(BF16)
    add_small(8, dy)
    rstd2 = r.stats[sl, 3:4, :]
    mhat = (r.xs[sl] + nn(r.wt_o[l], r.ctx[sl]) - r.stats[sl, 2:3, :]) * rstd2
    r.hat[...] = mhat
    r.n2[:D, :] = (mhat * wide(pr(2), T) + wide(pr(3), T)).astype(BF16)

    def add_tiles(t, v, gap=1):
        for a in range(2):
            at = r.place[24 * l + t + gap * a]
            r.acc[at] = r.acc[at] + v[128 * a : 128 * a + 128]

    def up(d, i):
        h = nn(r.wt_up[l, pl.ds(i * D, D), :], r.n2[:D, :]) + wide(pr(4 + i), T)
        d[0] = h, nn(r.w_down[l, pl.ds(i * D, D), :], r.dylow[...])

    def act(d, i):
        h, dg = d.pop(0)
        h2 = h * h
        t1 = 1.0 + jnp.tanh(h * (2 * GC0 + (8 * GC0 * GC1) * h2))
        g = h * t1
        du = dg * (t1 + g * (2.0 - t1) * (2 * GC0 + (24 * GC0 * GC1) * h2))
        g, du = g.astype(BF16), du.astype(BF16)
        r.du[pl.ds(i * D, D), :] = du
        d[1] = g, du

    def grads(d, i):
        g, du = d.pop(1)
        add_tiles(16 + 2 * i, nt(g, r.dylow[...]))
        v = nt(r.n2[...], du)
        add_tiles(8 + i, v, 4)
        r.sgb[l, i : i + 1, :] = r.sgb[l, i : i + 1, :] + v[D : D + 1]

    staged([(i,) for i in range(4)], (up, 0), (act, 0), (grads, -1))
    dn2 = nn(r.w_up[l], r.du[...])
    add_small(2, dn2 * r.hat[...])
    add_small(3, dn2)
    dm = r.dcur[...] + norm_back(dn2, r.hat[...], rstd2, wide(pr(2), T))
    r.dcur[...] = dm
    r.dmlow[...] = dm.astype(BF16)

    add_tiles(6, nt(r.ctx[sl], r.dmlow[...]))
    dctx = nn(r.w_o[l], r.dmlow[...])
    for h in range(HEADS):
        hs = slice(h * hd, h * hd + hd)
        r.dctx[hs, :] = (dctx[hs, :] * (r.linv[sl, pl.ds(h, 1), :] * c)).astype(BF16)
    c2 = hd**-0.5 * math.log2(math.e)
    nb = T // 256
    row = lax.broadcasted_iota(jnp.int32, (16, T), 0)
    ones3 = jnp.where(row < 3, 1.0, 0.0).astype(BF16)
    blk = lambda j: slice(256 * j, 256 * j + 256)

    def back_probs(d, h):
        dctx = r.dctx[pl.ds(h * hd, hd), :]
        ctx = r.ctx[sl, pl.ds(h * hd, hd), :].astype(F32)
        nd = -jnp.sum(dctx.astype(F32) * ctx, axis=0, keepdims=True)
        n0 = nd.astype(BF16).astype(F32)
        n1 = (nd - n0).astype(BF16).astype(F32)
        n2 = nd - n0 - n1
        extra = jnp.where(row == 0, n0, jnp.where(row == 1, n1, jnp.where(row == 2, n2, 0.0))).astype(BF16)
        de = jnp.concatenate([dctx, extra], axis=0)
        ve = jnp.concatenate([r.qkv[sl, pl.ds(2 * D + h * hd, hd), :], ones3], axis=0)
        d["dsr"] = [tn(ve[:, : 256 * (b + 1)], de[:, blk(b)]) for b in range(nb)]

    def probs_of(h, b):
        return r.es[sl, h, pl.ds(128 * b * (b + 1), 256 * (b + 1)), :]

    def back_scores(d, h):
        dsr = d.pop("dsr")
        d["ds"] = [(probs_of(h, b).astype(F32) * dsr[b]).astype(BF16) for b in range(nb)]

    def by_key(parts, j):
        return jnp.concatenate([parts[b][blk(j)] for b in range(j, nb)], axis=1)

    def back_v(d, h):
        e = [probs_of(h, b) for b in range(nb)]
        for j in range(nb):
            dv = nt(r.dctx[pl.ds(h * hd, hd), pl.ds(256 * j, T - 256 * j)], by_key(e, j))
            r.dqkv[pl.ds(2 * D + h * hd, hd), pl.ds(256 * j, 256)] = (dv * (1.0 / c)).astype(BF16)

    def back_k(d, h):
        ds = d["ds"]
        for j in range(nb):
            dk = nt(r.qkv[sl, pl.ds(h * hd, hd), pl.ds(256 * j, T - 256 * j)], by_key(ds, j))
            r.dqkv[pl.ds(D + h * hd, hd), pl.ds(256 * j, 256)] = (dk * (1.0 / c2)).astype(BF16)

    def back_q(d, h):
        ds = d["ds"]
        for b in range(nb):
            k = r.qkv[sl, pl.ds(D + h * hd, hd), pl.ds(0, 256 * (b + 1))]
            r.dqkv[pl.ds(h * hd, hd), pl.ds(256 * b, 256)] = nn(k, ds[b]).astype(BF16)

    staged([(h,) for h in range(HEADS)], (back_probs, 1), (back_v, 1), (back_scores, 0), (back_q, -1), (back_k, -1))
    rstd1 = r.stats[sl, 1:2, :]
    xhat = (r.xs[sl] - r.stats[sl, 0:1, :]) * rstd1
    r.hat[...] = xhat
    r.n1[...] = (xhat * wide(pr(0), T) + wide(pr(1), T)).astype(BF16)
    for i in range(3):
        add_tiles(2 * i, nt(r.n1[...], r.dqkv[pl.ds(i * D, D), :]))
    dn1 = nn(r.w_qkv[l], r.dqkv[...])
    add_small(0, dn1 * r.hat[...])
    add_small(1, dn1)
    r.dcur[...] = r.dcur[...] + norm_back(dn1, r.hat[...], rstd1, wide(pr(0), T))


def kernel(S, N, nprompts, npieces, counts, place, dst, rows, far, emb, cot, emb_far, cot_far, pbr, *refs):
    pieces = refs[:npieces]
    fe, keep, send, sgo = refs[npieces : npieces + 4]
    scr = refs[npieces + 4 :]
    r = R()
    (r.pb, r.wt_qkv, r.wt_o, r.wt_up, r.wt_down, r.w_qkv, r.w_o, r.w_up, r.w_down, r.mask,
     r.cur, r.dcur, r.embT, r.gsum, r.io, r.n1, r.n2, r.hat, r.du, r.dylow, r.dmlow, r.dctx, r.dqkv,
     r.xs, r.qkv, r.es, r.linv, r.ctx, r.sg, r.low, r.acc, r.io2, r.low2, r.sgb, r.stats,
     r.sem, r.sem2, r.sem_e, r.sem_c) = scr[:39]
    redo = N > S
    if redo:
        r.hs = scr[39]
    r.place = place
    T, D = r.io.shape
    C = T // N

    def load(p, near_ref, far_ref, to, sem):
        @pl.when(far[p] == 0)
        def _():
            pltpu.make_async_copy(near_ref.at[rows[p]], to, sem).start()

        @pl.when(far[p] != 0)
        def _():
            pltpu.make_async_copy(far_ref, to, sem).start()

    load(0, emb, emb_far, r.io, r.sem_e)
    load(0, cot, cot_far, r.io2, r.sem_c)

    def give(p, which, v, low, sem):
        cps = [pltpu.make_async_copy(low.at[pl.ds(C * i, C), :], fe.at[p, i, which], sem) for i in range(N)]

        @pl.when(p > 0)
        def _():
            for cp in cps:
                cp.wait()

        low[...] = v.T.astype(BF16)
        for cp in cps:
            cp.start()

    def spot(t):
        per = r.es.shape[2] // 64
        return r.es.at[0, t // per, pl.ds(pl.multiple_of(t % per * 64, 64), 64), :]

    cps = []
    for piece in pieces:
        for i in range(piece.shape[0]):
            cps.append(pltpu.make_async_copy(piece.at[i], spot(dst[len(cps)]), r.sem))
    for cp in cps:
        cp.start()
    r.acc[...] = jnp.zeros_like(r.acc)
    r.sg[...] = jnp.zeros_like(r.sg)
    r.sgb[...] = jnp.zeros_like(r.sgb)
    r.n2[D:, :] = jnp.where(lax.broadcasted_iota(jnp.int32, (16, T), 0) == 0, 1.0, 0.0).astype(BF16)
    for k in range(18):
        half = 0.5 if 4 <= k % 9 < 8 else 1.0
        r.pb[k // 9, k % 9 * D : k % 9 * D + D, :] = jnp.broadcast_to(pbr[k : k + 1, :] * half, (128, D)).T
    for cp in cps:
        cp.wait()
    for l in range(2):
        for t in range(24):
            per = r.es.shape[2] // 128
            u = 24 * l + t
            w = r.es[0, u // per, u % per * 128 : u % per * 128 + 128, :]
            if t < 6:
                r.w_qkv[l, t % 2 * 128 : t % 2 * 128 + 128, t // 2 * D : t // 2 * D + D] = w
            elif t < 8:
                r.w_o[l, (t - 6) * 128 : (t - 5) * 128, :] = w
            elif t < 16:
                o, b = (t - 8) // 4 * 128, (t - 8) % 4 * D
                r.w_up[l, o : o + 128, b : b + D] = w
            else:
                r.w_down[l, (t - 16) * 128 : (t - 15) * 128, :] = w
        for natural, turned in ((r.w_qkv, r.wt_qkv), (r.w_o, r.wt_o), (r.w_up, r.wt_up), (r.w_down, r.wt_down)):
            turned[l] = natural[l].T
        r.wt_up[l] = r.wt_up[l] * 0.5
        r.w_down[l] = r.w_down[l] * 0.5
    ki = lax.broadcasted_iota(jnp.int32, (128, 128), 0)
    qi = lax.broadcasted_iota(jnp.int32, (128, 128), 1)
    r.mask[...] = jnp.where(ki <= qi, 0.0, MASKED)

    def prompt(p, _):
        count = counts[p]
        pltpu.make_async_copy(emb_far, r.io, r.sem_e).wait()
        r.embT[...] = r.io[...].T

        @pl.when(p + 1 < nprompts)
        def _():
            load(p + 1, emb, emb_far, r.io, r.sem_e)

        r.cur[...] = jnp.zeros_like(r.cur)

        def forward(j):
            r.cur[...] = r.cur[...] + r.embT[...]

            def fl(l, _):
                layer_fwd(r, l, lax.rem(j, S) * 2 + l, T, D)
                return 0

            lax.fori_loop(0, 2, fl, 0)

        def floop(j, _):
            if redo:
                r.hs[j] = r.cur[...]
            forward(j)
            return 0

        lax.fori_loop(0, count, floop, 0)
        give(p, 0, r.cur[...], r.low, r.sem)
        pltpu.make_async_copy(cot_far, r.io2, r.sem_c).wait()
        r.dcur[...] = r.io2[...].T

        @pl.when(p + 1 < nprompts)
        def _():
            load(p + 1, cot, cot_far, r.io2, r.sem_c)

        r.gsum[...] = jnp.zeros_like(r.gsum)

        def bloop(jj, _):
            j = count - 1 - jj
            if redo:

                @pl.when(jj >= S)
                def _():
                    r.cur[...] = r.hs[j]
                    forward(j)

            def bl(ll, _):
                l = 1 - ll
                layer_bwd(r, l, lax.rem(j, S) * 2 + l, T, D)
                return 0

            lax.fori_loop(0, 2, bl, 0)
            r.gsum[...] = r.gsum[...] + r.dcur[...]
            return 0

        lax.fori_loop(0, count, bloop, 0)
        give(p, 1, r.gsum[...], r.low2, r.sem2)
        return 0

    lax.fori_loop(0, nprompts, prompt, 0)
    for which, low, sem in ((0, r.low, r.sem), (1, r.low2, r.sem2)):
        for i in range(N):
            pltpu.make_async_copy(low.at[pl.ds(C * i, C), :], fe.at[nprompts - 1, i, which], sem).wait()
    parts, Z, span, _ = keep.shape
    half = parts * Z * span // 128
    outs = []

    def put(src, dst, sem):
        for row in range(0, 128 * half, 64):
            o, w = row // (parts * span), row % (parts * span)
            at = dst.at[w // span, o, pl.ds(w % span, 64), :]
            outs.append(pltpu.make_async_copy(src(row), at, sem))
            outs[-1].start()

    put(lambda row: r.acc.at[row // 128, pl.ds(row % 128, 64), :], keep, r.sem)
    per = r.es.shape[2] // 128
    for t in range(half):
        r.es[0, t // per, t % per * 128 : t % per * 128 + 128, :] = r.acc[half + t].astype(BF16)
    put(lambda row: r.es.at[0, row // (128 * per), pl.ds(row % (128 * per), 64), :], send, r.sem2)
    for k in range(18):
        if 4 <= k % 9 < 8:
            sgo[k : k + 1, :] = r.sgb[k // 9, k % 9 - 4 : k % 9 - 3, :]
        else:
            part = r.sg[k // 9, k % 9 * D : k % 9 * D + D, :].T
            sgo[k : k + 1, :] = jnp.sum(part, axis=0, keepdims=True)
    for cp in outs:
        cp.wait()


def call(N, parts, OWN, counts, place, dst, rows, far, emb, cot, emb_far, cot_far, pbr, pieces):
    S = N if N <= 4 else 2
    n = counts.shape[0]
    _, T, D = emb.shape
    V = pltpu.VMEM
    H = 4 * D
    scr = [
        V((2, 9 * D, 128), F32), V((2, 3 * D, D), BF16), V((2, D, D), BF16), V((2, H, D), BF16), V((2, D, H), BF16),
        V((2, D, 3 * D), BF16), V((2, D, D), BF16), V((2, D, H), BF16), V((2, H, D), BF16),
        V((128, 128), F32),
        V((D, T), F32), V((D, T), F32), V((D, T), F32), V((D, T), F32), V((T, D), F32),
        V((D, T), BF16), V((D + 16, T), BF16), V((D, T), F32), V((H, T), BF16),
        V((D, T), BF16), V((D, T), BF16), V((D, T), BF16), V((3 * D, T), BF16),
        V((2 * S, D, T), F32), V((2 * S, 3 * D, T), BF16),
        V((2 * S, HEADS, T * (T // 256 + 1) // 2, 256), BF16), V((2 * S, HEADS, T), F32), V((2 * S, D, T), BF16),
        V((2, 9 * D, 128), F32), V((T, D), BF16), V((48, 128, D), F32),
        V((T, D), F32), V((T, D), BF16), V((2, 8, D), F32), V((2 * S, 8, T), F32),
        pltpu.SemaphoreType.DMA, pltpu.SemaphoreType.DMA, pltpu.SemaphoreType.DMA, pltpu.SemaphoreType.DMA,
    ]
    if N > S:
        scr.append(V((N, D, T), F32))
    half = (parts, 24 // OWN, OWN * 128 // parts, D)
    A = pl.BlockSpec(memory_space=pl.ANY)
    VM = pl.BlockSpec(memory_space=pltpu.VMEM)
    SM = pl.BlockSpec(memory_space=pltpu.SMEM)
    return pl.pallas_call(
        functools.partial(kernel, S, N, n, len(pieces)),
        out_shape=(
            jax.ShapeDtypeStruct((n, N, 2, T // N, D), BF16),
            jax.ShapeDtypeStruct(half, F32), jax.ShapeDtypeStruct(half, BF16),
            jax.ShapeDtypeStruct((18, D), F32)),
        in_specs=[SM] * 5 + [A] * 4 + [VM] + [A] * len(pieces),
        out_specs=(A, A, A, VM),
        scratch_shapes=scr,
        compiler_params=pltpu.CompilerParams(vmem_limit_bytes=63 * 1024 * 1024),
    )(counts, place, dst, rows, far, emb, cot, emb_far, cot_far, pbr, *pieces)


STEP = 10
beta_one = 0.9
beta_two = 0.999
learn_rate = 0.05
small_rate = 0.3
weight_decay = 0.1
adam_eps = 1e-08


def adam_update(gradient, first_old, second_old, weight, decay_rate, rate):
    first_new = beta_one * first_old + (1.0 - beta_one) * gradient
    second_new = beta_two * second_old + (1.0 - beta_two) * gradient * gradient
    corr_one = 1.0 - beta_one**STEP
    corr_two = 1.0 - beta_two**STEP
    update = first_new / corr_one / (jnp.sqrt(second_new / corr_two) + adam_eps)
    return (first_new, second_new, weight - rate * (update + decay_rate * weight))


def ranks(key, falling):
    n = key.shape[0]
    i = jnp.arange(n)
    ahead = (key[None, :] > key[:, None]) if falling else (key[None, :] < key[:, None])
    tie = (key[None, :] == key[:, None]) & (i[None, :] < i[:, None])
    return jnp.sum((ahead | tie).astype(jnp.int32), axis=1)


def swap(v, axis, k):
    n = lax.axis_size(axis)
    return lax.ppermute(v, axis, [(i, i ^ k) for i in range(n)])


def pick(v, i, axis):
    return lax.dynamic_index_in_dim(v, i, axis, keepdims=False)


def gather_tiles(own, N, Z, s):
    OWN, H, D = own.shape
    R = OWN * H // N
    part = pick(own.reshape(N, R, D), s, 0).astype(BF16)
    zs = jnp.stack([part] + [swap(part, "dp", 2 * k) for k in range(1, Z)])
    near = [zs] + [swap(zs, "section", k) for k in range(1, N)]
    pieces = near + [swap(v, "dp", 1) for v in near]
    where = [(cc, zz, k, h) for cc in (0, 1) for k in range(N) for zz in range(Z) for h in range(R // 64)]
    return [v.reshape(-1, 64, D) for v in pieces], where, near[1]


def tree(v):
    return v[0] if len(v) == 1 else tree([v[i] + v[i + 1] for i in range(0, len(v), 2)])


def reduce_all(keep, send, small, N, Z, s, z):
    if keep.shape[0] != N:
        keep, send = (v.reshape(Z, N, -1, v.shape[-1]).swapaxes(0, 1) for v in (keep, send))
    _, _, R, D = keep.shape
    n = small.shape[0]
    small = small + swap(small, "dp", 1)
    low = jnp.concatenate([small, jnp.zeros((-n % 8, D), F32)]).astype(BF16)
    ks = list(range(1, N)) + [0]
    got = {k: swap(pick(send, s ^ k, 0), "dp", 1) for k in ks}
    both = {k: (pick(keep, s ^ k, 0) + got[k].astype(F32)).reshape(Z * R, D) for k in ks}
    far = [swap(jnp.concatenate([both[k].astype(BF16), low]), "section", k) for k in range(1, N)]
    part = functools.reduce(lambda x, v: x + v[: Z * R].astype(F32), far, both[0]).reshape(Z, R, D)
    low = tree([low.astype(F32)] + [v[Z * R :].astype(F32) for v in far]).astype(BF16)
    far = [swap(jnp.concatenate([pick(part, z ^ k, 0).astype(BF16), low]), "dp", 2 * k) for k in range(1, Z)]
    done = functools.reduce(lambda x, v: x + v[:R].astype(F32), far, pick(part, z, 0)).astype(BF16)
    low = tree([low.astype(F32)] + [v[R:].astype(F32) for v in far])
    every = jnp.stack([done] + [swap(done, "section", k) for k in range(1, N)])
    return jnp.concatenate([pick(every, s ^ j, 0) for j in range(N)], axis=0).astype(F32), low[:n], part


def order_kernel(N, slots, at, *refs):
    ins, fin, eg = refs[:-2], refs[-2], refs[-1]

    def put(p, _):
        w = at[p]
        for k in range(N):
            for j in range(slots):

                @pl.when(w == k * slots + j)
                def _():
                    fin[p] = ins[k * slots + j][0].astype(F32)
                    eg[p] = ins[k * slots + j][1].astype(F32)

        return 0

    lax.fori_loop(0, fin.shape[0], put, 0)


def in_order(pieces, slots, at, prompts):
    _, C, D = pieces[0].shape
    N = len(pieces) // slots
    VM = pl.BlockSpec(memory_space=pltpu.VMEM)
    out = jax.ShapeDtypeStruct((prompts, C, D), F32)
    return pl.pallas_call(
        functools.partial(order_kernel, N, slots),
        out_shape=(out, out),
        in_specs=[pl.BlockSpec(memory_space=pltpu.SMEM)] + [VM] * len(pieces),
        out_specs=(VM, VM),
        compiler_params=pltpu.CompilerParams(vmem_limit_bytes=32 * 1024 * 1024),
    )(at, *pieces)


def plain_jobs(owner_list, counts, N, Z, OWN, s, c):
    PR = counts.shape[0]
    jobs = R()
    pos = ranks(owner_list, False)
    owner, slot = pos // OWN, pos % OWN
    jobs.place = ((owner % 2) ^ c) * (Z * OWN) + owner // 2 * OWN + slot
    tiles = jnp.arange(pos.shape[0])
    order = jnp.sum(jnp.where(tiles[:, None] == pos[None, :], tiles[None, :], 0), axis=1)
    jobs.dst = (2 * order[:, None] + jnp.arange(2)[None, :]).reshape(-1)
    rank = ranks(counts, True)
    slots = -(-PR // N)
    j = jnp.arange(slots)
    want = j * N + jnp.where(j % 2 == 0, s, N - 1 - s)
    hit = want[:, None] == rank[None, :]
    jobs.rows = jnp.sum(jnp.where(hit, jnp.arange(PR)[None, :], 0), axis=1).astype(jnp.int32)
    jobs.counts = jnp.sum(jnp.where(hit, counts[None, :], 0), axis=1).astype(jnp.int32)
    jobs.far = jnp.zeros((slots,), jnp.int32)
    k = rank // N
    w = jnp.where(k % 2 == 0, rank % N, N - 1 - rank % N)
    jobs.at = (w ^ s) * slots + k
    return jobs


def plan_kernel(N, Z, OWN, where, owner, mine, theirs, ids, place, dst, rows, cnts, far, at, order, used, srt, prm):
    s, z, c = ids[0], ids[1], ids[2]
    PR = 2 * N
    for o in range(2 * Z):
        used[o] = 0
    for t in range(place.shape[0]):
        o = owner[t]
        i = used[o]
        used[o] = i + 1
        order[o * OWN + i] = t
        place[t] = ((o & 1) ^ c) * (Z * OWN) + (o >> 1) * OWN + i
    for i, (cc, zz, k, h) in enumerate(where):
        half = (s ^ k) * (2 * OWN // N) + h
        dst[i] = 2 * order[((z ^ zz) * 2 + (c ^ cc)) * OWN + (half >> 1)] + (half & 1)

    def ranked(ref, base, keep):
        v = [ref[i] for i in range(PR)]
        got = []
        for i in range(PR):
            r = 0
            for j in range(PR):
                if j != i:
                    r = r + jnp.where(v[j] >= v[i] if j < i else v[j] > v[i], 1, 0)
            srt[base + r] = v[i]
            if keep:
                srt[2 * PR + r] = i
            got.append(r)
        return got

    rank = ranked(mine, c * PR, True)
    ranked(theirs, (1 - c) * PR, False)
    a = [srt[i] for i in range(PR)]
    b = [srt[PR + i] for i in range(PR)]
    kept, traded = {}, {}
    for i in range(N):
        for j in range(N):
            kept[i, j] = jnp.maximum(a[i] + a[PR - 1 - i], b[j] + b[PR - 1 - j])
            traded[i, j] = jnp.maximum(a[i] + b[PR - 1 - j], b[j] + a[PR - 1 - i])
    best = None
    for p in itertools.permutations(range(N)):
        worst = functools.reduce(jnp.maximum, [jnp.minimum(kept[i, p[i]], traded[i, p[i]]) for i in range(N)])
        if best is None:
            best, perm = worst, [jnp.int32(v) for v in p]
        else:
            less = worst < best
            best = jnp.where(less, worst, best)
            perm = [jnp.where(less, jnp.int32(v), u) for u, v in zip(perm, p)]
    for i in range(N):
        prm[i] = perm[i]
        prm[N + perm[i]] = i
    trade = jnp.int32(0)
    for i in range(N):
        for j in range(N):
            cell = (s == i) & (prm[i] == j)
            trade = jnp.where(cell & (traded[i, j] < kept[i, j]), 1, trade)
    pair = jnp.where(c == 0, s, prm[s])
    other = jnp.where(c == 0, prm[s], s)
    rows[0] = srt[2 * PR + pair]
    rows[1] = srt[2 * PR + PR - 1 - pair]
    far[0] = 0
    far[1] = trade
    cnts[0] = srt[c * PR + pair]
    cnts[1] = srt[jnp.where(trade != 0, (1 - c) * PR + PR - 1 - other, c * PR + PR - 1 - pair)]
    for p in range(PR):
        low = rank[p] >= N
        j = jnp.where(low, PR - 1 - rank[p], rank[p])
        w = jnp.where(c == 0, j, prm[N + j])
        at[p] = (w ^ s) * 2 + jnp.where(low, 1, 0)


def plan(owner_list, mine, theirs, ids, where, N, Z, OWN):
    SM = pl.BlockSpec(memory_space=pltpu.SMEM)
    tiles, PR = owner_list.shape[0], mine.shape[0]
    sizes = (tiles, 2 * tiles, 2, 2, 2, PR)
    jobs = R()
    jobs.place, jobs.dst, jobs.rows, jobs.counts, jobs.far, jobs.at = pl.pallas_call(
        functools.partial(plan_kernel, N, Z, OWN, where),
        out_shape=[jax.ShapeDtypeStruct((n,), jnp.int32) for n in sizes],
        in_specs=[SM] * 4,
        out_specs=[SM] * 6,
        scratch_shapes=[pltpu.SMEM((n,), jnp.int32) for n in (tiles, 2 * Z, 3 * PR, 2 * N)],
    )(owner_list, mine, theirs, ids)
    return jobs


def shards(embedding, cotangent, counts, owner_list, tiles_owned, first_owned, second_owned,
           small_params, small_first, small_second):
    N, DP = lax.axis_size("section"), lax.axis_size("dp")
    Z = DP // 2
    s, dp = lax.axis_index("section"), lax.axis_index("dp")
    z, c = dp // 2, dp % 2
    PR, T, D = embedding.shape
    OWN, H, _ = tiles_owned.shape
    shared = PR == 2 * N and OWN * H % (64 * N) == 0
    if shared:
        pieces, where, early = gather_tiles(tiles_owned, N, Z, s)
        jobs = plan(owner_list, counts, swap(counts, "dp", 1), jnp.stack([s, z, c]), where, N, Z, OWN)
        row = jobs.rows[1]
        emb_far, cot_far = (swap(pick(v, row, 0), "dp", 1) for v in (embedding, cotangent))
    else:
        pieces = [lax.all_gather(tiles_owned.astype(BF16), "dp", axis=0, tiled=True).reshape(-1, 64, D)]
        jobs = plain_jobs(owner_list, counts, N, Z, OWN, s, c)
        emb_far, cot_far = embedding[0], cotangent[0]
    fe, keep, send, sg = call(N, N if shared else 1, OWN, jobs.counts, jobs.place, jobs.dst, jobs.rows, jobs.far, embedding, cotangent,
                              emb_far, cot_far, small_params, pieces)
    slots = [fe[j] for j in range(fe.shape[0])]
    tile_grad, small_grad, halfway = reduce_all(keep, send, sg, N, Z, s, z)
    tile_grad = tile_grad.reshape(OWN, H, D)
    if shared:
        other = swap(slots[1], "dp", 1)
        mine = jnp.where(jobs.far[1] != 0, other, slots[1])
        slots[1] = mine
    done = [pick(v, s, 0) for v in slots]
    for k in range(1, N):
        done += [swap(pick(v, s ^ k, 0), "section", k) for v in slots]
    fin, eg = in_order(done, len(slots), jobs.at, PR)
    tile_first, tile_second, tile_new = adam_update(
        tile_grad, first_owned, second_owned, tiles_owned, weight_decay, learn_rate
    )
    small_first_new, small_second_new, small_new = adam_update(
        small_grad, small_first, small_second, small_params, 0.0, small_rate
    )
    return (fin, eg, tile_grad, tile_first, tile_second, tile_new,
            small_grad, small_first_new, small_second_new, small_new)


def solution(mesh):
    P = jax.sharding.PartitionSpec
    own, rep = P("dp", None, None), P()
    return jax.shard_map(
        shards,
        mesh=mesh,
        in_specs=(own, own, P("dp"), rep, own, own, own, rep, rep, rep),
        out_specs=(P("dp", "section", None),) * 2 + (own,) * 4 + (rep,) * 4,
        check_vma=False,
    )
```
